32 devices in a mesh: cuts: 2 (over y), idx: 8 (over z, x), half: 2 (over core).
Axes of the slice: x: 2, y: 2, z: 4, core: 2. Of those that a mesh axis runs over, the one named last changes fastest.
Arguments:
- left_factor: float32 [2, 4, 64, 1024, 256], P('half', 'cuts', 'idx'), parts along dimension 1, may hold values from -6 to 6
- right_factor: float32 [2, 4, 64, 256, 1024], P('half', 'cuts', None, 'idx'), parts along dimension 1, may hold values from -0.25 to 0.25
Outputs:
- amplitudes: float32 [1024, 4, 1024], P(('idx', 'half'), 'cuts'), parts along dimension 1
The draws below stay inside these ranges and needn't reach their ends.
There are 2 independent parts, one for each index of `cuts`. The reference program is written for one: setup_inputs(seed, part) draws one part's arguments, and reference() takes and returns one part's arrays. A program takes and returns all parts, laid end to end along the dimension named above; each array names one. Nothing has to cross between parts.
All inputs are finite; a program needn't handle non-finite values.
Results may differ from the reference program's by a relative error of at most 0.0003.
Values sent between devices are 32-bit elements; how exact they have to be, the bound alone decides.
No kernel may reach another device: no remote copies, remote signals or barrier semaphores. Data moves between devices by JAX's collectives and lax.ppermute only.
A program may use at most 256 MiB of HBM per device.

```python
import math
import jax
import jax.numpy as jnp
from jax import lax

BATCH = 64
M = 1024
K = 256
N = 1024


def strengthened(result, rng, source, target, shards_of, factor):
    def block_of(position):
        return (jnp.arange(result.shape[position]) // (result.shape[position] // shards_of)).reshape((-1,) + (1,) * (result.ndim - 1 - position))

    near = jax.random.permutation(rng, shards_of)[block_of(target)]
    far = (block_of(target) + shards_of // 2) % shards_of
    return jnp.where((block_of(source) == near) | (block_of(source) == far), factor * result, result)


def level_of(stream_key, extent, shards, smallest, top_value):
    def one(axis_at, blocks):
        draws = jax.random.uniform(jax.random.fold_in(jax.random.fold_in(stream_key, 6), axis_at), (blocks,), jnp.float32, smallest / len(shards), top_value / len(shards))
        return jnp.repeat(jnp.exp(draws), extent[axis_at] // blocks).reshape((-1,) + (1,) * (len(extent) - axis_at - 1))

    loudness = one(*shards[0])
    for cut in shards[1:]:
        loudness = loudness * one(*cut)
    return loudness


def centred(stream_key, shape, width, limit, pieces=(), held_as=jnp.bfloat16):
    entries = width * jax.random.normal(stream_key, shape, jnp.float32)
    if pieces:
        entries = entries * level_of(stream_key, shape, pieces, -0.22, 0.18)
    return jnp.clip(entries, -limit, limit).astype(held_as)


def heavy_noise(key, shape, spread, limit, shards, heavy, kind=jnp.bfloat16):
    values = spread * jax.random.normal(key, shape, jnp.float32)
    if shards:
        values = values * level_of(key, shape, shards, -0.22, 0.18)
    return jnp.clip(strengthened(values, jax.random.fold_in(key, 3), *heavy), -limit, limit).astype(kind)


def setup_inputs(seed: int = 0, part: int = 0) -> dict:
    splits = jax.random.split(jax.random.key(seed), 3)
    part_keys = jax.random.split(jax.random.fold_in(splits[2], part), 3)
    left_factor = heavy_noise(part_keys[0], (2, 2, BATCH, M, K), 1.0, 6.0, ((0, 2), (2, 8)), (2, 3, 8, 2.0), jnp.float32)
    right_factor = centred(part_keys[1], (2, 2, BATCH, K, N), (2 * K) ** -0.5, 0.25, ((0, 2), (3, 8)), jnp.float32)
    return dict(left_factor=left_factor, right_factor=right_factor)


def complex_product(left_real, left_imag, right_real, right_imag, pattern):
    highest = lax.Precision.HIGHEST
    real_part = jnp.einsum(pattern, left_real, right_real, precision=highest) - jnp.einsum(pattern, left_imag, right_imag, precision=highest)
    imag_part = jnp.einsum(pattern, left_real, right_imag, precision=highest) + jnp.einsum(pattern, left_imag, right_real, precision=highest)
    return (real_part, imag_part)

def reference(left_factor, right_factor):
    block_size = math.gcd(BATCH, 8)
    norm_scale = 1.0 / math.sqrt(2.0 * BATCH * N)

    def batch_block(running, block_index):
        first_row = (block_index * block_size).astype(jnp.int32)
        left_block = lax.dynamic_slice_in_dim(left_factor, first_row, block_size, 2)
        right_block = lax.dynamic_slice_in_dim(right_factor, first_row, block_size, 2)
        merged_zero = complex_product(left_block[0, 0], left_block[0, 1], right_block[0, 0], right_block[0, 1], 'bmk,bkn->bmn')
        merged_one = complex_product(left_block[1, 0], left_block[1, 1], right_block[1, 0], right_block[1, 1], 'bmk,bkn->bmn')
        real_part, imag_part = complex_product(merged_zero[0], merged_zero[1], merged_one[0], merged_one[1], 'bmn,bon->mo')
        return (running + jnp.stack([real_part, imag_part], axis=1) * norm_scale, None)
    start_value = jnp.zeros((M, 2, M), jnp.float32)
    total, unused = lax.scan(batch_block, start_value, jnp.arange(BATCH // block_size, dtype=jnp.int32))
    return total
```

```python
import math

import jax
import jax.numpy as jnp
from jax import lax
from jax.sharding import PartitionSpec as P

HIGH = lax.Precision.HIGH


def swapped(x, axis):
    return lax.ppermute(x, axis, [(i, i ^ 1) for i in range(lax.axis_size(axis))])


def complex_terms(left_real, left_imag, right_real, right_imag, pattern):
    first = jnp.einsum(pattern, left_real, right_real, precision=HIGH)
    second = jnp.einsum(pattern, left_imag, right_imag, precision=HIGH)
    mixed = jnp.einsum(pattern, left_real + left_imag, right_real + right_imag, precision=HIGH)
    return first, second, mixed


def on_device(left_factor, right_factor):
    idx_size = lax.axis_size("idx")
    half_size = lax.axis_size("half")
    left = left_factor[0]
    right = right_factor[0]
    _, local_batch, rows, inner = left.shape
    _, batch, inner_part, between = right.shape
    own_rows = rows // (idx_size * half_size)
    half_rows = rows // half_size
    half_cols = between // half_size
    is_lower = lax.axis_index("half") == 0
    scale = 1.0 / math.sqrt(2.0 * batch * between)

    pieces = right.reshape(2, idx_size, local_batch, inner_part, half_size, half_cols)

    split_rows = left.reshape(2, local_batch, idx_size, half_size, own_rows, inner)
    upper_rows = lax.ppermute(split_rows[:, :, :, 1], "half", [(0, 1)])
    other_whole = lax.ppermute(left, "half", [(1, 0)])
    first_left = jnp.where(is_lower, split_rows[:, :, :, 0], upper_rows)
    first_left = first_left.reshape(2, local_batch, half_rows, inner)
    second_left = jnp.where(is_lower, other_whole, left)

    totals = None
    for b in range(local_batch):
        outgoing = jnp.transpose(pieces[:, :, b], (1, 3, 0, 2, 4))
        outgoing = outgoing.reshape(idx_size * half_size, 2, inner_part, half_cols)
        arrived = lax.all_to_all(outgoing, ("idx", "half"), 0, 0, tiled=True)
        arrived = arrived.reshape(idx_size, half_size, 2, inner_part, half_cols)
        factors = jnp.transpose(arrived, (1, 2, 0, 3, 4)).reshape(2, 2, inner, half_cols)
        first, second, mixed = complex_terms(
            factors[0, 0], factors[0, 1], factors[1, 0], factors[1, 1], "kn,ln->kl"
        )
        core = jnp.stack([first - second, mixed - first - second]) * scale
        core = core + swapped(core, "half")
        first, second, mixed = complex_terms(
            first_left[0, b], first_left[1, b], core[0], core[1], "mk,kl->ml"
        )
        terms = complex_terms(
            first - second, mixed - first - second, second_left[0, b], second_left[1, b], "ml,ol->mo"
        )
        totals = terms if totals is None else [t + u for t, u in zip(totals, terms)]
    first, second, mixed = totals
    partial = jnp.stack([first - second, mixed - first - second], axis=1)
    return lax.psum_scatter(partial, "idx", scatter_dimension=0, tiled=True)


def solution(mesh):
    return jax.shard_map(
        on_device,
        mesh=mesh,
        in_specs=(P("half", "cuts", "idx", None, None), P("half", "cuts", None, "idx", None)),
        out_specs=P(("idx", "half"), "cuts", None),
        check_vma=False,
    )
```

```python
import functools
import math

import jax
import jax.numpy as jnp
from jax import lax
from jax.experimental import pallas as pl
from jax.experimental.pallas import tpu as pltpu
from jax.sharding import PartitionSpec as P

HIGH = lax.Precision.HIGH
MIB = 1 << 20
WINDOW = 4
ANYWHERE = pl.BlockSpec(memory_space=pl.ANY)
IN_VMEM = pl.BlockSpec(memory_space=pltpu.VMEM)
IN_SMEM = pl.BlockSpec(memory_space=pltpu.SMEM)


def swapped(x, axis):
    return lax.ppermute(x, axis, [(i, i ^ 1) for i in range(lax.axis_size(axis))])


def complex_terms(left_real, left_imag, right_real, right_imag, pattern):
    first = jnp.einsum(pattern, left_real, right_real, precision=HIGH)
    second = jnp.einsum(pattern, left_imag, right_imag, precision=HIGH)
    mixed = jnp.einsum(pattern, left_real + left_imag, right_real + right_imag, precision=HIGH)
    return first, second, mixed


def general(left_factor, right_factor):
    idx_size = lax.axis_size("idx")
    half_size = lax.axis_size("half")
    left = left_factor[0]
    right = right_factor[0]
    _, local_batch, rows, inner = left.shape
    _, batch, inner_part, between = right.shape
    own_rows = rows // (idx_size * half_size)
    half_rows = rows // half_size
    half_cols = between // half_size
    is_lower = lax.axis_index("half") == 0
    scale = 1.0 / math.sqrt(2.0 * batch * between)
    pieces = right.reshape(2, idx_size, local_batch, inner_part, half_size, half_cols)
    split_rows = left.reshape(2, local_batch, idx_size, half_size, own_rows, inner)
    upper_rows = lax.ppermute(split_rows[:, :, :, 1], "half", [(0, 1)])
    other_whole = lax.ppermute(left, "half", [(1, 0)])
    first_left = jnp.where(is_lower, split_rows[:, :, :, 0], upper_rows)
    first_left = first_left.reshape(2, local_batch, half_rows, inner)
    second_left = jnp.where(is_lower, other_whole, left)
    totals = None
    for b in range(local_batch):
        outgoing = jnp.transpose(pieces[:, :, b], (1, 3, 0, 2, 4))
        outgoing = outgoing.reshape(idx_size * half_size, 2, inner_part, half_cols)
        arrived = lax.all_to_all(outgoing, ("idx", "half"), 0, 0, tiled=True)
        arrived = arrived.reshape(idx_size, half_size, 2, inner_part, half_cols)
        factors = jnp.transpose(arrived, (1, 2, 0, 3, 4)).reshape(2, 2, inner, half_cols)
        first, second, mixed = complex_terms(
            factors[0, 0], factors[0, 1], factors[1, 0], factors[1, 1], "kn,ln->kl"
        )
        core = jnp.stack([first - second, mixed - first - second]) * scale
        core = core + swapped(core, "half")
        first, second, mixed = complex_terms(
            first_left[0, b], first_left[1, b], core[0], core[1], "mk,kl->ml"
        )
        terms = complex_terms(
            first - second, mixed - first - second, second_left[0, b], second_left[1, b], "ml,ol->mo"
        )
        totals = terms if totals is None else [t + u for t, u in zip(totals, terms)]
    first, second, mixed = totals
    partial = jnp.stack([first - second, mixed - first - second], axis=1)
    return lax.psum_scatter(partial, "idx", scatter_dimension=0, tiled=True)


def split_float(x):
    high = x.astype(jnp.bfloat16)
    return high, (x - high.astype(jnp.float32)).astype(jnp.bfloat16)


def dot_parts(left, right, dims):
    def dot(a, b):
        return lax.dot_general(a, b, (dims, ((), ())), preferred_element_type=jnp.float32)

    return dot(left[0], right[0]) + (dot(left[0], right[1]) + dot(left[1], right[0]))


def complex_dot(left_real, left_imag, right_real, right_imag, dims):
    first = dot_parts(split_float(left_real), split_float(right_real), dims)
    second = dot_parts(split_float(left_imag), split_float(right_imag), dims)
    mixed = dot_parts(
        split_float(left_real + left_imag), split_float(right_real + right_imag), dims
    )
    return first - second, mixed - first - second


NT = ((1,), (1,))
NN = ((1,), (0,))


def deal_kernel(start, count, half_cols, place, right, *refs):
    outs, sems = refs[:-1], refs[-1]
    idx, half = place[0], place[1]
    copies = []
    for slot, out in enumerate(outs):
        far, side = slot // 2, slot % 2
        column = pl.multiple_of((half ^ side) * half_cols, half_cols)
        source = right.at[:, idx ^ far, pl.ds(start, count), :, pl.ds(column, half_cols)]
        copy = pltpu.make_async_copy(source, out, sems.at[slot])
        copy.start()
        copies.append(copy)
    for copy in copies:
        copy.wait()


def core_kernel(count, inner_part, scale, place, *refs):
    pieces, core, factors, sems = refs[:-3], refs[-3], refs[-2], refs[-1]
    idx, half = place[0], place[1]
    copies = []
    for slot, piece in enumerate(pieces):
        far, side = slot // 2, slot % 2
        row = pl.multiple_of((idx ^ far) * inner_part, inner_part)
        target = factors.at[half ^ side, :, :, pl.ds(row, inner_part), :]
        copy = pltpu.make_async_copy(piece, target, sems.at[slot])
        copy.start()
        copies.append(copy)
    for copy in copies:
        copy.wait()
    for b in range(count):
        real, imag = complex_dot(
            factors[0, 0, b], factors[0, 1, b], factors[1, 0, b], factors[1, 1, b], NT
        )
        core[b, 0] = real * scale
        core[b, 1] = imag * scale


def amplitude_kernel(start, count, tile, fresh, place, own_core, other_core, own_left, other_left, *refs):
    before = None if fresh else refs[0]
    total, first, second, product, sems, sum_sem = refs[-6:]
    half = place[1]

    def copies(lower):
        pairs = (own_left, other_left) if lower else (other_left, own_left)
        side = 0 if lower else 1
        return [
            pltpu.make_async_copy(pairs[0].at[:, pl.ds(start, count), :, side], first, sems.at[0]),
            pltpu.make_async_copy(pairs[1].at[:, pl.ds(start, count)], second, sems.at[1]),
        ]

    for lower in (True, False):

        @pl.when(half == (0 if lower else 1))
        def _():
            for copy in copies(lower):
                copy.start()

    if not fresh:
        loading = pltpu.make_async_copy(before, total, sum_sem)
        loading.start()
    for lower in (True, False):

        @pl.when(half == (0 if lower else 1))
        def _():
            for copy in copies(lower):
                copy.wait()

    if not fresh:
        loading.wait()
    _, _, groups, own_rows, inner = first.shape
    rows = groups * own_rows
    columns = second.shape[2] * second.shape[3] * second.shape[4]
    for b in range(count):
        real, imag = complex_dot(
            first[0, b].reshape(rows, inner),
            first[1, b].reshape(rows, inner),
            own_core[b, 0] + other_core[b, 0],
            own_core[b, 1] + other_core[b, 1],
            NN,
        )
        for place_in, part in enumerate((real, imag, real + imag)):
            product[2 * place_in], product[2 * place_in + 1] = split_float(part)

        def column_tile(step, carry):
            at = pl.multiple_of(step * tile, tile)
            per = second.shape[3] * second.shape[4]
            right_real = second[0, b, pl.ds(step * (tile // per), tile // per)].reshape(tile, inner)
            right_imag = second[1, b, pl.ds(step * (tile // per), tile // per)].reshape(tile, inner)
            one = dot_parts((product[0], product[1]), split_float(right_real), NT)
            two = dot_parts((product[2], product[3]), split_float(right_imag), NT)
            three = dot_parts((product[4], product[5]), split_float(right_real + right_imag), NT)
            spot = pl.ds(at, tile)
            if fresh and b == 0:
                total[0, :, spot] = one - two
                total[1, :, spot] = three - one - two
            else:
                total[0, :, spot] += one - two
                total[1, :, spot] += three - one - two
            return carry

        lax.fori_loop(0, columns // tile, column_tile, 0)


def sending_order(devices):
    far = list(range(devices // 2, devices))
    near = list(range(1, devices // 2))
    order = []
    for i, slot in enumerate(far):
        order.append(slot)
        order += near[i : i + 1]
    return order


def pieces_of(arrived, pieces, q):
    return arrived[q] if q < len(arrived) else pieces


def chunks_of(count):
    sizes = []
    left = count
    while left:
        size = 2 if left > 2 else 1
        sizes.append(size)
        left -= size
    return sizes


def overlapped(left_factor, right_factor):
    idx_size = lax.axis_size("idx")
    _, _, local_batch, rows, inner = left_factor.shape
    _, _, batch, inner_part, between = right_factor.shape
    own_rows = rows // (idx_size * 2)
    half_rows = rows // 2
    half_cols = between // 2
    scale = 1.0 / math.sqrt(2.0 * batch * between)
    place = jnp.stack([lax.axis_index("idx"), lax.axis_index("half")]).astype(jnp.int32)
    right = right_factor.reshape(2, idx_size, local_batch, inner_part, between)
    devices = idx_size * 2
    params = pltpu.CompilerParams(vmem_limit_bytes=40 * MIB)

    sizes = chunks_of(local_batch)
    starts = [sum(sizes[:q]) for q in range(len(sizes))]
    shape = (2, local_batch, idx_size, 2, own_rows, inner)
    own_left = left_factor.reshape(shape)
    other_left = None

    def dealt(start, count, source):
        pieces = pl.pallas_call(
            functools.partial(deal_kernel, start, count, half_cols),
            out_shape=[jax.ShapeDtypeStruct((2, count, inner_part, half_cols), jnp.float32)] * devices,
            in_specs=[IN_SMEM, ANYWHERE],
            out_specs=[ANYWHERE] * devices,
            scratch_shapes=[pltpu.SemaphoreType.DMA((devices,))],
            cost_estimate=pl.CostEstimate(
                flops=0, bytes_accessed=2 * devices * 8 * count * inner_part * half_cols, transcendentals=0
            ),
            compiler_params=params,
        )(place, source)
        return list(pieces)

    def core_of(count, pieces):
        return pl.pallas_call(
            functools.partial(core_kernel, count, inner_part, scale),
            out_shape=jax.ShapeDtypeStruct((count, 2, inner, inner), jnp.float32),
            in_specs=[IN_SMEM] + [ANYWHERE] * devices,
            out_specs=IN_VMEM,
            scratch_shapes=[
                pltpu.VMEM((2, 2, count, inner, half_cols), jnp.float32),
                pltpu.SemaphoreType.DMA((devices,)),
            ],
            cost_estimate=pl.CostEstimate(
                flops=18 * count * inner * inner * half_cols,
                bytes_accessed=16 * count * inner * (inner + half_cols),
                transcendentals=0,
            ),
            compiler_params=params,
        )(place, *pieces)

    def added(start, count, core, other_core, total):
        fresh = total is None
        return pl.pallas_call(
            functools.partial(amplitude_kernel, start, count, 256, fresh),
            out_shape=jax.ShapeDtypeStruct((2, half_rows, rows), jnp.float32),
            in_specs=[IN_SMEM, IN_VMEM, IN_VMEM, ANYWHERE, ANYWHERE] + [ANYWHERE] * (not fresh),
            out_specs=IN_VMEM,
            scratch_shapes=[
                pltpu.VMEM((2, count, idx_size, own_rows, inner), jnp.float32),
                pltpu.VMEM((2, count, idx_size, 2, own_rows, inner), jnp.float32),
                pltpu.VMEM((6, half_rows, inner), jnp.bfloat16),
                pltpu.SemaphoreType.DMA((2,)),
                pltpu.SemaphoreType.DMA,
            ],
            cost_estimate=pl.CostEstimate(
                flops=18 * count * half_rows * inner * (inner + rows),
                bytes_accessed=count * 12 * rows * inner + 16 * half_rows * rows,
                transcendentals=0,
            ),
            compiler_params=params,
        )(place, core, other_core, own_left, other_left, *([] if fresh else [total]))

    order = sending_order(devices)
    other_left = None
    total = None
    landed = []
    arrived = []

    def finish(q):
        core = core_of(sizes[q], arrived[q])
        return added(starts[q], sizes[q], core, swapped(core, "half"), total)

    upcoming = dealt(starts[0], sizes[0], right)
    for q in range(len(sizes)):
        pieces = upcoming
        for turn, slot in enumerate(order):
            piece = pieces[slot]
            if len(landed) >= WINDOW:
                old_q, old_slot = landed[-WINDOW]
                piece, arrived_piece = lax.optimization_barrier((piece, pieces_of(arrived, pieces, old_q)[old_slot]))
                pieces_of(arrived, pieces, old_q)[old_slot] = arrived_piece
            if q and turn == WINDOW + 1:
                arrived[q - 1], pieces[order[1]] = lax.optimization_barrier((arrived[q - 1], pieces[order[1]]))
                total = finish(q - 1)
            if q and turn == len(order) - 4:
                piece, total = lax.optimization_barrier((piece, total))
            if q + 1 < len(sizes) and turn == WINDOW + 3:
                piece, upcoming = lax.optimization_barrier((piece, upcoming))
            pairs = [(i, i ^ slot) for i in range(devices)]
            pieces[slot] = lax.ppermute(piece, ("idx", "half"), pairs)
            landed.append((q, slot))
            if q == 0 and turn == 1:
                other_left = swapped(left_factor, "half").reshape(shape)
            if q + 1 < len(sizes) and turn == 4:
                source, pieces[order[0]] = lax.optimization_barrier((right, pieces[order[0]]))
                upcoming = dealt(starts[q + 1], sizes[q + 1], source)
        arrived.append(pieces)
    total = finish(len(sizes) - 1)

    return lax.psum_scatter(jnp.moveaxis(total, 0, 1), "idx", scatter_dimension=0, tiled=True)


def on_device(left_factor, right_factor):
    idx_size = lax.axis_size("idx")
    rows, inner_part, between = left_factor.shape[3], right_factor.shape[3], right_factor.shape[4]
    aligned = (
        lax.axis_size("half") == 2
        and idx_size in (2, 4, 8)
        and inner_part % 8 == 0
        and between % 256 == 0
        and rows % 256 == 0
        and rows % (16 * idx_size) == 0
        and 256 % (rows // idx_size) == 0
    )
    return (overlapped if aligned else general)(left_factor, right_factor)


def solution(mesh):
    return jax.shard_map(
        on_device,
        mesh=mesh,
        in_specs=(P("half", "cuts", "idx", None, None), P("half", "cuts", None, "idx", None)),
        out_specs=P(("idx", "half"), "cuts", None),
        check_vma=False,
    )
```

```python
import functools
import math

import jax
import jax.numpy as jnp
from jax import lax
from jax.experimental import pallas as pl
from jax.experimental.pallas import tpu as pltpu
from jax.sharding import PartitionSpec as P

HIGH = lax.Precision.HIGH
MIB = 1 << 20
ANYWHERE = pl.BlockSpec(memory_space=pl.ANY)
IN_VMEM = pl.BlockSpec(memory_space=pltpu.VMEM)
IN_SMEM = pl.BlockSpec(memory_space=pltpu.SMEM)


def swapped(x, axis):
    return lax.ppermute(x, axis, [(i, i ^ 1) for i in range(lax.axis_size(axis))])


def complex_terms(left_real, left_imag, right_real, right_imag, pattern):
    first = jnp.einsum(pattern, left_real, right_real, precision=HIGH)
    second = jnp.einsum(pattern, left_imag, right_imag, precision=HIGH)
    mixed = jnp.einsum(pattern, left_real + left_imag, right_real + right_imag, precision=HIGH)
    return first, second, mixed


def general(left_factor, right_factor):
    idx_size = lax.axis_size("idx")
    half_size = lax.axis_size("half")
    left = left_factor[0]
    right = right_factor[0]
    _, local_batch, rows, inner = left.shape
    _, batch, inner_part, between = right.shape
    own_rows = rows // (idx_size * half_size)
    half_rows = rows // half_size
    half_cols = between // half_size
    is_lower = lax.axis_index("half") == 0
    scale = 1.0 / math.sqrt(2.0 * batch * between)
    pieces = right.reshape(2, idx_size, local_batch, inner_part, half_size, half_cols)
    split_rows = left.reshape(2, local_batch, idx_size, half_size, own_rows, inner)
    upper_rows = lax.ppermute(split_rows[:, :, :, 1], "half", [(0, 1)])
    other_whole = lax.ppermute(left, "half", [(1, 0)])
    first_left = jnp.where(is_lower, split_rows[:, :, :, 0], upper_rows)
    first_left = first_left.reshape(2, local_batch, half_rows, inner)
    second_left = jnp.where(is_lower, other_whole, left)
    totals = None
    for b in range(local_batch):
        outgoing = jnp.transpose(pieces[:, :, b], (1, 3, 0, 2, 4))
        outgoing = outgoing.reshape(idx_size * half_size, 2, inner_part, half_cols)
        arrived = lax.all_to_all(outgoing, ("idx", "half"), 0, 0, tiled=True)
        arrived = arrived.reshape(idx_size, half_size, 2, inner_part, half_cols)
        factors = jnp.transpose(arrived, (1, 2, 0, 3, 4)).reshape(2, 2, inner, half_cols)
        first, second, mixed = complex_terms(
            factors[0, 0], factors[0, 1], factors[1, 0], factors[1, 1], "kn,ln->kl"
        )
        core = jnp.stack([first - second, mixed - first - second]) * scale
        core = core + swapped(core, "half")
        first, second, mixed = complex_terms(
            first_left[0, b], first_left[1, b], core[0], core[1], "mk,kl->ml"
        )
        terms = complex_terms(
            first - second, mixed - first - second, second_left[0, b], second_left[1, b], "ml,ol->mo"
        )
        totals = terms if totals is None else [t + u for t, u in zip(totals, terms)]
    first, second, mixed = totals
    partial = jnp.stack([first - second, mixed - first - second], axis=1)
    return lax.psum_scatter(partial, "idx", scatter_dimension=0, tiled=True)


def split_float(x):
    high = x.astype(jnp.bfloat16)
    return high, (x - high.astype(jnp.float32)).astype(jnp.bfloat16)


def dot_parts(left, right, dims):
    def dot(a, b):
        return lax.dot_general(a, b, (dims, ((), ())), preferred_element_type=jnp.float32)

    return dot(left[0], right[0]) + (dot(left[0], right[1]) + dot(left[1], right[0]))


def complex_dot(left_real, left_imag, right_real, right_imag, dims):
    first = dot_parts(split_float(left_real), split_float(right_real), dims)
    second = dot_parts(split_float(left_imag), split_float(right_imag), dims)
    mixed = dot_parts(
        split_float(left_real + left_imag), split_float(right_real + right_imag), dims
    )
    return first - second, mixed - first - second


NT = ((1,), (1,))
NN = ((1,), (0,))


def deal_kernel(start, count, half_cols, right, out, sems):
    copies = []
    for half in range(2):
        for plane in range(2):
            source = right.at[plane, :, pl.ds(start, count), :, pl.ds(half * half_cols, half_cols)]
            copies.append(pltpu.make_async_copy(source, out.at[:, half, plane], sems.at[2 * half + plane]))
    for copy in copies:
        copy.start()
    for copy in copies:
        copy.wait()


def core_kernel(count, scale, arrived, core, factors, sems):
    inner = core.shape[2]
    copies = {}
    for b in range(count):
        for part in range(4):
            source = arrived.at[:, part // 2, part % 2, b]
            copies[b, part] = pltpu.make_async_copy(source, factors.at[b, part], sems.at[b, part])
            copies[b, part].start()
    for b in range(count):
        for part in range(4):
            copies[b, part].wait()
        planes = [factors[b, part].reshape(inner, factors.shape[4]) for part in range(4)]
        real, imag = complex_dot(*planes, NT)
        core[b, 0] = real * scale
        core[b, 1] = imag * scale


def amplitude_kernel(start, count, tile, fresh, place, own_core, other_core, own_left, other_left, *refs):
    before = None if fresh else refs[0]
    total, first, second, product, sems, sum_sem = refs[-6:]
    half = place[0]

    def copies(lower, b):
        pairs = (own_left, other_left) if lower else (other_left, own_left)
        side = 0 if lower else 1
        return [
            pltpu.make_async_copy(pairs[0].at[:, start + b, :, side], first.at[b], sems.at[0, b]),
            pltpu.make_async_copy(pairs[1].at[:, start + b], second.at[b], sems.at[1, b]),
        ]

    for lower in (True, False):

        @pl.when(half == (0 if lower else 1))
        def _():
            for b in range(count):
                for copy in copies(lower, b):
                    copy.start()

    if not fresh:
        loading = pltpu.make_async_copy(before, total, sum_sem)
        loading.start()
    _, _, groups, own_rows, inner = first.shape
    rows = groups * own_rows
    columns = second.shape[2] * second.shape[3] * second.shape[4]
    per = second.shape[3] * second.shape[4]
    for b in range(count):
        for copy in copies(True, b):
            copy.wait()
        real, imag = complex_dot(
            first[b, 0].reshape(rows, inner),
            first[b, 1].reshape(rows, inner),
            own_core[b, 0] + other_core[b, 0],
            own_core[b, 1] + other_core[b, 1],
            NN,
        )
        for place_in, part in enumerate((real, imag, real + imag)):
            product[2 * place_in], product[2 * place_in + 1] = split_float(part)
        if b == 0 and not fresh:
            loading.wait()

        def column_tile(step, carry):
            at = pl.multiple_of(step * tile, tile)
            right_real = second[b, 0, pl.ds(step * (tile // per), tile // per)].reshape(tile, inner)
            right_imag = second[b, 1, pl.ds(step * (tile // per), tile // per)].reshape(tile, inner)
            one = dot_parts((product[0], product[1]), split_float(right_real), NT)
            two = dot_parts((product[2], product[3]), split_float(right_imag), NT)
            three = dot_parts((product[4], product[5]), split_float(right_real + right_imag), NT)
            spot = pl.ds(at, tile)
            if fresh and b == 0:
                total[0, :, spot] = one - two
                total[1, :, spot] = three - one - two
            else:
                total[0, :, spot] += one - two
                total[1, :, spot] += three - one - two
            return carry

        lax.fori_loop(0, columns // tile, column_tile, 0)


def chunks_of(count):
    last = min(2, count - 1)
    return [count - last, last]


def overlapped(left_factor, right_factor):
    idx_size = lax.axis_size("idx")
    _, _, local_batch, rows, inner = left_factor.shape
    _, _, batch, inner_part, between = right_factor.shape
    own_rows = rows // (idx_size * 2)
    half_rows = rows // 2
    half_cols = between // 2
    scale = 1.0 / math.sqrt(2.0 * batch * between)
    place = lax.axis_index("half").astype(jnp.int32)[None]
    right = right_factor.reshape(2, idx_size, local_batch, inner_part, between)
    params = pltpu.CompilerParams(vmem_limit_bytes=44 * MIB)
    shape = (2, local_batch, idx_size, 2, own_rows, inner)
    own_left = left_factor.reshape(shape)

    def dealt(start, count):
        return pl.pallas_call(
            functools.partial(deal_kernel, start, count, half_cols),
            out_shape=jax.ShapeDtypeStruct((idx_size, 2, 2, count, inner_part, half_cols), jnp.float32),
            in_specs=[ANYWHERE],
            out_specs=ANYWHERE,
            scratch_shapes=[pltpu.SemaphoreType.DMA((4,))],
            cost_estimate=pl.CostEstimate(
                flops=0, bytes_accessed=32 * idx_size * count * inner_part * half_cols, transcendentals=0
            ),
            compiler_params=params,
        )(right)

    def sent(pieces):
        flat = pieces.reshape(2 * idx_size, *pieces.shape[2:])
        return lax.all_to_all(flat, ("idx", "half"), 0, 0, tiled=True).reshape(pieces.shape)

    def core_of(count, arrived):
        return pl.pallas_call(
            functools.partial(core_kernel, count, scale),
            out_shape=jax.ShapeDtypeStruct((count, 2, inner, inner), jnp.float32),
            in_specs=[ANYWHERE],
            out_specs=IN_VMEM,
            scratch_shapes=[
                pltpu.VMEM((count, 4, idx_size, inner_part, half_cols), jnp.float32),
                pltpu.SemaphoreType.DMA((count, 4)),
            ],
            cost_estimate=pl.CostEstimate(
                flops=18 * count * inner * inner * half_cols,
                bytes_accessed=16 * count * inner * (inner + half_cols),
                transcendentals=0,
            ),
            compiler_params=params,
        )(arrived)

    def added(start, count, core, other_core, other_left, total):
        fresh = total is None
        return pl.pallas_call(
            functools.partial(amplitude_kernel, start, count, 256, fresh),
            out_shape=jax.ShapeDtypeStruct((2, half_rows, rows), jnp.float32),
            in_specs=[IN_SMEM, IN_VMEM, IN_VMEM, ANYWHERE, ANYWHERE] + [ANYWHERE] * (not fresh),
            out_specs=IN_VMEM,
            scratch_shapes=[
                pltpu.VMEM((count, 2, idx_size, own_rows, inner), jnp.float32),
                pltpu.VMEM((count, 2, idx_size, 2, own_rows, inner), jnp.float32),
                pltpu.VMEM((6, half_rows, inner), jnp.bfloat16),
                pltpu.SemaphoreType.DMA((2, count)),
                pltpu.SemaphoreType.DMA,
            ],
            cost_estimate=pl.CostEstimate(
                flops=18 * count * half_rows * inner * (inner + rows),
                bytes_accessed=count * 12 * rows * inner + 16 * half_rows * rows,
                transcendentals=0,
            ),
            compiler_params=params,
        )(place, core, other_core, own_left, other_left, *([] if fresh else [total]))

    many, few = chunks_of(local_batch)
    other_left = swapped(left_factor, "half").reshape(shape)
    arrived = sent(dealt(0, many))
    pieces, other_left = lax.optimization_barrier((dealt(many, few), other_left))
    late = sent(pieces)
    core = core_of(many, arrived)
    total = added(0, many, core, swapped(core, "half"), other_left, None)
    core = core_of(few, late)
    total = added(many, few, core, swapped(core, "half"), other_left, total)

    return lax.psum_scatter(jnp.moveaxis(total, 0, 1), "idx", scatter_dimension=0, tiled=True)


def on_device(left_factor, right_factor):
    idx_size = lax.axis_size("idx")
    rows, inner_part, between = left_factor.shape[3], right_factor.shape[3], right_factor.shape[4]
    aligned = (
        lax.axis_size("half") == 2
        and left_factor.shape[2] > 1
        and idx_size in (2, 4, 8)
        and inner_part % 8 == 0
        and between % 256 == 0
        and rows % 256 == 0
        and rows % (16 * idx_size) == 0
        and 256 % (rows // idx_size) == 0
    )
    return (overlapped if aligned else general)(left_factor, right_factor)


def solution(mesh):
    return jax.shard_map(
        on_device,
        mesh=mesh,
        in_specs=(P("half", "cuts", "idx", None, None), P("half", "cuts", None, "idx", None)),
        out_specs=P(("idx", "half"), "cuts", None),
        check_vma=False,
    )
```

```python
import functools
import math

import jax
import jax.numpy as jnp
from jax import lax
from jax.experimental import pallas as pl
from jax.experimental.pallas import tpu as pltpu
from jax.sharding import PartitionSpec as P

HIGH = lax.Precision.HIGH
MIB = 1 << 20
ANYWHERE = pl.BlockSpec(memory_space=pl.ANY)
IN_VMEM = pl.BlockSpec(memory_space=pltpu.VMEM)
IN_SMEM = pl.BlockSpec(memory_space=pltpu.SMEM)


def swapped(x, axis):
    return lax.ppermute(x, axis, [(i, i ^ 1) for i in range(lax.axis_size(axis))])


def complex_terms(left_real, left_imag, right_real, right_imag, pattern):
    first = jnp.einsum(pattern, left_real, right_real, precision=HIGH)
    second = jnp.einsum(pattern, left_imag, right_imag, precision=HIGH)
    mixed = jnp.einsum(pattern, left_real + left_imag, right_real + right_imag, precision=HIGH)
    return first, second, mixed


def general(left_factor, right_factor):
    idx_size = lax.axis_size("idx")
    half_size = lax.axis_size("half")
    left = left_factor[0]
    right = right_factor[0]
    _, local_batch, rows, inner = left.shape
    _, batch, inner_part, between = right.shape
    own_rows = rows // (idx_size * half_size)
    half_rows = rows // half_size
    half_cols = between // half_size
    is_lower = lax.axis_index("half") == 0
    scale = 1.0 / math.sqrt(2.0 * batch * between)
    pieces = right.reshape(2, idx_size, local_batch, inner_part, half_size, half_cols)
    split_rows = left.reshape(2, local_batch, idx_size, half_size, own_rows, inner)
    upper_rows = lax.ppermute(split_rows[:, :, :, 1], "half", [(0, 1)])
    other_whole = lax.ppermute(left, "half", [(1, 0)])
    first_left = jnp.where(is_lower, split_rows[:, :, :, 0], upper_rows)
    first_left = first_left.reshape(2, local_batch, half_rows, inner)
    second_left = jnp.where(is_lower, other_whole, left)
    totals = None
    for b in range(local_batch):
        outgoing = jnp.transpose(pieces[:, :, b], (1, 3, 0, 2, 4))
        outgoing = outgoing.reshape(idx_size * half_size, 2, inner_part, half_cols)
        arrived = lax.all_to_all(outgoing, ("idx", "half"), 0, 0, tiled=True)
        arrived = arrived.reshape(idx_size, half_size, 2, inner_part, half_cols)
        factors = jnp.transpose(arrived, (1, 2, 0, 3, 4)).reshape(2, 2, inner, half_cols)
        first, second, mixed = complex_terms(
            factors[0, 0], factors[0, 1], factors[1, 0], factors[1, 1], "kn,ln->kl"
        )
        core = jnp.stack([first - second, mixed - first - second]) * scale
        core = core + swapped(core, "half")
        first, second, mixed = complex_terms(
            first_left[0, b], first_left[1, b], core[0], core[1], "mk,kl->ml"
        )
        terms = complex_terms(
            first - second, mixed - first - second, second_left[0, b], second_left[1, b], "ml,ol->mo"
        )
        totals = terms if totals is None else [t + u for t, u in zip(totals, terms)]
    first, second, mixed = totals
    partial = jnp.stack([first - second, mixed - first - second], axis=1)
    return lax.psum_scatter(partial, "idx", scatter_dimension=0, tiled=True)


def split_float(x):
    high = x.astype(jnp.bfloat16)
    return high, (x - high.astype(jnp.float32)).astype(jnp.bfloat16)


def dot_parts(left, right, dims):
    def dot(a, b):
        return lax.dot_general(a, b, (dims, ((), ())), preferred_element_type=jnp.float32)

    return dot(left[0], right[0]) + (dot(left[0], right[1]) + dot(left[1], right[0]))


def complex_dot(left_real, left_imag, right_real, right_imag, dims):
    first = dot_parts(split_float(left_real), split_float(right_real), dims)
    second = dot_parts(split_float(left_imag), split_float(right_imag), dims)
    mixed = dot_parts(
        split_float(left_real + left_imag), split_float(right_real + right_imag), dims
    )
    return first - second, mixed - first - second


NT = ((1,), (1,))
NN = ((1,), (0,))


def deal_kernel(half_cols, right, out):
    for half in range(2):
        out[0, half] = right[:, 0, :, :, half * half_cols : (half + 1) * half_cols]


def core_kernel(count, scale, arrived, core, factors, sems):
    inner = core.shape[2]
    copies = {}
    for b in range(count):
        for part in range(4):
            source = arrived.at[:, part // 2, part % 2, b]
            copies[b, part] = pltpu.make_async_copy(source, factors.at[b, part], sems.at[b, part])
            copies[b, part].start()
    for b in range(count):
        for part in range(4):
            copies[b, part].wait()
        planes = [factors[b, part].reshape(inner, factors.shape[4]) for part in range(4)]
        real, imag = complex_dot(*planes, NT)
        core[b, 0] = real * scale
        core[b, 1] = imag * scale


def amplitude_kernel(start, count, tile, fresh, place, own_core, other_core, own_left, other_left, *refs):
    before = None if fresh else refs[0]
    total, first, second, product, sems, sum_sem = refs[-6:]
    half = place[0]

    def copies(lower, b):
        pairs = (own_left, other_left) if lower else (other_left, own_left)
        side = 0 if lower else 1
        return [
            pltpu.make_async_copy(pairs[0].at[:, start + b, :, side], first.at[b], sems.at[0, b]),
            pltpu.make_async_copy(pairs[1].at[:, start + b], second.at[b], sems.at[1, b]),
        ]

    for lower in (True, False):

        @pl.when(half == (0 if lower else 1))
        def _():
            for b in range(count):
                for copy in copies(lower, b):
                    copy.start()

    if not fresh:
        loading = pltpu.make_async_copy(before, total, sum_sem)
        loading.start()
    _, _, groups, own_rows, inner = first.shape
    rows = groups * own_rows
    columns = second.shape[2] * second.shape[3] * second.shape[4]
    per = second.shape[3] * second.shape[4]
    for b in range(count):
        for copy in copies(True, b):
            copy.wait()
        real, imag = complex_dot(
            first[b, 0].reshape(rows, inner),
            first[b, 1].reshape(rows, inner),
            own_core[b, 0] + other_core[b, 0],
            own_core[b, 1] + other_core[b, 1],
            NN,
        )
        for place_in, part in enumerate((real, imag, real + imag)):
            product[2 * place_in], product[2 * place_in + 1] = split_float(part)
        if b == 0 and not fresh:
            loading.wait()

        def column_tile(step, carry):
            at = pl.multiple_of(step * tile, tile)
            right_real = second[b, 0, pl.ds(step * (tile // per), tile // per)].reshape(tile, inner)
            right_imag = second[b, 1, pl.ds(step * (tile // per), tile // per)].reshape(tile, inner)
            one = dot_parts((product[0], product[1]), split_float(right_real), NT)
            two = dot_parts((product[2], product[3]), split_float(right_imag), NT)
            three = dot_parts((product[4], product[5]), split_float(right_real + right_imag), NT)
            spot = pl.ds(at, tile)
            if fresh and b == 0:
                total[0, :, spot] = one - two
                total[1, :, spot] = three - one - two
            else:
                total[0, :, spot] += one - two
                total[1, :, spot] += three - one - two
            return carry

        lax.fori_loop(0, columns // tile, column_tile, 0)


def chunks_of(count):
    return count - 1, 1


def overlapped(left_factor, right_factor):
    idx_size = lax.axis_size("idx")
    _, _, local_batch, rows, inner = left_factor.shape
    _, _, batch, inner_part, between = right_factor.shape
    own_rows = rows // (idx_size * 2)
    half_rows = rows // 2
    half_cols = between // 2
    scale = 1.0 / math.sqrt(2.0 * batch * between)
    place = lax.axis_index("half").astype(jnp.int32)[None]
    right = right_factor.reshape(2, idx_size, local_batch, inner_part, between)
    params = pltpu.CompilerParams(vmem_limit_bytes=44 * MIB)
    shape = (2, local_batch, idx_size, 2, own_rows, inner)
    own_left = left_factor.reshape(shape)

    def dealt(start, count):
        return pl.pallas_call(
            functools.partial(deal_kernel, half_cols),
            grid=(idx_size,),
            out_shape=jax.ShapeDtypeStruct((idx_size, 2, 2, count, inner_part, half_cols), jnp.float32),
            in_specs=[pl.BlockSpec((2, 1, count, inner_part, between), lambda i: (0, i, start // count, 0, 0))],
            out_specs=pl.BlockSpec((1, 2, 2, count, inner_part, half_cols), lambda i: (i, 0, 0, 0, 0, 0)),
            cost_estimate=pl.CostEstimate(
                flops=0, bytes_accessed=32 * idx_size * count * inner_part * half_cols, transcendentals=0
            ),
            compiler_params=params,
        )(right)

    def sent(pieces):
        flat = pieces.reshape(2 * idx_size, *pieces.shape[2:])
        return lax.all_to_all(flat, ("idx", "half"), 0, 0, tiled=True).reshape(pieces.shape)

    def core_of(count, arrived):
        return pl.pallas_call(
            functools.partial(core_kernel, count, scale),
            out_shape=jax.ShapeDtypeStruct((count, 2, inner, inner), jnp.float32),
            in_specs=[ANYWHERE],
            out_specs=IN_VMEM,
            scratch_shapes=[
                pltpu.VMEM((count, 4, idx_size, inner_part, half_cols), jnp.float32),
                pltpu.SemaphoreType.DMA((count, 4)),
            ],
            cost_estimate=pl.CostEstimate(
                flops=18 * count * inner * inner * half_cols,
                bytes_accessed=16 * count * inner * (inner + half_cols),
                transcendentals=0,
            ),
            compiler_params=params,
        )(arrived)

    def added(start, count, core, other_core, other_left, total):
        fresh = total is None
        return pl.pallas_call(
            functools.partial(amplitude_kernel, start, count, 256, fresh),
            out_shape=jax.ShapeDtypeStruct((2, half_rows, rows), jnp.float32),
            in_specs=[IN_SMEM, IN_VMEM, IN_VMEM, ANYWHERE, ANYWHERE] + [ANYWHERE] * (not fresh),
            out_specs=IN_VMEM,
            scratch_shapes=[
                pltpu.VMEM((count, 2, idx_size, own_rows, inner), jnp.float32),
                pltpu.VMEM((count, 2, idx_size, 2, own_rows, inner), jnp.float32),
                pltpu.VMEM((6, half_rows, inner), jnp.bfloat16),
                pltpu.SemaphoreType.DMA((2, count)),
                pltpu.SemaphoreType.DMA,
            ],
            cost_estimate=pl.CostEstimate(
                flops=18 * count * half_rows * inner * (inner + rows),
                bytes_accessed=count * 12 * rows * inner + 16 * half_rows * rows,
                transcendentals=0,
            ),
            compiler_params=params,
        )(place, core, other_core, own_left, other_left, *([] if fresh else [total]))

    many, few = chunks_of(local_batch)
    other_left = swapped(left_factor, "half").reshape(shape)
    arrived = sent(dealt(0, many))
    pieces, other_left = lax.optimization_barrier((dealt(many, few), other_left))
    late = sent(pieces)
    core = core_of(many, arrived)
    total = added(0, many, core, swapped(core, "half"), other_left, None)
    late, total = lax.optimization_barrier((late, total))
    core = core_of(few, late)
    total = added(many, few, core, swapped(core, "half"), other_left, total)

    return lax.psum_scatter(jnp.moveaxis(total, 0, 1), "idx", scatter_dimension=0, tiled=True)


def on_device(left_factor, right_factor):
    idx_size = lax.axis_size("idx")
    rows, inner_part, between = left_factor.shape[3], right_factor.shape[3], right_factor.shape[4]
    aligned = (
        lax.axis_size("half") == 2
        and left_factor.shape[2] > 1
        and idx_size in (2, 4, 8)
        and inner_part % 8 == 0
        and between % 256 == 0
        and rows % 256 == 0
        and rows % (16 * idx_size) == 0
        and 256 % (rows // idx_size) == 0
    )
    return (overlapped if aligned else general)(left_factor, right_factor)


def solution(mesh):
    return jax.shard_map(
        on_device,
        mesh=mesh,
        in_specs=(P("half", "cuts", "idx", None, None), P("half", "cuts", None, "idx", None)),
        out_specs=P(("idx", "half"), "cuts", None),
        check_vma=False,
    )
```

```python
import functools
import math

import jax
import jax.numpy as jnp
from jax import lax
from jax.experimental import pallas as pl
from jax.experimental.pallas import tpu as pltpu
from jax.sharding import PartitionSpec as P

HIGH = lax.Precision.HIGH
MIB = 1 << 20
ANYWHERE = pl.BlockSpec(memory_space=pl.ANY)
IN_VMEM = pl.BlockSpec(memory_space=pltpu.VMEM)
IN_SMEM = pl.BlockSpec(memory_space=pltpu.SMEM)


def swapped(x, axis):
    return lax.ppermute(x, axis, [(i, i ^ 1) for i in range(lax.axis_size(axis))])


def complex_terms(left_real, left_imag, right_real, right_imag, pattern):
    first = jnp.einsum(pattern, left_real, right_real, precision=HIGH)
    second = jnp.einsum(pattern, left_imag, right_imag, precision=HIGH)
    mixed = jnp.einsum(pattern, left_real + left_imag, right_real + right_imag, precision=HIGH)
    return first, second, mixed


def general(left_factor, right_factor):
    idx_size = lax.axis_size("idx")
    half_size = lax.axis_size("half")
    left = left_factor[0]
    right = right_factor[0]
    _, local_batch, rows, inner = left.shape
    _, batch, inner_part, between = right.shape
    own_rows = rows // (idx_size * half_size)
    half_rows = rows // half_size
    half_cols = between // half_size
    is_lower = lax.axis_index("half") == 0
    scale = 1.0 / math.sqrt(2.0 * batch * between)
    pieces = right.reshape(2, idx_size, local_batch, inner_part, half_size, half_cols)
    split_rows = left.reshape(2, local_batch, idx_size, half_size, own_rows, inner)
    upper_rows = lax.ppermute(split_rows[:, :, :, 1], "half", [(0, 1)])
    other_whole = lax.ppermute(left, "half", [(1, 0)])
    first_left = jnp.where(is_lower, split_rows[:, :, :, 0], upper_rows)
    first_left = first_left.reshape(2, local_batch, half_rows, inner)
    second_left = jnp.where(is_lower, other_whole, left)
    totals = None
    for b in range(local_batch):
        outgoing = jnp.transpose(pieces[:, :, b], (1, 3, 0, 2, 4))
        outgoing = outgoing.reshape(idx_size * half_size, 2, inner_part, half_cols)
        arrived = lax.all_to_all(outgoing, ("idx", "half"), 0, 0, tiled=True)
        arrived = arrived.reshape(idx_size, half_size, 2, inner_part, half_cols)
        factors = jnp.transpose(arrived, (1, 2, 0, 3, 4)).reshape(2, 2, inner, half_cols)
        first, second, mixed = complex_terms(
            factors[0, 0], factors[0, 1], factors[1, 0], factors[1, 1], "kn,ln->kl"
        )
        core = jnp.stack([first - second, mixed - first - second]) * scale
        core = core + swapped(core, "half")
        first, second, mixed = complex_terms(
            first_left[0, b], first_left[1, b], core[0], core[1], "mk,kl->ml"
        )
        terms = complex_terms(
            first - second, mixed - first - second, second_left[0, b], second_left[1, b], "ml,ol->mo"
        )
        totals = terms if totals is None else [t + u for t, u in zip(totals, terms)]
    first, second, mixed = totals
    partial = jnp.stack([first - second, mixed - first - second], axis=1)
    return lax.psum_scatter(partial, "idx", scatter_dimension=0, tiled=True)


def split_float(x):
    high = x.astype(jnp.bfloat16)
    return high, (x - high.astype(jnp.float32)).astype(jnp.bfloat16)


def dot_parts(left, right, dims):
    def dot(a, b):
        return lax.dot_general(a, b, (dims, ((), ())), preferred_element_type=jnp.float32)

    return dot(left[0], right[0]) + (dot(left[0], right[1]) + dot(left[1], right[0]))


def complex_dot(left_real, left_imag, right_real, right_imag, dims):
    first = dot_parts(split_float(left_real), split_float(right_real), dims)
    second = dot_parts(split_float(left_imag), split_float(right_imag), dims)
    mixed = dot_parts(
        split_float(left_real + left_imag), split_float(right_real + right_imag), dims
    )
    return first - second, mixed - first - second


BRIEF = pl.CostEstimate(flops=0, bytes_accessed=1024, transcendentals=0)
NT = ((1,), (1,))
NN = ((1,), (0,))


def deal_kernel(half_cols, right, out):
    for half in range(2):
        out[0, half] = right[:, 0, :, :, half * half_cols : (half + 1) * half_cols]


def core_kernel(count, scale, arrived, core, factors, sems):
    inner = core.shape[2]
    copies = {}
    for b in range(count):
        for part in range(4):
            source = arrived.at[:, part // 2, part % 2, b]
            copies[b, part] = pltpu.make_async_copy(source, factors.at[b, part], sems.at[b, part])
            copies[b, part].start()
    for b in range(count):
        for part in range(4):
            copies[b, part].wait()
        planes = [factors[b, part].reshape(inner, factors.shape[4]) for part in range(4)]
        real, imag = complex_dot(*planes, NT)
        core[b, 0] = real * scale
        core[b, 1] = imag * scale


def amplitude_kernel(start, count, tile, fresh, place, own_core, other_core, own_left, other_left, *refs):
    before = None if fresh else refs[0]
    total, first, second, product, sems, sum_sem = refs[-6:]
    half = place[0]

    def copies(lower, b):
        pairs = (own_left, other_left) if lower else (other_left, own_left)
        side = 0 if lower else 1
        return [
            pltpu.make_async_copy(pairs[0].at[:, start + b, :, side], first.at[b], sems.at[0, b]),
            pltpu.make_async_copy(pairs[1].at[:, start + b], second.at[b], sems.at[1, b]),
        ]

    for lower in (True, False):

        @pl.when(half == (0 if lower else 1))
        def _():
            for b in range(count):
                for copy in copies(lower, b):
                    copy.start()

    if not fresh:
        loading = pltpu.make_async_copy(before, total, sum_sem)
        loading.start()
    _, _, groups, own_rows, inner = first.shape
    rows = groups * own_rows
    columns = second.shape[2] * second.shape[3] * second.shape[4]
    per = second.shape[3] * second.shape[4]
    for b in range(count):
        for copy in copies(True, b):
            copy.wait()
        real, imag = complex_dot(
            first[b, 0].reshape(rows, inner),
            first[b, 1].reshape(rows, inner),
            own_core[b, 0] + other_core[b, 0],
            own_core[b, 1] + other_core[b, 1],
            NN,
        )
        for place_in, part in enumerate((real, imag, real + imag)):
            product[2 * place_in], product[2 * place_in + 1] = split_float(part)
        if b == 0 and not fresh:
            loading.wait()

        def column_tile(step, carry):
            at = pl.multiple_of(step * tile, tile)
            right_real = second[b, 0, pl.ds(step * (tile // per), tile // per)].reshape(tile, inner)
            right_imag = second[b, 1, pl.ds(step * (tile // per), tile // per)].reshape(tile, inner)
            one = dot_parts((product[0], product[1]), split_float(right_real), NT)
            two = dot_parts((product[2], product[3]), split_float(right_imag), NT)
            three = dot_parts((product[4], product[5]), split_float(right_real + right_imag), NT)
            spot = pl.ds(at, tile)
            if fresh and b == 0:
                total[0, :, spot] = one - two
                total[1, :, spot] = three - one - two
            else:
                total[0, :, spot] += one - two
                total[1, :, spot] += three - one - two
            return carry

        lax.fori_loop(0, columns // tile, column_tile, 0)


def chunks_of(count):
    return count - 1, 1


def overlapped(left_factor, right_factor):
    idx_size = lax.axis_size("idx")
    _, _, local_batch, rows, inner = left_factor.shape
    _, _, batch, inner_part, between = right_factor.shape
    own_rows = rows // (idx_size * 2)
    half_rows = rows // 2
    half_cols = between // 2
    scale = 1.0 / math.sqrt(2.0 * batch * between)
    place = lax.axis_index("half").astype(jnp.int32)[None]
    right = right_factor.reshape(2, idx_size, local_batch, inner_part, between)
    params = pltpu.CompilerParams(vmem_limit_bytes=44 * MIB)
    shape = (2, local_batch, idx_size, 2, own_rows, inner)
    own_left = left_factor.reshape(shape)

    def dealt(start, count):
        return pl.pallas_call(
            functools.partial(deal_kernel, half_cols),
            grid=(idx_size,),
            out_shape=jax.ShapeDtypeStruct((idx_size, 2, 2, count, inner_part, half_cols), jnp.float32),
            in_specs=[pl.BlockSpec((2, 1, count, inner_part, between), lambda i: (0, i, start // count, 0, 0))],
            out_specs=pl.BlockSpec((1, 2, 2, count, inner_part, half_cols), lambda i: (i, 0, 0, 0, 0, 0)),
            cost_estimate=BRIEF,
            compiler_params=params,
        )(right)

    def sent(pieces):
        flat = pieces.reshape(2 * idx_size, *pieces.shape[2:])
        return lax.all_to_all(flat, ("idx", "half"), 0, 0, tiled=True).reshape(pieces.shape)

    def core_of(count, arrived):
        return pl.pallas_call(
            functools.partial(core_kernel, count, scale),
            out_shape=jax.ShapeDtypeStruct((count, 2, inner, inner), jnp.float32),
            in_specs=[ANYWHERE],
            out_specs=IN_VMEM,
            scratch_shapes=[
                pltpu.VMEM((count, 4, idx_size, inner_part, half_cols), jnp.float32),
                pltpu.SemaphoreType.DMA((count, 4)),
            ],
            cost_estimate=BRIEF,
            compiler_params=params,
        )(arrived)

    def added(start, count, core, other_core, other_left, total):
        fresh = total is None
        return pl.pallas_call(
            functools.partial(amplitude_kernel, start, count, 256, fresh),
            out_shape=jax.ShapeDtypeStruct((2, half_rows, rows), jnp.float32),
            in_specs=[IN_SMEM, IN_VMEM, IN_VMEM, ANYWHERE, ANYWHERE] + [ANYWHERE] * (not fresh),
            out_specs=IN_VMEM,
            scratch_shapes=[
                pltpu.VMEM((count, 2, idx_size, own_rows, inner), jnp.float32),
                pltpu.VMEM((count, 2, idx_size, 2, own_rows, inner), jnp.float32),
                pltpu.VMEM((6, half_rows, inner), jnp.bfloat16),
                pltpu.SemaphoreType.DMA((2, count)),
                pltpu.SemaphoreType.DMA,
            ],
            cost_estimate=BRIEF,
            compiler_params=params,
        )(place, core, other_core, own_left, other_left, *([] if fresh else [total]))

    many, few = chunks_of(local_batch)
    other_left = swapped(left_factor, "half").reshape(shape)
    arrived = sent(dealt(0, many))
    pieces = dealt(many, few)
    late = sent(pieces)
    arrived, pieces = lax.optimization_barrier((arrived, pieces))
    core = core_of(many, arrived)
    total = added(0, many, core, swapped(core, "half"), other_left, None)
    late, total = lax.optimization_barrier((late, total))
    core = core_of(few, late)
    total = added(many, few, core, swapped(core, "half"), other_left, total)

    return lax.psum_scatter(jnp.moveaxis(total, 0, 1), "idx", scatter_dimension=0, tiled=True)


def on_device(left_factor, right_factor):
    idx_size = lax.axis_size("idx")
    rows, inner_part, between = left_factor.shape[3], right_factor.shape[3], right_factor.shape[4]
    aligned = (
        lax.axis_size("half") == 2
        and left_factor.shape[2] > 1
        and idx_size in (2, 4, 8)
        and inner_part % 8 == 0
        and between % 256 == 0
        and rows % 256 == 0
        and rows % (16 * idx_size) == 0
        and 256 % (rows // idx_size) == 0
    )
    return (overlapped if aligned else general)(left_factor, right_factor)


def solution(mesh):
    return jax.shard_map(
        on_device,
        mesh=mesh,
        in_specs=(P("half", "cuts", "idx", None, None), P("half", "cuts", None, "idx", None)),
        out_specs=P(("idx", "half"), "cuts", None),
        check_vma=False,
    )
```

```python
import functools
import math

import jax
import jax.numpy as jnp
from jax import lax
from jax.experimental import pallas as pl
from jax.experimental.pallas import tpu as pltpu
from jax.sharding import PartitionSpec as P

HIGH = lax.Precision.HIGH
MIB = 1 << 20
ANYWHERE = pl.BlockSpec(memory_space=pl.ANY)
IN_VMEM = pl.BlockSpec(memory_space=pltpu.VMEM)
IN_SMEM = pl.BlockSpec(memory_space=pltpu.SMEM)


def swapped(x, axis):
    return lax.ppermute(x, axis, [(i, i ^ 1) for i in range(lax.axis_size(axis))])


def complex_terms(left_real, left_imag, right_real, right_imag, pattern):
    first = jnp.einsum(pattern, left_real, right_real, precision=HIGH)
    second = jnp.einsum(pattern, left_imag, right_imag, precision=HIGH)
    mixed = jnp.einsum(pattern, left_real + left_imag, right_real + right_imag, precision=HIGH)
    return first, second, mixed


def general(left_factor, right_factor):
    idx_size = lax.axis_size("idx")
    half_size = lax.axis_size("half")
    left = left_factor[0]
    right = right_factor[0]
    _, local_batch, rows, inner = left.shape
    _, batch, inner_part, between = right.shape
    own_rows = rows // (idx_size * half_size)
    half_rows = rows // half_size
    half_cols = between // half_size
    is_lower = lax.axis_index("half") == 0
    scale = 1.0 / math.sqrt(2.0 * batch * between)
    pieces = right.reshape(2, idx_size, local_batch, inner_part, half_size, half_cols)
    split_rows = left.reshape(2, local_batch, idx_size, half_size, own_rows, inner)
    upper_rows = lax.ppermute(split_rows[:, :, :, 1], "half", [(0, 1)])
    other_whole = lax.ppermute(left, "half", [(1, 0)])
    first_left = jnp.where(is_lower, split_rows[:, :, :, 0], upper_rows)
    first_left = first_left.reshape(2, local_batch, half_rows, inner)
    second_left = jnp.where(is_lower, other_whole, left)
    totals = None
    for b in range(local_batch):
        outgoing = jnp.transpose(pieces[:, :, b], (1, 3, 0, 2, 4))
        outgoing = outgoing.reshape(idx_size * half_size, 2, inner_part, half_cols)
        arrived = lax.all_to_all(outgoing, ("idx", "half"), 0, 0, tiled=True)
        arrived = arrived.reshape(idx_size, half_size, 2, inner_part, half_cols)
        factors = jnp.transpose(arrived, (1, 2, 0, 3, 4)).reshape(2, 2, inner, half_cols)
        first, second, mixed = complex_terms(
            factors[0, 0], factors[0, 1], factors[1, 0], factors[1, 1], "kn,ln->kl"
        )
        core = jnp.stack([first - second, mixed - first - second]) * scale
        core = core + swapped(core, "half")
        first, second, mixed = complex_terms(
            first_left[0, b], first_left[1, b], core[0], core[1], "mk,kl->ml"
        )
        terms = complex_terms(
            first - second, mixed - first - second, second_left[0, b], second_left[1, b], "ml,ol->mo"
        )
        totals = terms if totals is None else [t + u for t, u in zip(totals, terms)]
    first, second, mixed = totals
    partial = jnp.stack([first - second, mixed - first - second], axis=1)
    return lax.psum_scatter(partial, "idx", scatter_dimension=0, tiled=True)


def split_float(x):
    high = x.astype(jnp.bfloat16)
    return high, (x - high.astype(jnp.float32)).astype(jnp.bfloat16)


def stacked(parts, axis):
    return jnp.concatenate(parts, axis=axis)


def left_stack(x, axis):
    high, low = split_float(x)
    return stacked([high, high, low], axis)


def right_stack(x, axis):
    high, low = split_float(x)
    return stacked([high, low, high], axis)


def dot_stacks(left, right, dims):
    return lax.dot_general(left, right, (dims, ((), ())), preferred_element_type=jnp.float32)


def complex_dot(left_real, left_imag, right_real, right_imag, dims):
    left_axis, right_axis = dims[0][0], dims[1][0]

    def term(left, right):
        return dot_stacks(left_stack(left, left_axis), right_stack(right, right_axis), dims)

    first = term(left_real, right_real)
    second = term(left_imag, right_imag)
    mixed = term(left_real + left_imag, right_real + right_imag)
    return first - second, mixed - first - second


BRIEF = pl.CostEstimate(flops=0, bytes_accessed=1024, transcendentals=0)
NT = ((1,), (1,))
NN = ((1,), (0,))


def deal_kernel(half_cols, right, out):
    for half in range(2):
        out[0, half] = right[:, 0, :, :, half * half_cols : (half + 1) * half_cols]


def core_kernel(count, scale, arrived, core, factors, sems):
    inner = core.shape[2]
    copies = {}
    for b in range(count):
        for part in range(4):
            source = arrived.at[:, part // 2, part % 2, b]
            copies[b, part] = pltpu.make_async_copy(source, factors.at[b, part], sems.at[b, part])
            copies[b, part].start()
    for b in range(count):
        for part in range(4):
            copies[b, part].wait()
        planes = [factors[b, part].reshape(inner, factors.shape[4]) for part in range(4)]
        real, imag = complex_dot(*planes, NT)
        core[b, 0] = real * scale
        core[b, 1] = imag * scale


def row_slots(idx_size):
    return list(range(0, idx_size, 2)) + list(range(1, idx_size, 2))


def amplitude_kernel(start, count, columns, store, n_before, n_out, place, own_core, other_core, *refs):
    own_split, other_split, own_flat, other_flat = refs[:4]
    before = refs[4 : 4 + n_before]
    outs = refs[4 + n_before : 4 + n_before + n_out]
    first, second, product, sems, *more = refs[4 + n_before + n_out :]
    half, idx = place[0], place[1]
    low, high = columns
    _, _, groups, own_rows, inner = first.shape
    rows = groups * own_rows

    def first_copy(lower, b, position, slot):
        source = own_split if lower else other_split
        return pltpu.make_async_copy(
            source.at[:, start + b, idx ^ slot, 0 if lower else 1], first.at[b, :, position], sems.at[0, b]
        )

    def second_copy(lower, b):
        source = other_flat if lower else own_flat
        return pltpu.make_async_copy(
            source.at[:, start + b, low:high], second.at[b], sems.at[1, b]
        )

    for lower in (True, False):

        @pl.when(half == (0 if lower else 1))
        def _():
            for b in range(count):
                for position, slot in enumerate(row_slots(groups)):
                    first_copy(lower, b, position, slot).start()
                second_copy(lower, b).start()

    if n_before:
        held, held_sem = more
        loading = pltpu.make_async_copy(before[0], held, held_sem)
        loading.start()
    else:
        held = None
        for out in outs:
            out[...] = jnp.zeros_like(out)

    def one_value(b, carry):
        whole = own_split.at[:, start + b, :, 0]
        pltpu.make_async_copy(whole, first.at[b], sems.at[0, b]).wait()
        second_copy(True, b).wait()
        real, imag = complex_dot(
            first[b, 0].reshape(rows, inner),
            first[b, 1].reshape(rows, inner),
            own_core[b, 0] + other_core[b, 0],
            own_core[b, 1] + other_core[b, 1],
            NN,
        )
        for part, value in enumerate((real, imag, real + imag)):
            product[part] = left_stack(value, 1)
        if n_before:
            loading.wait()
        at = 0
        while at < high - low:
            wide = min(256, high - low - at)
            right_real, right_imag = second[b, 0, at : at + wide], second[b, 1, at : at + wide]
            one = dot_stacks(product[0], right_stack(right_real, 1), NT)
            two = dot_stacks(product[1], right_stack(right_imag, 1), NT)
            three = dot_stacks(product[2], right_stack(right_real + right_imag, 1), NT)
            store(outs, held, at, wide, one - two, three - one - two)
            at += wide
        return carry

    if count == 1:
        one_value(0, 0)
    else:
        lax.fori_loop(0, count, one_value, 0)


def add_running(cut, outs, held, at, wide, real, imag):
    for out, low, high in ((outs[0], 0, cut), (outs[1], cut, 1 << 30)):
        left, right = max(at, low), min(at + wide, high)
        if left < right:
            for plane, value in enumerate((real, imag)):
                out[plane, :, left - low : right - low] += value[:, left - at : right - at]


def put_near(outs, held, at, wide, real, imag):
    rows = outs[0].shape[1]
    for plane, value in enumerate((real, imag)):
        value = value + held[plane, :, at : at + wide]
        for bit in range(2):
            outs[bit][plane, :, at : at + wide] = value[bit * rows : (bit + 1) * rows]


def put_far(outs, held, at, wide, real, imag):
    own_rows = outs[0].shape[2]
    for plane, value in enumerate((real, imag)):
        value = value + held[plane, :, at : at + wide]
        for bit in range(2):
            for far, out in enumerate(outs):
                row = (bit * len(outs) + far) * own_rows
                out[plane, bit, :, at : at + wide] = value[row : row + own_rows]


def chunks_of(count):
    return count - 1, 1


def overlapped(left_factor, right_factor):
    idx_size = lax.axis_size("idx")
    _, _, local_batch, rows, inner = left_factor.shape
    _, _, batch, inner_part, between = right_factor.shape
    own_rows = rows // (idx_size * 2)
    half_rows = rows // 2
    half_cols = between // 2
    scale = 1.0 / math.sqrt(2.0 * batch * between)
    place = jnp.stack([lax.axis_index("half"), lax.axis_index("idx")]).astype(jnp.int32)
    depth = idx_size // 2
    cut = rows * 5 // 8 // 128 * 128
    right = right_factor.reshape(2, idx_size, local_batch, inner_part, between)
    params = pltpu.CompilerParams(vmem_limit_bytes=44 * MIB)
    shape = (2, local_batch, idx_size, 2, own_rows, inner)
    own_left = left_factor.reshape(shape)

    def dealt(start, count):
        return pl.pallas_call(
            functools.partial(deal_kernel, half_cols),
            grid=(idx_size,),
            out_shape=jax.ShapeDtypeStruct((idx_size, 2, 2, count, inner_part, half_cols), jnp.float32),
            in_specs=[pl.BlockSpec((2, 1, count, inner_part, between), lambda i: (0, i, start // count, 0, 0))],
            out_specs=pl.BlockSpec((1, 2, 2, count, inner_part, half_cols), lambda i: (i, 0, 0, 0, 0, 0)),
            cost_estimate=BRIEF,
            compiler_params=params,
        )(right)

    def sent(pieces):
        flat = pieces.reshape(2 * idx_size, *pieces.shape[2:])
        return lax.all_to_all(flat, ("idx", "half"), 0, 0, tiled=True).reshape(pieces.shape)

    def core_of(count, arrived):
        return pl.pallas_call(
            functools.partial(core_kernel, count, scale),
            out_shape=jax.ShapeDtypeStruct((count, 2, inner, inner), jnp.float32),
            in_specs=[ANYWHERE],
            out_specs=IN_VMEM,
            scratch_shapes=[
                pltpu.VMEM((count, 4, idx_size, inner_part, half_cols), jnp.float32),
                pltpu.SemaphoreType.DMA((count, 4)),
            ],
            cost_estimate=BRIEF,
            compiler_params=params,
        )(arrived)

    def added(start, count, columns, store, core, other_core, other_left, before, shapes):
        low, high = columns
        flat = (2, local_batch, rows, inner)
        scratch = [
            pltpu.VMEM((count, 2, idx_size, own_rows, inner), jnp.float32),
            pltpu.VMEM((count, 2, high - low, inner), jnp.float32),
            pltpu.VMEM((3, half_rows, 3 * inner), jnp.bfloat16),
            pltpu.SemaphoreType.DMA((2, count)),
        ]
        if before:
            scratch += [pltpu.VMEM(before[0].shape, jnp.float32), pltpu.SemaphoreType.DMA]
        return pl.pallas_call(
            functools.partial(amplitude_kernel, start, count, columns, store, len(before), len(shapes)),
            out_shape=[jax.ShapeDtypeStruct(shape, jnp.float32) for shape in shapes],
            in_specs=[IN_SMEM, IN_VMEM, IN_VMEM] + [ANYWHERE] * (4 + len(before)),
            out_specs=[IN_VMEM] * len(shapes),
            scratch_shapes=scratch,
            cost_estimate=BRIEF,
            compiler_params=params,
        )(
            place, core, other_core, own_left, other_left,
            own_left.reshape(flat), other_left.reshape(flat), *before,
        )

    def hop(x, mask):
        return lax.ppermute(x, "idx", [(i, i ^ mask) for i in range(idx_size)])

    many, few = chunks_of(local_batch)
    other_left = swapped(left_factor, "half").reshape(shape)
    arrived = sent(dealt(0, many))
    pieces = dealt(many, few)
    late = sent(pieces)
    arrived, pieces = lax.optimization_barrier((arrived, pieces))
    core = core_of(many, arrived)
    sums = added(
        0, many, (0, rows), functools.partial(add_running, cut), core, swapped(core, "half"), other_left, [],
        [(2, half_rows, cut), (2, half_rows, rows - cut)],
    )
    late, sums = lax.optimization_barrier((late, sums))
    core = core_of(few, late)
    other_core = swapped(core, "half")
    near = added(
        many, few, (0, cut), put_near, core, other_core, other_left, [sums[0]],
        [(2, half_rows // 2, cut)] * 2,
    )
    far = added(
        many, few, (cut, rows), put_far, core, other_core, other_left, [sums[1]],
        [(2, 2, own_rows, rows - cut)] * depth,
    )
    near_sum = (near[0] + hop(near[1], 1)).reshape(2, depth, own_rows, cut)
    far_sum = far[0]
    for d in range(1, depth):
        far_sum = far_sum + hop(far[d], 2 * d)
    near_out = near_sum[:, 0]
    for d in range(1, depth):
        near_out = near_out + hop(near_sum[:, d], 2 * d)
    far_out = far_sum[:, 0] + hop(far_sum[:, 1], 1)
    return jnp.moveaxis(jnp.concatenate([near_out, far_out], axis=2), 0, 1)


def on_device(left_factor, right_factor):
    idx_size = lax.axis_size("idx")
    rows, inner_part, between = left_factor.shape[3], right_factor.shape[3], right_factor.shape[4]
    aligned = (
        lax.axis_size("half") == 2
        and left_factor.shape[2] > 1
        and idx_size in (2, 4, 8)
        and inner_part % 8 == 0
        and between % 256 == 0
        and rows % 256 == 0
        and rows % (16 * idx_size) == 0
        and 256 % (rows // idx_size) == 0
    )
    return (overlapped if aligned else general)(left_factor, right_factor)


def solution(mesh):
    return jax.shard_map(
        on_device,
        mesh=mesh,
        in_specs=(P("half", "cuts", "idx", None, None), P("half", "cuts", None, "idx", None)),
        out_specs=P(("idx", "half"), "cuts", None),
        check_vma=False,
    )
```

```python
import functools
import math

import jax
import jax.numpy as jnp
from jax import lax
from jax.experimental import pallas as pl
from jax.experimental.pallas import tpu as pltpu
from jax.sharding import PartitionSpec as P

HIGH = lax.Precision.HIGH
MIB = 1 << 20
ANYWHERE = pl.BlockSpec(memory_space=pl.ANY)
IN_VMEM = pl.BlockSpec(memory_space=pltpu.VMEM)
IN_SMEM = pl.BlockSpec(memory_space=pltpu.SMEM)


def swapped(x, axis):
    return lax.ppermute(x, axis, [(i, i ^ 1) for i in range(lax.axis_size(axis))])


def complex_terms(left_real, left_imag, right_real, right_imag, pattern):
    first = jnp.einsum(pattern, left_real, right_real, precision=HIGH)
    second = jnp.einsum(pattern, left_imag, right_imag, precision=HIGH)
    mixed = jnp.einsum(pattern, left_real + left_imag, right_real + right_imag, precision=HIGH)
    return first, second, mixed


def general(left_factor, right_factor):
    idx_size = lax.axis_size("idx")
    half_size = lax.axis_size("half")
    left = left_factor[0]
    right = right_factor[0]
    _, local_batch, rows, inner = left.shape
    _, batch, inner_part, between = right.shape
    own_rows = rows // (idx_size * half_size)
    half_rows = rows // half_size
    half_cols = between // half_size
    is_lower = lax.axis_index("half") == 0
    scale = 1.0 / math.sqrt(2.0 * batch * between)
    pieces = right.reshape(2, idx_size, local_batch, inner_part, half_size, half_cols)
    split_rows = left.reshape(2, local_batch, idx_size, half_size, own_rows, inner)
    upper_rows = lax.ppermute(split_rows[:, :, :, 1], "half", [(0, 1)])
    other_whole = lax.ppermute(left, "half", [(1, 0)])
    first_left = jnp.where(is_lower, split_rows[:, :, :, 0], upper_rows)
    first_left = first_left.reshape(2, local_batch, half_rows, inner)
    second_left = jnp.where(is_lower, other_whole, left)
    totals = None
    for b in range(local_batch):
        outgoing = jnp.transpose(pieces[:, :, b], (1, 3, 0, 2, 4))
        outgoing = outgoing.reshape(idx_size * half_size, 2, inner_part, half_cols)
        arrived = lax.all_to_all(outgoing, ("idx", "half"), 0, 0, tiled=True)
        arrived = arrived.reshape(idx_size, half_size, 2, inner_part, half_cols)
        factors = jnp.transpose(arrived, (1, 2, 0, 3, 4)).reshape(2, 2, inner, half_cols)
        first, second, mixed = complex_terms(
            factors[0, 0], factors[0, 1], factors[1, 0], factors[1, 1], "kn,ln->kl"
        )
        core = jnp.stack([first - second, mixed - first - second]) * scale
        core = core + swapped(core, "half")
        first, second, mixed = complex_terms(
            first_left[0, b], first_left[1, b], core[0], core[1], "mk,kl->ml"
        )
        terms = complex_terms(
            first - second, mixed - first - second, second_left[0, b], second_left[1, b], "ml,ol->mo"
        )
        totals = terms if totals is None else [t + u for t, u in zip(totals, terms)]
    first, second, mixed = totals
    partial = jnp.stack([first - second, mixed - first - second], axis=1)
    return lax.psum_scatter(partial, "idx", scatter_dimension=0, tiled=True)


def split_float(x):
    high = x.astype(jnp.bfloat16)
    return high, (x - high.astype(jnp.float32)).astype(jnp.bfloat16)


def stacked(parts, axis):
    return jnp.concatenate(parts, axis=axis)


def left_stack(x, axis):
    high, low = split_float(x)
    return stacked([high, high, low], axis)


def right_stack(x, axis):
    high, low = split_float(x)
    return stacked([high, low, high], axis)


def dot_stacks(left, right, dims):
    return lax.dot_general(left, right, (dims, ((), ())), preferred_element_type=jnp.float32)


def complex_dot(left_real, left_imag, right_real, right_imag, dims):
    left_axis, right_axis = dims[0][0], dims[1][0]

    def term(left, right):
        return dot_stacks(left_stack(left, left_axis), right_stack(right, right_axis), dims)

    first = term(left_real, right_real)
    second = term(left_imag, right_imag)
    mixed = term(left_real + left_imag, right_real + right_imag)
    return first - second, mixed - first - second


BRIEF = pl.CostEstimate(flops=0, bytes_accessed=1024, transcendentals=0)
NT = ((1,), (1,))
NN = ((1,), (0,))


def deal_kernel(start, count, half_cols, right, out, sems):
    copies = []
    for half in range(2):
        for plane in range(2):
            source = right.at[plane, :, pl.ds(start, count), :, pl.ds(half * half_cols, half_cols)]
            copies.append(pltpu.make_async_copy(source, out.at[:, half, plane], sems.at[2 * half + plane]))
    for copy in copies:
        copy.start()
    for copy in copies:
        copy.wait()


def core_kernel(count, scale, arrived, core, factors, sems):
    inner = core.shape[2]
    copies = {}
    for b in range(count):
        for part in range(4):
            source = arrived.at[:, part // 2, part % 2, b]
            copies[b, part] = pltpu.make_async_copy(source, factors.at[b, part], sems.at[b, part])
            copies[b, part].start()
    for b in range(count):
        for part in range(4):
            copies[b, part].wait()
        planes = [factors[b, part].reshape(inner, factors.shape[4]) for part in range(4)]
        real, imag = complex_dot(*planes, NT)
        core[b, 0] = real * scale
        core[b, 1] = imag * scale


def amplitude_kernel(start, count, slots, n_before, n_out, place, own_core, other_core, *refs):
    own_split, other_split, own_flat, other_flat = refs[:4]
    before = refs[4 : 4 + n_before]
    outs = refs[4 + n_before : 4 + n_before + n_out]
    first, second, product, sems = refs[4 + n_before + n_out :]
    half, idx = place[0], place[1]
    _, _, groups, own_rows, inner = first.shape
    rows, columns = groups * own_rows, second.shape[2]

    def first_copy(lower, b, position, slot):
        source = own_split if lower else other_split
        return pltpu.make_async_copy(
            source.at[:, start + b, idx ^ slot, 0 if lower else 1], first.at[b, :, position], sems.at[0, b]
        )

    def second_copy(lower, b):
        source = other_flat if lower else own_flat
        return pltpu.make_async_copy(source.at[:, start + b], second.at[b], sems.at[1, b])

    for lower in (True, False):

        @pl.when(half == (0 if lower else 1))
        def _():
            for b in range(count):
                for position, slot in enumerate(slots):
                    first_copy(lower, b, position, slot).start()
                second_copy(lower, b).start()

    if not n_before:
        for out in outs:
            out[...] = jnp.zeros_like(out)
    piece = rows // n_out

    def one_value(b, carry):
        whole = own_split.at[:, start + b, :groups, 0]
        pltpu.make_async_copy(whole, first.at[b], sems.at[0, b]).wait()
        real, imag = complex_dot(
            first[b, 0].reshape(rows, inner),
            first[b, 1].reshape(rows, inner),
            own_core[b, 0] + other_core[b, 0],
            own_core[b, 1] + other_core[b, 1],
            NN,
        )
        for part, value in enumerate((real, imag, real + imag)):
            product[part] = left_stack(value, 1)
        second_copy(True, b).wait()
        for at in range(0, columns, 256):
            spot = slice(at, at + 256)
            right_real, right_imag = second[b, 0, spot], second[b, 1, spot]
            one = dot_stacks(product[0], right_stack(right_real, 1), NT)
            two = dot_stacks(product[1], right_stack(right_imag, 1), NT)
            three = dot_stacks(product[2], right_stack(right_real + right_imag, 1), NT)
            for plane, value in enumerate((one - two, three - one - two)):
                if n_before:
                    value = value + before[0][plane, :, spot]
                for number, out in enumerate(outs):
                    part = value[number * piece : (number + 1) * piece]
                    if n_before:
                        out[plane, :, spot] = part
                    else:
                        out[plane, :, spot] += part
        return carry

    if count == 1:
        one_value(0, 0)
    else:
        lax.fori_loop(0, count, one_value, 0)


def chunks_of(count):
    return count - 1, 1


def overlapped(left_factor, right_factor):
    idx_size = lax.axis_size("idx")
    _, _, local_batch, rows, inner = left_factor.shape
    _, _, batch, inner_part, between = right_factor.shape
    own_rows = rows // (idx_size * 2)
    half_rows = rows // 2
    half_cols = between // 2
    scale = 1.0 / math.sqrt(2.0 * batch * between)
    place = jnp.stack([lax.axis_index("half"), lax.axis_index("idx")]).astype(jnp.int32)
    depth = idx_size // 2
    right = right_factor.reshape(2, idx_size, local_batch, inner_part, between)
    params = pltpu.CompilerParams(vmem_limit_bytes=44 * MIB)
    shape = (2, local_batch, idx_size, 2, own_rows, inner)
    own_left = left_factor.reshape(shape)

    def dealt(start, count):
        return pl.pallas_call(
            functools.partial(deal_kernel, start, count, half_cols),
            out_shape=jax.ShapeDtypeStruct((idx_size, 2, 2, count, inner_part, half_cols), jnp.float32),
            in_specs=[ANYWHERE],
            out_specs=IN_VMEM,
            scratch_shapes=[pltpu.SemaphoreType.DMA((4,))],
            cost_estimate=BRIEF,
            compiler_params=pltpu.CompilerParams(vmem_limit_bytes=38 * MIB),
        )(right)

    def sent(pieces):
        flat = pieces.reshape(2 * idx_size, *pieces.shape[2:])
        return lax.all_to_all(flat, ("idx", "half"), 0, 0, tiled=True).reshape(pieces.shape)

    def core_of(count, arrived):
        return pl.pallas_call(
            functools.partial(core_kernel, count, scale),
            out_shape=jax.ShapeDtypeStruct((count, 2, inner, inner), jnp.float32),
            in_specs=[ANYWHERE],
            out_specs=IN_VMEM,
            scratch_shapes=[
                pltpu.VMEM((count, 4, idx_size, inner_part, half_cols), jnp.float32),
                pltpu.SemaphoreType.DMA((count, 4)),
            ],
            cost_estimate=BRIEF,
            compiler_params=params,
        )(arrived)

    def added(start, count, slots, n_out, core, other_core, other_left, before):
        flat = (2, local_batch, rows, inner)
        kept_rows = len(slots) * own_rows
        return pl.pallas_call(
            functools.partial(amplitude_kernel, start, count, slots, len(before), n_out),
            out_shape=[jax.ShapeDtypeStruct((2, kept_rows // n_out, rows), jnp.float32)] * n_out,
            in_specs=[IN_SMEM, IN_VMEM, IN_VMEM] + [ANYWHERE] * 4 + [IN_VMEM] * len(before),
            out_specs=[IN_VMEM] * n_out,
            scratch_shapes=[
                pltpu.VMEM((count, 2, len(slots), own_rows, inner), jnp.float32),
                pltpu.VMEM((count, 2, rows, inner), jnp.float32),
                pltpu.VMEM((3, kept_rows, 3 * inner), jnp.bfloat16),
                pltpu.SemaphoreType.DMA((2, count)),
            ],
            cost_estimate=BRIEF,
            compiler_params=params,
        )(
            place, core, other_core, own_left, other_left,
            own_left.reshape(flat), other_left.reshape(flat), *before,
        )

    def hop(x, mask):
        return lax.ppermute(x, "idx", [(i, i ^ mask) for i in range(idx_size)])

    many, few = chunks_of(local_batch)
    other_left = swapped(left_factor, "half").reshape(shape)
    arrived = sent(dealt(0, many))
    pieces = dealt(many, few)
    late = sent(pieces)
    arrived, pieces = lax.optimization_barrier((arrived, pieces))
    core = core_of(many, arrived)
    odd = list(range(idx_size - 1, 0, -2))
    even = [slot - 1 for slot in odd]
    sums = added(0, many, odd + even, 2, core, swapped(core, "half"), other_left, [])
    late, sums = lax.optimization_barrier((late, sums))
    core = core_of(few, late)
    other_core = swapped(core, "half")
    leaving = added(many, few, odd, depth, core, other_core, other_left, [sums[0]])
    core, leaving = lax.optimization_barrier((core, leaving))
    staying = added(many, few, even, depth, core, other_core, other_left, [sums[1]])
    landed = [hop(block, 1) for block in leaving]
    blocks = [kept + block for kept, block in zip(staying, landed)]
    arrived = [hop(block, slot) for block, slot in zip(blocks, even) if slot]
    result = blocks[-1]
    for block in arrived:
        result = result + block
    return jnp.moveaxis(result, 0, 1)


def on_device(left_factor, right_factor):
    idx_size = lax.axis_size("idx")
    rows, inner_part, between = left_factor.shape[3], right_factor.shape[3], right_factor.shape[4]
    aligned = (
        lax.axis_size("half") == 2
        and left_factor.shape[2] > 1
        and idx_size in (2, 4, 8)
        and inner_part % 8 == 0
        and between % 256 == 0
        and rows % 256 == 0
        and rows % (16 * idx_size) == 0
        and 256 % (rows // idx_size) == 0
    )
    return (overlapped if aligned else general)(left_factor, right_factor)


def solution(mesh):
    return jax.shard_map(
        on_device,
        mesh=mesh,
        in_specs=(P("half", "cuts", "idx", None, None), P("half", "cuts", None, "idx", None)),
        out_specs=P(("idx", "half"), "cuts", None),
        check_vma=False,
    )
```

```python
import functools
import math

import jax
import jax.numpy as jnp
from jax import lax
from jax.experimental import pallas as pl
from jax.experimental.pallas import tpu as pltpu
from jax.sharding import PartitionSpec as P

HIGH = lax.Precision.HIGH
MIB = 1 << 20
PIECES = 2
ANYWHERE = pl.BlockSpec(memory_space=pl.ANY)
IN_VMEM = pl.BlockSpec(memory_space=pltpu.VMEM)
IN_SMEM = pl.BlockSpec(memory_space=pltpu.SMEM)


def swapped(x, axis):
    return lax.ppermute(x, axis, [(i, i ^ 1) for i in range(lax.axis_size(axis))])


def complex_terms(left_real, left_imag, right_real, right_imag, pattern):
    first = jnp.einsum(pattern, left_real, right_real, precision=HIGH)
    second = jnp.einsum(pattern, left_imag, right_imag, precision=HIGH)
    mixed = jnp.einsum(pattern, left_real + left_imag, right_real + right_imag, precision=HIGH)
    return first, second, mixed


def general(left_factor, right_factor):
    idx_size = lax.axis_size("idx")
    half_size = lax.axis_size("half")
    left = left_factor[0]
    right = right_factor[0]
    _, local_batch, rows, inner = left.shape
    _, batch, inner_part, between = right.shape
    own_rows = rows // (idx_size * half_size)
    half_rows = rows // half_size
    half_cols = between // half_size
    is_lower = lax.axis_index("half") == 0
    scale = 1.0 / math.sqrt(2.0 * batch * between)
    pieces = right.reshape(2, idx_size, local_batch, inner_part, half_size, half_cols)
    split_rows = left.reshape(2, local_batch, idx_size, half_size, own_rows, inner)
    upper_rows = lax.ppermute(split_rows[:, :, :, 1], "half", [(0, 1)])
    other_whole = lax.ppermute(left, "half", [(1, 0)])
    first_left = jnp.where(is_lower, split_rows[:, :, :, 0], upper_rows)
    first_left = first_left.reshape(2, local_batch, half_rows, inner)
    second_left = jnp.where(is_lower, other_whole, left)
    totals = None
    for b in range(local_batch):
        outgoing = jnp.transpose(pieces[:, :, b], (1, 3, 0, 2, 4))
        outgoing = outgoing.reshape(idx_size * half_size, 2, inner_part, half_cols)
        arrived = lax.all_to_all(outgoing, ("idx", "half"), 0, 0, tiled=True)
        arrived = arrived.reshape(idx_size, half_size, 2, inner_part, half_cols)
        factors = jnp.transpose(arrived, (1, 2, 0, 3, 4)).reshape(2, 2, inner, half_cols)
        first, second, mixed = complex_terms(
            factors[0, 0], factors[0, 1], factors[1, 0], factors[1, 1], "kn,ln->kl"
        )
        core = jnp.stack([first - second, mixed - first - second]) * scale
        core = core + swapped(core, "half")
        first, second, mixed = complex_terms(
            first_left[0, b], first_left[1, b], core[0], core[1], "mk,kl->ml"
        )
        terms = complex_terms(
            first - second, mixed - first - second, second_left[0, b], second_left[1, b], "ml,ol->mo"
        )
        totals = terms if totals is None else [t + u for t, u in zip(totals, terms)]
    first, second, mixed = totals
    partial = jnp.stack([first - second, mixed - first - second], axis=1)
    return lax.psum_scatter(partial, "idx", scatter_dimension=0, tiled=True)


def split_float(x):
    high = x.astype(jnp.bfloat16)
    return high, (x - high.astype(jnp.float32)).astype(jnp.bfloat16)


def stacked(parts, axis):
    return jnp.concatenate(parts, axis=axis)


def left_stack(x, axis):
    high, low = split_float(x)
    return stacked([high, high, low], axis)


def right_stack(x, axis):
    high, low = split_float(x)
    return stacked([high, low, high], axis)


def dot_stacks(left, right, dims):
    return lax.dot_general(left, right, (dims, ((), ())), preferred_element_type=jnp.float32)


def complex_dot(left_real, left_imag, right_real, right_imag, dims):
    left_axis, right_axis = dims[0][0], dims[1][0]

    def term(left, right):
        return dot_stacks(left_stack(left, left_axis), right_stack(right, right_axis), dims)

    first = term(left_real, right_real)
    second = term(left_imag, right_imag)
    mixed = term(left_real + left_imag, right_real + right_imag)
    return first - second, mixed - first - second


BRIEF = pl.CostEstimate(flops=0, bytes_accessed=1024, transcendentals=0)
NT = ((1,), (1,))
NN = ((1,), (0,))


def deal_kernel(start, count, half_cols, right, out, sems):
    copies = []
    for half in range(2):
        for plane in range(2):
            source = right.at[plane, :, pl.ds(start, count), :, pl.ds(half * half_cols, half_cols)]
            copies.append(pltpu.make_async_copy(source, out.at[:, half, plane], sems.at[2 * half + plane]))
    for copy in copies:
        copy.start()
    for copy in copies:
        copy.wait()


def core_kernel(count, scale, arrived, core, factors, sems):
    inner = core.shape[2]
    copies = {}
    for b in range(count):
        for part in range(4):
            source = arrived.at[:, part // 2, part % 2, b]
            copies[b, part] = pltpu.make_async_copy(source, factors.at[b, part], sems.at[b, part])
            copies[b, part].start()
    for b in range(count):
        for part in range(4):
            copies[b, part].wait()
        planes = [factors[b, part].reshape(inner, factors.shape[4]) for part in range(4)]
        real, imag = complex_dot(*planes, NT)
        core[b, 0] = real * scale
        core[b, 1] = imag * scale


def amplitude_kernel(start, count, slots, n_before, n_out, place, own_core, other_core, *refs):
    own_split, other_split, own_flat, other_flat = refs[:4]
    before = refs[4 : 4 + n_before]
    outs = refs[4 + n_before : 4 + n_before + n_out]
    first, second, product, sems = refs[4 + n_before + n_out :]
    half, idx = place[0], place[1]
    _, _, groups, own_rows, inner = first.shape
    rows, columns = groups * own_rows, second.shape[2]

    def first_copy(lower, b, position, slot):
        source = own_split if lower else other_split
        return pltpu.make_async_copy(
            source.at[:, start + b, idx ^ slot, 0 if lower else 1], first.at[b, :, position], sems.at[0, b]
        )

    def second_copy(lower, b):
        source = other_flat if lower else own_flat
        return pltpu.make_async_copy(source.at[:, start + b], second.at[b], sems.at[1, b])

    for lower in (True, False):

        @pl.when(half == (0 if lower else 1))
        def _():
            for b in range(count):
                for position, slot in enumerate(slots):
                    first_copy(lower, b, position, slot).start()
                second_copy(lower, b).start()

    if not n_before:
        for out in outs:
            out[...] = jnp.zeros_like(out)
    piece = rows // n_out

    def one_value(b, carry):
        whole = own_split.at[:, start + b, :groups, 0]
        pltpu.make_async_copy(whole, first.at[b], sems.at[0, b]).wait()
        real, imag = complex_dot(
            first[b, 0].reshape(rows, inner),
            first[b, 1].reshape(rows, inner),
            own_core[b, 0] + other_core[b, 0],
            own_core[b, 1] + other_core[b, 1],
            NN,
        )
        for part, value in enumerate((real, imag, real + imag)):
            product[part] = left_stack(value, 1)
        second_copy(True, b).wait()
        for at in range(0, columns, 256):
            spot = slice(at, at + 256)
            right_real, right_imag = second[b, 0, spot], second[b, 1, spot]
            one = dot_stacks(product[0], right_stack(right_real, 1), NT)
            two = dot_stacks(product[1], right_stack(right_imag, 1), NT)
            three = dot_stacks(product[2], right_stack(right_real + right_imag, 1), NT)
            for plane, value in enumerate((one - two, three - one - two)):
                if n_before:
                    value = value + before[0][plane, :, spot]
                for number, out in enumerate(outs):
                    part = value[number * piece : (number + 1) * piece]
                    if n_before:
                        out[plane, :, spot] = part
                    else:
                        out[plane, :, spot] += part
        return carry

    if count == 1:
        one_value(0, 0)
    else:
        lax.fori_loop(0, count, one_value, 0)


def chunks_of(count):
    return count - 1, 1


def overlapped(left_factor, right_factor):
    idx_size = lax.axis_size("idx")
    _, _, local_batch, rows, inner = left_factor.shape
    _, _, batch, inner_part, between = right_factor.shape
    own_rows = rows // (idx_size * 2)
    half_rows = rows // 2
    half_cols = between // 2
    scale = 1.0 / math.sqrt(2.0 * batch * between)
    place = jnp.stack([lax.axis_index("half"), lax.axis_index("idx")]).astype(jnp.int32)
    depth = idx_size // 2
    right = right_factor.reshape(2, idx_size, local_batch, inner_part, between)
    params = pltpu.CompilerParams(vmem_limit_bytes=44 * MIB)
    small = pltpu.CompilerParams(vmem_limit_bytes=20 * MIB)
    shape = (2, local_batch, idx_size, 2, own_rows, inner)
    own_left = left_factor.reshape(shape)

    def dealt(start, count):
        return pl.pallas_call(
            functools.partial(deal_kernel, start, count, half_cols),
            out_shape=jax.ShapeDtypeStruct((idx_size, 2, 2, count, inner_part, half_cols), jnp.float32),
            in_specs=[ANYWHERE],
            out_specs=IN_VMEM,
            scratch_shapes=[pltpu.SemaphoreType.DMA((4,))],
            cost_estimate=BRIEF,
            compiler_params=pltpu.CompilerParams(vmem_limit_bytes=38 * MIB),
        )(right)

    def sent(pieces):
        flat = pieces.reshape(2 * idx_size, *pieces.shape[2:])
        return lax.all_to_all(flat, ("idx", "half"), 0, 0, tiled=True).reshape(pieces.shape)

    def core_of(count, arrived):
        return pl.pallas_call(
            functools.partial(core_kernel, count, scale),
            out_shape=jax.ShapeDtypeStruct((count, 2, inner, inner), jnp.float32),
            in_specs=[ANYWHERE],
            out_specs=IN_VMEM,
            scratch_shapes=[
                pltpu.VMEM((count, 4, idx_size, inner_part, half_cols), jnp.float32),
                pltpu.SemaphoreType.DMA((count, 4)),
            ],
            cost_estimate=BRIEF,
            compiler_params=params if count > 1 else small,
        )(arrived)

    def added(start, count, slots, n_out, core, other_core, other_left, before):
        flat = (2, local_batch, rows, inner)
        kept_rows = len(slots) * own_rows
        return pl.pallas_call(
            functools.partial(amplitude_kernel, start, count, slots, len(before), n_out),
            out_shape=[jax.ShapeDtypeStruct((2, kept_rows // n_out, rows), jnp.float32)] * n_out,
            in_specs=[IN_SMEM, IN_VMEM, IN_VMEM] + [ANYWHERE] * 4 + [IN_VMEM] * len(before),
            out_specs=[IN_VMEM] * n_out,
            scratch_shapes=[
                pltpu.VMEM((count, 2, len(slots), own_rows, inner), jnp.float32),
                pltpu.VMEM((count, 2, rows, inner), jnp.float32),
                pltpu.VMEM((3, kept_rows, 3 * inner), jnp.bfloat16),
                pltpu.SemaphoreType.DMA((2, count)),
            ],
            cost_estimate=BRIEF,
            compiler_params=params if count > 1 else small,
        )(
            place, core, other_core, own_left, other_left,
            own_left.reshape(flat), other_left.reshape(flat), *before,
        )

    def hop(x, mask):
        return lax.ppermute(x, "idx", [(i, i ^ mask) for i in range(idx_size)])

    many, few = chunks_of(local_batch)
    other_left = swapped(left_factor, "half").reshape(shape)
    arrived = sent(dealt(0, many))
    pieces = dealt(many, few)
    late = sent(pieces)
    arrived, pieces = lax.optimization_barrier((arrived, pieces))
    core = core_of(many, arrived)
    odd = list(range(idx_size - 1, 0, -2))
    even = [slot - 1 for slot in odd]
    sums = added(0, many, odd + even, 2, core, swapped(core, "half"), other_left, [])
    late, _ = lax.optimization_barrier((late, sums[0][0, :8, :128]))
    core = core_of(few, late)
    other_core = swapped(core, "half")
    leaving = added(many, few, odd, PIECES * depth, core, other_core, other_left, [sums[0]])
    core, leaving = lax.optimization_barrier((core, leaving))
    staying = added(many, few, even, PIECES * depth, core, other_core, other_left, [sums[1]])
    landed = [hop(block, 1) for block in leaving]
    blocks = [kept + block for kept, block in zip(staying, landed)]
    blocks = {even[n // PIECES] // 2: blocks[n : n + PIECES] for n in range(0, PIECES * depth, PIECES)}
    bit = 1
    while bit < depth:
        for d in sorted(blocks, reverse=True):
            if d & bit:
                coming = [hop(block, 2 * bit) for block in blocks.pop(d)]
                blocks[d ^ bit] = [mine + block for mine, block in zip(blocks[d ^ bit], coming)]
        bit *= 2
    return jnp.moveaxis(jnp.concatenate(blocks[0], axis=1), 0, 1)


def on_device(left_factor, right_factor):
    idx_size = lax.axis_size("idx")
    rows, inner_part, between = left_factor.shape[3], right_factor.shape[3], right_factor.shape[4]
    aligned = (
        lax.axis_size("half") == 2
        and left_factor.shape[2] > 1
        and idx_size in (2, 4, 8)
        and inner_part % 8 == 0
        and between % 256 == 0
        and rows % 256 == 0
        and rows % (32 * idx_size) == 0
        and 256 % (rows // idx_size) == 0
    )
    return (overlapped if aligned else general)(left_factor, right_factor)


def solution(mesh):
    return jax.shard_map(
        on_device,
        mesh=mesh,
        in_specs=(P("half", "cuts", "idx", None, None), P("half", "cuts", None, "idx", None)),
        out_specs=P(("idx", "half"), "cuts", None),
        check_vma=False,
    )
```

```python
import functools
import math

import jax
import jax.numpy as jnp
from jax import lax
from jax.experimental import pallas as pl
from jax.experimental.pallas import tpu as pltpu
from jax.sharding import PartitionSpec as P

HIGH = lax.Precision.HIGH
MIB = 1 << 20
PIECES = 2
WINDOW = 4
ANYWHERE = pl.BlockSpec(memory_space=pl.ANY)
IN_VMEM = pl.BlockSpec(memory_space=pltpu.VMEM)
IN_SMEM = pl.BlockSpec(memory_space=pltpu.SMEM)


def swapped(x, axis):
    return lax.ppermute(x, axis, [(i, i ^ 1) for i in range(lax.axis_size(axis))])


def complex_terms(left_real, left_imag, right_real, right_imag, pattern):
    first = jnp.einsum(pattern, left_real, right_real, precision=HIGH)
    second = jnp.einsum(pattern, left_imag, right_imag, precision=HIGH)
    mixed = jnp.einsum(pattern, left_real + left_imag, right_real + right_imag, precision=HIGH)
    return first, second, mixed


def general(left_factor, right_factor):
    idx_size = lax.axis_size("idx")
    half_size = lax.axis_size("half")
    left = left_factor[0]
    right = right_factor[0]
    _, local_batch, rows, inner = left.shape
    _, batch, inner_part, between = right.shape
    own_rows = rows // (idx_size * half_size)
    half_rows = rows // half_size
    half_cols = between // half_size
    is_lower = lax.axis_index("half") == 0
    scale = 1.0 / math.sqrt(2.0 * batch * between)
    pieces = right.reshape(2, idx_size, local_batch, inner_part, half_size, half_cols)
    split_rows = left.reshape(2, local_batch, idx_size, half_size, own_rows, inner)
    upper_rows = lax.ppermute(split_rows[:, :, :, 1], "half", [(0, 1)])
    other_whole = lax.ppermute(left, "half", [(1, 0)])
    first_left = jnp.where(is_lower, split_rows[:, :, :, 0], upper_rows)
    first_left = first_left.reshape(2, local_batch, half_rows, inner)
    second_left = jnp.where(is_lower, other_whole, left)
    totals = None
    for b in range(local_batch):
        outgoing = jnp.transpose(pieces[:, :, b], (1, 3, 0, 2, 4))
        outgoing = outgoing.reshape(idx_size * half_size, 2, inner_part, half_cols)
        arrived = lax.all_to_all(outgoing, ("idx", "half"), 0, 0, tiled=True)
        arrived = arrived.reshape(idx_size, half_size, 2, inner_part, half_cols)
        factors = jnp.transpose(arrived, (1, 2, 0, 3, 4)).reshape(2, 2, inner, half_cols)
        first, second, mixed = complex_terms(
            factors[0, 0], factors[0, 1], factors[1, 0], factors[1, 1], "kn,ln->kl"
        )
        core = jnp.stack([first - second, mixed - first - second]) * scale
        core = core + swapped(core, "half")
        first, second, mixed = complex_terms(
            first_left[0, b], first_left[1, b], core[0], core[1], "mk,kl->ml"
        )
        terms = complex_terms(
            first - second, mixed - first - second, second_left[0, b], second_left[1, b], "ml,ol->mo"
        )
        totals = terms if totals is None else [t + u for t, u in zip(totals, terms)]
    first, second, mixed = totals
    partial = jnp.stack([first - second, mixed - first - second], axis=1)
    return lax.psum_scatter(partial, "idx", scatter_dimension=0, tiled=True)


def split_float(x):
    high = x.astype(jnp.bfloat16)
    return high, (x - high.astype(jnp.float32)).astype(jnp.bfloat16)


def stacked(parts, axis):
    return jnp.concatenate(parts, axis=axis)


def left_stack(x, axis):
    high, low = split_float(x)
    return stacked([high, high, low], axis)


def right_stack(x, axis):
    high, low = split_float(x)
    return stacked([high, low, high], axis)


def dot_stacks(left, right, dims):
    return lax.dot_general(left, right, (dims, ((), ())), preferred_element_type=jnp.float32)


def complex_dot(left_real, left_imag, right_real, right_imag, dims):
    left_axis, right_axis = dims[0][0], dims[1][0]

    def term(left, right):
        return dot_stacks(left_stack(left, left_axis), right_stack(right, right_axis), dims)

    first = term(left_real, right_real)
    second = term(left_imag, right_imag)
    mixed = term(left_real + left_imag, right_real + right_imag)
    return first - second, mixed - first - second


BRIEF = pl.CostEstimate(flops=0, bytes_accessed=1024, transcendentals=0)
NT = ((1,), (1,))
NN = ((1,), (0,))


def deal_kernel(start, count, half_cols, right, out, sems):
    copies = []
    for half in range(2):
        for plane in range(2):
            source = right.at[plane, :, pl.ds(start, count), :, pl.ds(half * half_cols, half_cols)]
            copies.append(pltpu.make_async_copy(source, out.at[:, half, plane], sems.at[2 * half + plane]))
    for copy in copies:
        copy.start()
    for copy in copies:
        copy.wait()


def core_kernel(count, scale, arrived, *refs):
    core, factors, sems = refs[-3:]
    inner = core.shape[2]
    copies = {}
    for b in range(count):
        for part in range(4):
            source = arrived.at[:, part // 2, part % 2, b]
            copies[b, part] = pltpu.make_async_copy(source, factors.at[b, part], sems.at[b, part])
            copies[b, part].start()
    for b in range(count):
        for part in range(4):
            copies[b, part].wait()
        planes = [factors[b, part].reshape(inner, factors.shape[4]) for part in range(4)]
        real, imag = complex_dot(*planes, NT)
        core[b, 0] = real * scale
        core[b, 1] = imag * scale


def amplitude_kernel(start, count, slots, n_before, n_out, place, own_core, other_core, *refs):
    own_split, other_split, own_flat, other_flat = refs[:4]
    before = refs[4 : 4 + n_before]
    outs = refs[4 + n_before : 4 + n_before + n_out]
    first, second, product, sems, *more = refs[4 + n_before + n_out :]
    half, idx = place[0], place[1]
    _, _, groups, own_rows, inner = first.shape
    rows, columns = groups * own_rows, second.shape[2]

    def first_copy(lower, b, position, slot):
        source = own_split if lower else other_split
        return pltpu.make_async_copy(
            source.at[:, start + b, idx ^ slot, 0 if lower else 1], first.at[b, :, position], sems.at[0, b]
        )

    def second_copy(lower, b):
        source = other_flat if lower else own_flat
        return pltpu.make_async_copy(source.at[:, start + b], second.at[b], sems.at[1, b])

    for lower in (True, False):

        @pl.when(half == (0 if lower else 1))
        def _():
            for b in range(count):
                for position, slot in enumerate(slots):
                    first_copy(lower, b, position, slot).start()
                second_copy(lower, b).start()

    if n_before:
        held, held_sem = more
        loading = pltpu.make_async_copy(before[0], held, held_sem)
        loading.start()
    else:
        for out in outs:
            out[...] = jnp.zeros_like(out)
    piece = rows // n_out

    def one_value(b, carry):
        whole = own_split.at[:, start + b, :groups, 0]
        pltpu.make_async_copy(whole, first.at[b], sems.at[0, b]).wait()
        real, imag = complex_dot(
            first[b, 0].reshape(rows, inner),
            first[b, 1].reshape(rows, inner),
            own_core[b, 0] + other_core[b, 0],
            own_core[b, 1] + other_core[b, 1],
            NN,
        )
        for part, value in enumerate((real, imag, real + imag)):
            product[part] = left_stack(value, 1)
        second_copy(True, b).wait()
        if n_before:
            loading.wait()
        for at in range(0, columns, 256):
            spot = slice(at, at + 256)
            right_real, right_imag = second[b, 0, spot], second[b, 1, spot]
            one = dot_stacks(product[0], right_stack(right_real, 1), NT)
            two = dot_stacks(product[1], right_stack(right_imag, 1), NT)
            three = dot_stacks(product[2], right_stack(right_real + right_imag, 1), NT)
            for plane, value in enumerate((one - two, three - one - two)):
                if n_before:
                    value = value + held[plane, :, spot]
                for number, out in enumerate(outs):
                    part = value[number * piece : (number + 1) * piece]
                    if n_before:
                        out[plane, :, spot] = part
                    else:
                        out[plane, :, spot] += part
        return carry

    if count == 1:
        one_value(0, 0)
    else:
        lax.fori_loop(0, count, one_value, 0)


def chunks_of(count):
    return count - 1, 1


def overlapped(left_factor, right_factor):
    idx_size = lax.axis_size("idx")
    _, _, local_batch, rows, inner = left_factor.shape
    _, _, batch, inner_part, between = right_factor.shape
    own_rows = rows // (idx_size * 2)
    half_rows = rows // 2
    half_cols = between // 2
    scale = 1.0 / math.sqrt(2.0 * batch * between)
    place = jnp.stack([lax.axis_index("half"), lax.axis_index("idx")]).astype(jnp.int32)
    depth = idx_size // 2
    right = right_factor.reshape(2, idx_size, local_batch, inner_part, between)
    params = pltpu.CompilerParams(vmem_limit_bytes=44 * MIB)
    shape = (2, local_batch, idx_size, 2, own_rows, inner)
    own_left = left_factor.reshape(shape)

    def dealt(start, count):
        return pl.pallas_call(
            functools.partial(deal_kernel, start, count, half_cols),
            out_shape=jax.ShapeDtypeStruct((idx_size, 2, 2, count, inner_part, half_cols), jnp.float32),
            in_specs=[ANYWHERE],
            out_specs=IN_VMEM,
            scratch_shapes=[pltpu.SemaphoreType.DMA((4,))],
            cost_estimate=BRIEF,
            compiler_params=pltpu.CompilerParams(vmem_limit_bytes=38 * MIB),
        )(right)

    def sent(pieces):
        flat = pieces.reshape(2 * idx_size, *pieces.shape[2:])
        return lax.all_to_all(flat, ("idx", "half"), 0, 0, tiled=True).reshape(pieces.shape)

    def core_of(count, arrived, after=()):
        return pl.pallas_call(
            functools.partial(core_kernel, count, scale),
            out_shape=jax.ShapeDtypeStruct((count, 2, inner, inner), jnp.float32),
            in_specs=[ANYWHERE] + [IN_VMEM] * len(after),
            out_specs=IN_VMEM,
            scratch_shapes=[
                pltpu.VMEM((count, 4, idx_size, inner_part, half_cols), jnp.float32),
                pltpu.SemaphoreType.DMA((count, 4)),
            ],
            cost_estimate=BRIEF,
            compiler_params=params,
        )(arrived, *after)

    def added(start, count, slots, n_out, core, other_core, other_left, before):
        flat = (2, local_batch, rows, inner)
        kept_rows = len(slots) * own_rows
        return pl.pallas_call(
            functools.partial(amplitude_kernel, start, count, slots, len(before), n_out),
            out_shape=[jax.ShapeDtypeStruct((2, kept_rows // n_out, rows), jnp.float32)] * n_out,
            in_specs=[IN_SMEM, IN_VMEM, IN_VMEM] + [ANYWHERE] * (4 + len(before)),
            out_specs=[IN_VMEM] * n_out,
            scratch_shapes=[
                pltpu.VMEM((count, 2, len(slots), own_rows, inner), jnp.float32),
                pltpu.VMEM((count, 2, rows, inner), jnp.float32),
                pltpu.VMEM((3, kept_rows, 3 * inner), jnp.bfloat16),
                pltpu.SemaphoreType.DMA((2, count)),
            ]
            + [pltpu.VMEM(part.shape, jnp.float32) for part in before]
            + [pltpu.SemaphoreType.DMA] * len(before),
            cost_estimate=BRIEF,
            compiler_params=params,
        )(
            place, core, other_core, own_left, other_left,
            own_left.reshape(flat), other_left.reshape(flat), *before,
        )

    def hop(x, mask):
        return lax.ppermute(x, "idx", [(i, i ^ mask) for i in range(idx_size)])

    many, few = chunks_of(local_batch)
    other_left = swapped(left_factor, "half").reshape(shape)
    arrived = sent(dealt(0, many))
    pieces = dealt(many, few)
    late = sent(pieces)
    arrived, pieces = lax.optimization_barrier((arrived, pieces))
    core = core_of(many, arrived)
    odd = list(range(idx_size - 1, 0, -2))
    even = [slot - 1 for slot in odd]
    sums = added(0, many, odd + even, 2, core, swapped(core, "half"), other_left, [])
    core = core_of(few, late, (sums[0][0, :8, :128],))
    other_core = swapped(core, "half")
    leaving = added(many, few, odd, PIECES * depth, core, other_core, other_left, [sums[0]])
    core, leaving = lax.optimization_barrier((core, leaving))
    staying = list(added(many, few, even, PIECES * depth, core, other_core, other_left, [sums[1]]))
    mine, coming = [], {}
    for n, block in enumerate(leaving):
        if n >= WINDOW:
            block, mine[n - WINDOW] = lax.optimization_barrier((block, mine[n - WINDOW]))
        if n - WINDOW - 2 in coming:
            block, coming[n - WINDOW - 2] = lax.optimization_barrier((block, coming[n - WINDOW - 2]))
        mine.append(staying[n] + hop(block, 1))
        if even[n // PIECES] // 2 % 2:
            coming[n] = hop(mine[n], 2)
    for n, block in coming.items():
        target = n + PIECES
        mine[target] = mine[target] + block
    blocks = {even[n // PIECES] // 2: mine[n : n + PIECES] for n in range(0, PIECES * depth, PIECES)}
    bit = 2
    while bit < depth:
        for d in range(bit, depth, 2 * bit):
            arriving = [hop(block, 2 * bit) for block in blocks[d]]
            blocks[d - bit] = [block + new for block, new in zip(blocks[d - bit], arriving)]
        bit *= 2
    return jnp.moveaxis(jnp.concatenate(blocks[0], axis=1), 0, 1)


def on_device(left_factor, right_factor):
    idx_size = lax.axis_size("idx")
    rows, inner_part, between = left_factor.shape[3], right_factor.shape[3], right_factor.shape[4]
    aligned = (
        lax.axis_size("half") == 2
        and left_factor.shape[2] > 1
        and idx_size in (2, 4, 8)
        and inner_part % 8 == 0
        and between % 256 == 0
        and rows % 256 == 0
        and rows % (32 * idx_size) == 0
        and 256 % (rows // idx_size) == 0
    )
    return (overlapped if aligned else general)(left_factor, right_factor)


def solution(mesh):
    return jax.shard_map(
        on_device,
        mesh=mesh,
        in_specs=(P("half", "cuts", "idx", None, None), P("half", "cuts", None, "idx", None)),
        out_specs=P(("idx", "half"), "cuts", None),
        check_vma=False,
    )
```

```python
import functools
import math

import jax
import jax.numpy as jnp
from jax import lax
from jax.experimental import pallas as pl
from jax.experimental.pallas import tpu as pltpu
from jax.sharding import PartitionSpec as P

HIGH = lax.Precision.HIGH
MIB = 1 << 20
PIECES = 2
WINDOW = 4
ANYWHERE = pl.BlockSpec(memory_space=pl.ANY)
IN_VMEM = pl.BlockSpec(memory_space=pltpu.VMEM)
IN_SMEM = pl.BlockSpec(memory_space=pltpu.SMEM)


def swapped(x, axis):
    return lax.ppermute(x, axis, [(i, i ^ 1) for i in range(lax.axis_size(axis))])


def complex_terms(left_real, left_imag, right_real, right_imag, pattern):
    first = jnp.einsum(pattern, left_real, right_real, precision=HIGH)
    second = jnp.einsum(pattern, left_imag, right_imag, precision=HIGH)
    mixed = jnp.einsum(pattern, left_real + left_imag, right_real + right_imag, precision=HIGH)
    return first, second, mixed


def general(left_factor, right_factor):
    idx_size = lax.axis_size("idx")
    half_size = lax.axis_size("half")
    left = left_factor[0]
    right = right_factor[0]
    _, local_batch, rows, inner = left.shape
    _, batch, inner_part, between = right.shape
    own_rows = rows // (idx_size * half_size)
    half_rows = rows // half_size
    half_cols = between // half_size
    is_lower = lax.axis_index("half") == 0
    scale = 1.0 / math.sqrt(2.0 * batch * between)
    pieces = right.reshape(2, idx_size, local_batch, inner_part, half_size, half_cols)
    split_rows = left.reshape(2, local_batch, idx_size, half_size, own_rows, inner)
    upper_rows = lax.ppermute(split_rows[:, :, :, 1], "half", [(0, 1)])
    other_whole = lax.ppermute(left, "half", [(1, 0)])
    first_left = jnp.where(is_lower, split_rows[:, :, :, 0], upper_rows)
    first_left = first_left.reshape(2, local_batch, half_rows, inner)
    second_left = jnp.where(is_lower, other_whole, left)
    totals = None
    for b in range(local_batch):
        outgoing = jnp.transpose(pieces[:, :, b], (1, 3, 0, 2, 4))
        outgoing = outgoing.reshape(idx_size * half_size, 2, inner_part, half_cols)
        arrived = lax.all_to_all(outgoing, ("idx", "half"), 0, 0, tiled=True)
        arrived = arrived.reshape(idx_size, half_size, 2, inner_part, half_cols)
        factors = jnp.transpose(arrived, (1, 2, 0, 3, 4)).reshape(2, 2, inner, half_cols)
        first, second, mixed = complex_terms(
            factors[0, 0], factors[0, 1], factors[1, 0], factors[1, 1], "kn,ln->kl"
        )
        core = jnp.stack([first - second, mixed - first - second]) * scale
        core = core + swapped(core, "half")
        first, second, mixed = complex_terms(
            first_left[0, b], first_left[1, b], core[0], core[1], "mk,kl->ml"
        )
        terms = complex_terms(
            first - second, mixed - first - second, second_left[0, b], second_left[1, b], "ml,ol->mo"
        )
        totals = terms if totals is None else [t + u for t, u in zip(totals, terms)]
    first, second, mixed = totals
    partial = jnp.stack([first - second, mixed - first - second], axis=1)
    return lax.psum_scatter(partial, "idx", scatter_dimension=0, tiled=True)


def split_float(x):
    high = x.astype(jnp.bfloat16)
    return high, (x - high.astype(jnp.float32)).astype(jnp.bfloat16)


def stacked(parts, axis):
    return jnp.concatenate(parts, axis=axis)


def left_stack(x, axis):
    high, low = split_float(x)
    return stacked([high, high, low], axis)


def right_stack(x, axis):
    high, low = split_float(x)
    return stacked([high, low, high], axis)


def dot_stacks(left, right, dims):
    return lax.dot_general(left, right, (dims, ((), ())), preferred_element_type=jnp.float32)


def complex_dot(left_real, left_imag, right_real, right_imag, dims):
    left_axis, right_axis = dims[0][0], dims[1][0]

    def term(left, right):
        return dot_stacks(left_stack(left, left_axis), right_stack(right, right_axis), dims)

    first = term(left_real, right_real)
    second = term(left_imag, right_imag)
    mixed = term(left_real + left_imag, right_real + right_imag)
    return first - second, mixed - first - second


BRIEF = pl.CostEstimate(flops=0, bytes_accessed=1024, transcendentals=0)
NT = ((1,), (1,))
NN = ((1,), (0,))


def deal_kernel(start, count, half_cols, right, out, sems):
    copies = []
    for half in range(2):
        for plane in range(2):
            source = right.at[plane, :, pl.ds(start, count), :, pl.ds(half * half_cols, half_cols)]
            copies.append(pltpu.make_async_copy(source, out.at[:, half, plane], sems.at[2 * half + plane]))
    for copy in copies:
        copy.start()
    for copy in copies:
        copy.wait()


def core_kernel(count, scale, arrived, *refs):
    core, factors, sems = refs[-3:]
    inner = core.shape[2]
    copies = {}
    for b in range(count):
        for part in range(4):
            source = arrived.at[:, part // 2, part % 2, b]
            copies[b, part] = pltpu.make_async_copy(source, factors.at[b, part], sems.at[b, part])
            copies[b, part].start()
    for b in range(count):
        for part in range(4):
            copies[b, part].wait()
        planes = [factors[b, part].reshape(inner, factors.shape[4]) for part in range(4)]
        real, imag = complex_dot(*planes, NT)
        core[b, 0] = real * scale
        core[b, 1] = imag * scale


def amplitude_kernel(start, count, slots, n_before, sizes, place, own_core, other_core, *refs):
    n_out = len(sizes)
    own_split, other_split, own_flat, other_flat = refs[:4]
    before = refs[4 : 4 + n_before]
    outs = refs[4 + n_before : 4 + n_before + n_out]
    first, second, product, sems, *more = refs[4 + n_before + n_out :]
    half, idx = place[0], place[1]
    _, _, groups, own_rows, inner = first.shape
    rows, columns = groups * own_rows, second.shape[2]

    def first_copy(lower, b, position, slot):
        source = own_split if lower else other_split
        return pltpu.make_async_copy(
            source.at[:, start + b, idx ^ slot, 0 if lower else 1], first.at[b, :, position], sems.at[0, b]
        )

    def second_copy(lower, b):
        source = other_flat if lower else own_flat
        return pltpu.make_async_copy(source.at[:, start + b], second.at[b], sems.at[1, b])

    for lower in (True, False):

        @pl.when(half == (0 if lower else 1))
        def _():
            for b in range(count):
                for position, slot in enumerate(slots):
                    first_copy(lower, b, position, slot).start()
                second_copy(lower, b).start()

    if n_before:
        held, held_sem = more
        loading = pltpu.make_async_copy(before[0], held, held_sem)
        loading.start()
    else:
        for out in outs:
            out[...] = jnp.zeros_like(out)
    offsets = [sum(sizes[:n]) for n in range(n_out)]

    def one_value(b, carry):
        whole = own_split.at[:, start + b, :groups, 0]
        pltpu.make_async_copy(whole, first.at[b], sems.at[0, b]).wait()
        real, imag = complex_dot(
            first[b, 0].reshape(rows, inner),
            first[b, 1].reshape(rows, inner),
            own_core[b, 0] + other_core[b, 0],
            own_core[b, 1] + other_core[b, 1],
            NN,
        )
        for part, value in enumerate((real, imag, real + imag)):
            product[part] = left_stack(value, 1)
        second_copy(True, b).wait()
        if n_before:
            loading.wait()
        for at in range(0, columns, 256):
            spot = slice(at, at + 256)
            right_real, right_imag = second[b, 0, spot], second[b, 1, spot]
            one = dot_stacks(product[0], right_stack(right_real, 1), NT)
            two = dot_stacks(product[1], right_stack(right_imag, 1), NT)
            three = dot_stacks(product[2], right_stack(right_real + right_imag, 1), NT)
            for plane, value in enumerate((one - two, three - one - two)):
                if n_before:
                    value = value + held[plane, :, spot]
                for number, out in enumerate(outs):
                    part = value[offsets[number] : offsets[number] + sizes[number]]
                    if n_before:
                        out[plane, :, spot] = part
                    else:
                        out[plane, :, spot] += part
        return carry

    if count == 1:
        one_value(0, 0)
    else:
        lax.fori_loop(0, count, one_value, 0)


def chunks_of(count):
    return count - 1, 1


def overlapped(left_factor, right_factor):
    idx_size = lax.axis_size("idx")
    _, _, local_batch, rows, inner = left_factor.shape
    _, _, batch, inner_part, between = right_factor.shape
    own_rows = rows // (idx_size * 2)
    half_rows = rows // 2
    half_cols = between // 2
    scale = 1.0 / math.sqrt(2.0 * batch * between)
    place = jnp.stack([lax.axis_index("half"), lax.axis_index("idx")]).astype(jnp.int32)
    depth = idx_size // 2
    right = right_factor.reshape(2, idx_size, local_batch, inner_part, between)
    params = pltpu.CompilerParams(vmem_limit_bytes=44 * MIB)
    shape = (2, local_batch, idx_size, 2, own_rows, inner)
    own_left = left_factor.reshape(shape)

    def dealt(start, count):
        return pl.pallas_call(
            functools.partial(deal_kernel, start, count, half_cols),
            out_shape=jax.ShapeDtypeStruct((idx_size, 2, 2, count, inner_part, half_cols), jnp.float32),
            in_specs=[ANYWHERE],
            out_specs=IN_VMEM,
            scratch_shapes=[pltpu.SemaphoreType.DMA((4,))],
            cost_estimate=BRIEF,
            compiler_params=pltpu.CompilerParams(vmem_limit_bytes=38 * MIB),
        )(right)

    def sent(pieces):
        flat = pieces.reshape(2 * idx_size, *pieces.shape[2:])
        return lax.all_to_all(flat, ("idx", "half"), 0, 0, tiled=True).reshape(pieces.shape)

    def core_of(count, arrived, after=()):
        return pl.pallas_call(
            functools.partial(core_kernel, count, scale),
            out_shape=jax.ShapeDtypeStruct((count, 2, inner, inner), jnp.float32),
            in_specs=[ANYWHERE] + [IN_VMEM] * len(after),
            out_specs=IN_VMEM,
            scratch_shapes=[
                pltpu.VMEM((count, 4, idx_size, inner_part, half_cols), jnp.float32),
                pltpu.SemaphoreType.DMA((count, 4)),
            ],
            cost_estimate=BRIEF,
            compiler_params=params,
        )(arrived, *after)

    def added(start, count, slots, sizes, core, other_core, other_left, before):
        flat = (2, local_batch, rows, inner)
        kept_rows = len(slots) * own_rows
        return pl.pallas_call(
            functools.partial(amplitude_kernel, start, count, slots, len(before), sizes),
            out_shape=[jax.ShapeDtypeStruct((2, size, rows), jnp.float32) for size in sizes],
            in_specs=[IN_SMEM, IN_VMEM, IN_VMEM] + [ANYWHERE] * (4 + len(before)),
            out_specs=[IN_VMEM] * len(sizes),
            scratch_shapes=[
                pltpu.VMEM((count, 2, len(slots), own_rows, inner), jnp.float32),
                pltpu.VMEM((count, 2, rows, inner), jnp.float32),
                pltpu.VMEM((3, kept_rows, 3 * inner), jnp.bfloat16),
                pltpu.SemaphoreType.DMA((2, count)),
            ]
            + [pltpu.VMEM(part.shape, jnp.float32) for part in before]
            + [pltpu.SemaphoreType.DMA] * len(before),
            cost_estimate=BRIEF,
            compiler_params=params,
        )(
            place, core, other_core, own_left, other_left,
            own_left.reshape(flat), other_left.reshape(flat), *before,
        )

    def hop(x, mask):
        return lax.ppermute(x, "idx", [(i, i ^ mask) for i in range(idx_size)])

    many, few = chunks_of(local_batch)
    other_left = swapped(left_factor, "half").reshape(shape)
    arrived = sent(dealt(0, many))
    pieces = dealt(many, few)
    late = sent(pieces)
    arrived, pieces = lax.optimization_barrier((arrived, pieces))
    core = core_of(many, arrived)
    odd = list(range(idx_size - 1, 0, -2))
    even = [slot - 1 for slot in odd]
    sums = added(0, many, odd + even, [half_rows // 2] * 2, core, swapped(core, "half"), other_left, [])
    core = core_of(few, late, (sums[0][0, :8, :128],))
    other_core = swapped(core, "half")
    sizes = [own_rows * 3 // 8] * PIECES + [own_rows // 4]
    stride = len(sizes)
    leaving = added(many, few, odd, sizes * depth, core, other_core, other_left, [sums[0]])
    core, leaving = lax.optimization_barrier((core, leaving))
    staying = added(many, few, even, sizes * depth, core, other_core, other_left, [sums[1]])
    far_of = [slot // 2 for slot in even]

    def halved(parts, bit):
        while bit < depth:
            for d in range(bit, depth, 2 * bit):
                parts[d - bit] = parts[d - bit] + hop(parts[d], 2 * bit)
            bit *= 2
        return parts[0]

    last_leaving = halved({d: leaving[at * stride + PIECES] for at, d in enumerate(far_of)}, 1)
    last_staying = halved({d: staying[at * stride + PIECES] for at, d in enumerate(far_of)}, 1)
    last_coming = None
    mine, coming = [], {}
    count = PIECES * depth
    for n in range(count):
        at, part = n // PIECES, n % PIECES
        block = leaving[at * stride + part]
        if n >= WINDOW:
            block, mine[n - WINDOW] = lax.optimization_barrier((block, mine[n - WINDOW]))
        if n - WINDOW - 2 in coming:
            block, coming[n - WINDOW - 2] = lax.optimization_barrier((block, coming[n - WINDOW - 2]))
        if n == count - 1:
            block, last_leaving = lax.optimization_barrier((block, last_leaving))
            last_coming = hop(last_leaving, 1)
        mine.append(staying[at * stride + part] + hop(block, 1))
        if far_of[at] % 2:
            coming[n] = hop(mine[n], 2)
    for n, block in coming.items():
        target = n + PIECES
        mine[target] = mine[target] + block
    parts = [
        halved({d: mine[at * PIECES + part] for at, d in enumerate(far_of) if d % 2 == 0}, 2)
        for part in range(PIECES)
    ]
    result = jnp.concatenate(parts + [last_staying + last_coming], axis=1)
    return jnp.moveaxis(result, 0, 1)


def on_device(left_factor, right_factor):
    idx_size = lax.axis_size("idx")
    rows, inner_part, between = left_factor.shape[3], right_factor.shape[3], right_factor.shape[4]
    aligned = (
        lax.axis_size("half") == 2
        and left_factor.shape[2] > 1
        and idx_size in (2, 4, 8)
        and inner_part % 8 == 0
        and between % 256 == 0
        and rows % 256 == 0
        and rows % (128 * idx_size) == 0
        and 256 % (rows // idx_size) == 0
    )
    return (overlapped if aligned else general)(left_factor, right_factor)


def solution(mesh):
    return jax.shard_map(
        on_device,
        mesh=mesh,
        in_specs=(P("half", "cuts", "idx", None, None), P("half", "cuts", None, "idx", None)),
        out_specs=P(("idx", "half"), "cuts", None),
        check_vma=False,
    )
```

```python
import functools
import math

import jax
import jax.numpy as jnp
from jax import lax
from jax.experimental import pallas as pl
from jax.experimental.pallas import tpu as pltpu
from jax.sharding import PartitionSpec as P

HIGH = lax.Precision.HIGH
MIB = 1 << 20
PIECES = 2
WINDOW = 4
ANYWHERE = pl.BlockSpec(memory_space=pl.ANY)
IN_HBM = pl.BlockSpec(memory_space=pltpu.HBM)
IN_VMEM = pl.BlockSpec(memory_space=pltpu.VMEM)
IN_SMEM = pl.BlockSpec(memory_space=pltpu.SMEM)


def swapped(x, axis):
    return lax.ppermute(x, axis, [(i, i ^ 1) for i in range(lax.axis_size(axis))])


def complex_terms(left_real, left_imag, right_real, right_imag, pattern):
    first = jnp.einsum(pattern, left_real, right_real, precision=HIGH)
    second = jnp.einsum(pattern, left_imag, right_imag, precision=HIGH)
    mixed = jnp.einsum(pattern, left_real + left_imag, right_real + right_imag, precision=HIGH)
    return first, second, mixed


def general(left_factor, right_factor):
    idx_size = lax.axis_size("idx")
    half_size = lax.axis_size("half")
    left = left_factor[0]
    right = right_factor[0]
    _, local_batch, rows, inner = left.shape
    _, batch, inner_part, between = right.shape
    own_rows = rows // (idx_size * half_size)
    half_rows = rows // half_size
    half_cols = between // half_size
    is_lower = lax.axis_index("half") == 0
    scale = 1.0 / math.sqrt(2.0 * batch * between)
    pieces = right.reshape(2, idx_size, local_batch, inner_part, half_size, half_cols)
    split_rows = left.reshape(2, local_batch, idx_size, half_size, own_rows, inner)
    upper_rows = lax.ppermute(split_rows[:, :, :, 1], "half", [(0, 1)])
    other_whole = lax.ppermute(left, "half", [(1, 0)])
    first_left = jnp.where(is_lower, split_rows[:, :, :, 0], upper_rows)
    first_left = first_left.reshape(2, local_batch, half_rows, inner)
    second_left = jnp.where(is_lower, other_whole, left)
    totals = None
    for b in range(local_batch):
        outgoing = jnp.transpose(pieces[:, :, b], (1, 3, 0, 2, 4))
        outgoing = outgoing.reshape(idx_size * half_size, 2, inner_part, half_cols)
        arrived = lax.all_to_all(outgoing, ("idx", "half"), 0, 0, tiled=True)
        arrived = arrived.reshape(idx_size, half_size, 2, inner_part, half_cols)
        factors = jnp.transpose(arrived, (1, 2, 0, 3, 4)).reshape(2, 2, inner, half_cols)
        first, second, mixed = complex_terms(
            factors[0, 0], factors[0, 1], factors[1, 0], factors[1, 1], "kn,ln->kl"
        )
        core = jnp.stack([first - second, mixed - first - second]) * scale
        core = core + swapped(core, "half")
        first, second, mixed = complex_terms(
            first_left[0, b], first_left[1, b], core[0], core[1], "mk,kl->ml"
        )
        terms = complex_terms(
            first - second, mixed - first - second, second_left[0, b], second_left[1, b], "ml,ol->mo"
        )
        totals = terms if totals is None else [t + u for t, u in zip(totals, terms)]
    first, second, mixed = totals
    partial = jnp.stack([first - second, mixed - first - second], axis=1)
    return lax.psum_scatter(partial, "idx", scatter_dimension=0, tiled=True)


def split_float(x):
    high = x.astype(jnp.bfloat16)
    return high, (x - high.astype(jnp.float32)).astype(jnp.bfloat16)


def stacked(parts, axis):
    return jnp.concatenate(parts, axis=axis)


def left_stack(x, axis):
    high, low = split_float(x)
    return stacked([high, high, low], axis)


def right_stack(x, axis):
    high, low = split_float(x)
    return stacked([high, low, high], axis)


def dot_stacks(left, right, dims):
    return lax.dot_general(left, right, (dims, ((), ())), preferred_element_type=jnp.float32)


def complex_dot(left_real, left_imag, right_real, right_imag, dims):
    left_axis, right_axis = dims[0][0], dims[1][0]

    def term(left, right):
        return dot_stacks(left_stack(left, left_axis), right_stack(right, right_axis), dims)

    first = term(left_real, right_real)
    second = term(left_imag, right_imag)
    mixed = term(left_real + left_imag, right_real + right_imag)
    return first - second, mixed - first - second


BRIEF = pl.CostEstimate(flops=0, bytes_accessed=1024, transcendentals=0)
NT = ((1,), (1,))
NN = ((1,), (0,))


def deal_kernel(start, count, half_cols, right, out, held, in_sems, out_sems):
    incoming, leaving = [], []
    for to in range(out.shape[0]):
        for part in range(4):
            column = part // 2 * half_cols
            source = right.at[part % 2, to, start : start + count, :, column : column + half_cols]
            target = held.at[to, part // 2, part % 2]
            incoming.append(pltpu.make_async_copy(source, target, in_sems.at[to, part]))
            incoming[-1].start()
    for to in range(out.shape[0]):
        for part in range(4):
            incoming[4 * to + part].wait()
        leaving.append(pltpu.make_async_copy(held.at[to], out.at[to], out_sems.at[to]))
        leaving[-1].start()
    for copy in leaving:
        copy.wait()


def core_kernel(start, count, scale, arrived, *refs):
    core, factors, sems = refs[-3:]
    inner = core.shape[2]
    copies = {}
    for b in range(count):
        for part in range(4):
            source = arrived.at[:, part // 2, part % 2, start + b]
            copies[b, part] = pltpu.make_async_copy(source, factors.at[b, part], sems.at[b, part])
            copies[b, part].start()
    for b in range(count):
        for part in range(4):
            copies[b, part].wait()
        planes = [factors[b, part].reshape(inner, factors.shape[4]) for part in range(4)]
        real, imag = complex_dot(*planes, NT)
        core[b, 0] = real * scale
        core[b, 1] = imag * scale


def amplitude_kernel(start, n_cores, slots, n_before, n_out, place, *refs):
    own_cores, other_cores, refs = refs[:n_cores], refs[n_cores : 2 * n_cores], refs[2 * n_cores :]
    count = sum(core.shape[0] for core in own_cores)
    own_split, other_split, own_flat, other_flat = refs[:4]
    before = refs[4 : 4 + n_before]
    outs = refs[4 + n_before : 4 + n_before + n_out]
    first, second, product, sems, *more = refs[4 + n_before + n_out :]
    half, idx = place[0], place[1]
    _, _, groups, own_rows, inner = first.shape
    rows, columns = groups * own_rows, second.shape[2]

    def first_copy(lower, b, position, slot):
        source = own_split if lower else other_split
        return pltpu.make_async_copy(
            source.at[:, start + b, idx ^ slot, 0 if lower else 1], first.at[b, :, position], sems.at[0, b]
        )

    def second_copy(lower, b):
        source = other_flat if lower else own_flat
        return pltpu.make_async_copy(source.at[:, start + b], second.at[b], sems.at[1, b])

    for lower in (True, False):

        @pl.when(half == (0 if lower else 1))
        def _():
            for b in range(count):
                for position, slot in enumerate(slots):
                    first_copy(lower, b, position, slot).start()
                second_copy(lower, b).start()

    if n_before:
        held, held_sem = more
        loading = pltpu.make_async_copy(before[0], held, held_sem)
        loading.start()
    else:
        for out in outs:
            out[...] = jnp.zeros_like(out)
    piece = rows // n_out

    def one_value(own_core, other_core, first_b, at_b, carry):
        b = first_b + at_b
        whole = own_split.at[:, start + b, :groups, 0]
        pltpu.make_async_copy(whole, first.at[b], sems.at[0, b]).wait()
        real, imag = complex_dot(
            first[b, 0].reshape(rows, inner),
            first[b, 1].reshape(rows, inner),
            own_core[at_b, 0] + other_core[at_b, 0],
            own_core[at_b, 1] + other_core[at_b, 1],
            NN,
        )
        for part, value in enumerate((real, imag, real + imag)):
            product[part] = left_stack(value, 1)
        second_copy(True, b).wait()
        if n_before:
            loading.wait()
        for at in range(0, columns, 256):
            spot = slice(at, at + 256)
            right_real, right_imag = second[b, 0, spot], second[b, 1, spot]
            one = dot_stacks(product[0], right_stack(right_real, 1), NT)
            two = dot_stacks(product[1], right_stack(right_imag, 1), NT)
            three = dot_stacks(product[2], right_stack(right_real + right_imag, 1), NT)
            for plane, value in enumerate((one - two, three - one - two)):
                if n_before:
                    value = value + held[plane, :, spot]
                for number, out in enumerate(outs):
                    part = value[number * piece : (number + 1) * piece]
                    if n_before:
                        out[plane, :, spot] = part
                    else:
                        out[plane, :, spot] += part
        return carry

    first_b = 0
    for own_core, other_core in zip(own_cores, other_cores):
        values = functools.partial(one_value, own_core, other_core, first_b)
        if own_core.shape[0] == 1:
            values(0, 0)
        else:
            lax.fori_loop(0, own_core.shape[0], values, 0)
        first_b += own_core.shape[0]


def chunks_of(count):
    return count - 1, 1


def overlapped(left_factor, right_factor):
    idx_size = lax.axis_size("idx")
    _, _, local_batch, rows, inner = left_factor.shape
    _, _, batch, inner_part, between = right_factor.shape
    own_rows = rows // (idx_size * 2)
    half_rows = rows // 2
    half_cols = between // 2
    scale = 1.0 / math.sqrt(2.0 * batch * between)
    place = jnp.stack([lax.axis_index("half"), lax.axis_index("idx")]).astype(jnp.int32)
    depth = idx_size // 2
    right = right_factor.reshape(2, idx_size, local_batch, inner_part, between)
    params = pltpu.CompilerParams(vmem_limit_bytes=44 * MIB)
    shape = (2, local_batch, idx_size, 2, own_rows, inner)
    own_left = left_factor.reshape(shape)

    def dealt(start, count):
        laid = (idx_size, 2, 2, count, inner_part, half_cols)
        return pl.pallas_call(
            functools.partial(deal_kernel, start, count, half_cols),
            out_shape=jax.ShapeDtypeStruct(laid, jnp.float32),
            in_specs=[ANYWHERE],
            out_specs=IN_HBM,
            scratch_shapes=[
                pltpu.VMEM(laid, jnp.float32),
                pltpu.SemaphoreType.DMA((idx_size, 4)),
                pltpu.SemaphoreType.DMA((idx_size,)),
            ],
            cost_estimate=BRIEF,
            compiler_params=params,
        )(right)

    def sent(pieces):
        flat = pieces.reshape(2 * idx_size, *pieces.shape[2:])
        return lax.all_to_all(flat, ("idx", "half"), 0, 0, tiled=True).reshape(pieces.shape)

    def core_of(start, count, arrived, after=()):
        return pl.pallas_call(
            functools.partial(core_kernel, start, count, scale),
            out_shape=jax.ShapeDtypeStruct((count, 2, inner, inner), jnp.float32),
            in_specs=[ANYWHERE] + [IN_VMEM] * len(after),
            out_specs=IN_VMEM,
            scratch_shapes=[
                pltpu.VMEM((count, 4, idx_size, inner_part, half_cols), jnp.float32),
                pltpu.SemaphoreType.DMA((count, 4)),
            ],
            cost_estimate=BRIEF,
            compiler_params=params,
        )(arrived, *after)

    def added(start, count, slots, n_out, cores, other_cores, other_left, before):
        flat = (2, local_batch, rows, inner)
        kept_rows = len(slots) * own_rows
        return pl.pallas_call(
            functools.partial(amplitude_kernel, start, len(cores), slots, len(before), n_out),
            out_shape=[jax.ShapeDtypeStruct((2, kept_rows // n_out, rows), jnp.float32)] * n_out,
            in_specs=[IN_SMEM] + [IN_VMEM] * (2 * len(cores)) + [ANYWHERE] * (4 + len(before)),
            out_specs=[IN_VMEM] * n_out,
            scratch_shapes=[
                pltpu.VMEM((count, 2, len(slots), own_rows, inner), jnp.float32),
                pltpu.VMEM((count, 2, rows, inner), jnp.float32),
                pltpu.VMEM((3, kept_rows, 3 * inner), jnp.bfloat16),
                pltpu.SemaphoreType.DMA((2, count)),
            ]
            + [pltpu.VMEM(part.shape, jnp.float32) for part in before]
            + [pltpu.SemaphoreType.DMA] * len(before),
            cost_estimate=BRIEF,
            compiler_params=params,
        )(
            place, *cores, *other_cores, own_left, other_left,
            own_left.reshape(flat), other_left.reshape(flat), *before,
        )

    def hop(x, mask):
        return lax.ppermute(x, "idx", [(i, i ^ mask) for i in range(idx_size)])

    many, few = chunks_of(local_batch)
    other_left = swapped(left_factor, "half").reshape(shape)
    arrived = sent(dealt(0, many))
    pieces = dealt(many, few)
    late = sent(pieces)
    arrived, pieces = lax.optimization_barrier((arrived, pieces))
    share = (many + 1) // 2
    cores = [core_of(0, share, arrived)]
    swaps = [swapped(cores[0], "half")]
    if many > share:
        cores.append(core_of(share, many - share, arrived))
        swaps.append(swapped(cores[1], "half"))
    odd = list(range(idx_size - 1, 0, -2))
    even = [slot - 1 for slot in odd]
    sums = added(0, many, odd + even, 2, cores, swaps, other_left, [])
    core = core_of(0, few, late, (sums[0][0, :8, :128],))
    other_core = swapped(core, "half")
    leaving = added(many, few, odd, PIECES * depth, [core], [other_core], other_left, [sums[0]])
    core, leaving = lax.optimization_barrier((core, leaving))
    staying = list(added(many, few, even, PIECES * depth, [core], [other_core], other_left, [sums[1]]))
    mine, coming = [], {}
    for n, block in enumerate(leaving):
        if n >= WINDOW:
            block, mine[n - WINDOW] = lax.optimization_barrier((block, mine[n - WINDOW]))
        if n - WINDOW - 2 in coming:
            block, coming[n - WINDOW - 2] = lax.optimization_barrier((block, coming[n - WINDOW - 2]))
        mine.append(staying[n] + hop(block, 1))
        if even[n // PIECES] // 2 % 2:
            coming[n] = hop(mine[n], 2)
    for n, block in coming.items():
        target = n + PIECES
        mine[target] = mine[target] + block
    blocks = {even[n // PIECES] // 2: mine[n : n + PIECES] for n in range(0, PIECES * depth, PIECES)}
    bit = 2
    while bit < depth:
        for d in range(bit, depth, 2 * bit):
            arriving = [hop(block, 2 * bit) for block in blocks[d]]
            blocks[d - bit] = [block + new for block, new in zip(blocks[d - bit], arriving)]
        bit *= 2
    return jnp.moveaxis(jnp.concatenate(blocks[0], axis=1), 0, 1)


def on_device(left_factor, right_factor):
    idx_size = lax.axis_size("idx")
    rows, inner_part, between = left_factor.shape[3], right_factor.shape[3], right_factor.shape[4]
    aligned = (
        lax.axis_size("half") == 2
        and left_factor.shape[2] > 1
        and idx_size in (2, 4, 8)
        and inner_part % 8 == 0
        and between % 256 == 0
        and rows % 256 == 0
        and rows % (32 * idx_size) == 0
        and 256 % (rows // idx_size) == 0
    )
    return (overlapped if aligned else general)(left_factor, right_factor)


def solution(mesh):
    return jax.shard_map(
        on_device,
        mesh=mesh,
        in_specs=(P("half", "cuts", "idx", None, None), P("half", "cuts", None, "idx", None)),
        out_specs=P(("idx", "half"), "cuts", None),
        check_vma=False,
    )
```

```python
import functools
import math

import jax
import jax.numpy as jnp
from jax import lax
from jax.experimental import pallas as pl
from jax.experimental.pallas import tpu as pltpu
from jax.sharding import PartitionSpec as P

HIGH = lax.Precision.HIGH
MIB = 1 << 20
PIECES = 2
WINDOW = 3
ANYWHERE = pl.BlockSpec(memory_space=pl.ANY)
IN_VMEM = pl.BlockSpec(memory_space=pltpu.VMEM)
IN_SMEM = pl.BlockSpec(memory_space=pltpu.SMEM)


def swapped(x, axis):
    return lax.ppermute(x, axis, [(i, i ^ 1) for i in range(lax.axis_size(axis))])


def complex_terms(left_real, left_imag, right_real, right_imag, pattern):
    first = jnp.einsum(pattern, left_real, right_real, precision=HIGH)
    second = jnp.einsum(pattern, left_imag, right_imag, precision=HIGH)
    mixed = jnp.einsum(pattern, left_real + left_imag, right_real + right_imag, precision=HIGH)
    return first, second, mixed


def general(left_factor, right_factor):
    idx_size = lax.axis_size("idx")
    half_size = lax.axis_size("half")
    left = left_factor[0]
    right = right_factor[0]
    _, local_batch, rows, inner = left.shape
    _, batch, inner_part, between = right.shape
    own_rows = rows // (idx_size * half_size)
    half_rows = rows // half_size
    half_cols = between // half_size
    is_lower = lax.axis_index("half") == 0
    scale = 1.0 / math.sqrt(2.0 * batch * between)
    pieces = right.reshape(2, idx_size, local_batch, inner_part, half_size, half_cols)
    split_rows = left.reshape(2, local_batch, idx_size, half_size, own_rows, inner)
    upper_rows = lax.ppermute(split_rows[:, :, :, 1], "half", [(0, 1)])
    other_whole = lax.ppermute(left, "half", [(1, 0)])
    first_left = jnp.where(is_lower, split_rows[:, :, :, 0], upper_rows)
    first_left = first_left.reshape(2, local_batch, half_rows, inner)
    second_left = jnp.where(is_lower, other_whole, left)
    totals = None
    for b in range(local_batch):
        outgoing = jnp.transpose(pieces[:, :, b], (1, 3, 0, 2, 4))
        outgoing = outgoing.reshape(idx_size * half_size, 2, inner_part, half_cols)
        arrived = lax.all_to_all(outgoing, ("idx", "half"), 0, 0, tiled=True)
        arrived = arrived.reshape(idx_size, half_size, 2, inner_part, half_cols)
        factors = jnp.transpose(arrived, (1, 2, 0, 3, 4)).reshape(2, 2, inner, half_cols)
        first, second, mixed = complex_terms(
            factors[0, 0], factors[0, 1], factors[1, 0], factors[1, 1], "kn,ln->kl"
        )
        core = jnp.stack([first - second, mixed - first - second]) * scale
        core = core + swapped(core, "half")
        first, second, mixed = complex_terms(
            first_left[0, b], first_left[1, b], core[0], core[1], "mk,kl->ml"
        )
        terms = complex_terms(
            first - second, mixed - first - second, second_left[0, b], second_left[1, b], "ml,ol->mo"
        )
        totals = terms if totals is None else [t + u for t, u in zip(totals, terms)]
    first, second, mixed = totals
    partial = jnp.stack([first - second, mixed - first - second], axis=1)
    return lax.psum_scatter(partial, "idx", scatter_dimension=0, tiled=True)


def split_float(x):
    high = x.astype(jnp.bfloat16)
    return high, (x - high.astype(jnp.float32)).astype(jnp.bfloat16)


def stacked(parts, axis):
    return jnp.concatenate(parts, axis=axis)


def left_stack(x, axis):
    high, low = split_float(x)
    return stacked([high, high, low], axis)


def right_stack(x, axis):
    high, low = split_float(x)
    return stacked([high, low, high], axis)


def dot_stacks(left, right, dims):
    return lax.dot_general(left, right, (dims, ((), ())), preferred_element_type=jnp.float32)


def complex_dot(left_real, left_imag, right_real, right_imag, dims):
    left_axis, right_axis = dims[0][0], dims[1][0]

    def term(left, right):
        return dot_stacks(left_stack(left, left_axis), right_stack(right, right_axis), dims)

    first = term(left_real, right_real)
    second = term(left_imag, right_imag)
    mixed = term(left_real + left_imag, right_real + right_imag)
    return first - second, mixed - first - second


BRIEF = pl.CostEstimate(flops=0, bytes_accessed=1024, transcendentals=0)
NT = ((1,), (1,))
NN = ((1,), (0,))


def deal_kernel(start, count, half_cols, right, out, sems):
    copies = []
    for half in range(2):
        for plane in range(2):
            source = right.at[plane, :, pl.ds(start, count), :, pl.ds(half * half_cols, half_cols)]
            copies.append(pltpu.make_async_copy(source, out.at[:, half, plane], sems.at[2 * half + plane]))
    for copy in copies:
        copy.start()
    for copy in copies:
        copy.wait()


def core_kernel(count, scale, arrived, *refs):
    core, factors, sems = refs[-3:]
    inner = core.shape[2]
    copies = {}
    for b in range(count):
        for part in range(4):
            source = arrived.at[:, part // 2, part % 2, b]
            copies[b, part] = pltpu.make_async_copy(source, factors.at[b, part], sems.at[b, part])
            copies[b, part].start()
    for b in range(count):
        for part in range(4):
            copies[b, part].wait()
        planes = [factors[b, part].reshape(inner, factors.shape[4]) for part in range(4)]
        real, imag = complex_dot(*planes, NT)
        core[b, 0] = real * scale
        core[b, 1] = imag * scale


def amplitude_kernel(start, count, slots, n_before, n_out, place, own_core, other_core, *refs):
    own_split, other_split, own_flat, other_flat = refs[:4]
    before = refs[4 : 4 + n_before]
    outs = refs[4 + n_before : 4 + n_before + n_out]
    first, second, product, sems, *more = refs[4 + n_before + n_out :]
    half, idx = place[0], place[1]
    _, _, groups, own_rows, inner = first.shape
    rows, columns = groups * own_rows, second.shape[2]

    def first_copy(lower, b, position, slot):
        source = own_split if lower else other_split
        return pltpu.make_async_copy(
            source.at[:, start + b, idx ^ slot, 0 if lower else 1], first.at[b, :, position], sems.at[0, b]
        )

    def second_copy(lower, b):
        source = other_flat if lower else own_flat
        return pltpu.make_async_copy(source.at[:, start + b], second.at[b], sems.at[1, b])

    for lower in (True, False):

        @pl.when(half == (0 if lower else 1))
        def _():
            for b in range(count):
                for position, slot in enumerate(slots):
                    first_copy(lower, b, position, slot).start()
                second_copy(lower, b).start()

    if n_before:
        held, held_sem = more
        loading = pltpu.make_async_copy(before[0], held, held_sem)
        loading.start()
    else:
        for out in outs:
            out[...] = jnp.zeros_like(out)
    piece = rows // n_out

    def one_value(b, carry):
        whole = own_split.at[:, start + b, :groups, 0]
        pltpu.make_async_copy(whole, first.at[b], sems.at[0, b]).wait()
        real, imag = complex_dot(
            first[b, 0].reshape(rows, inner),
            first[b, 1].reshape(rows, inner),
            own_core[b, 0] + other_core[b, 0],
            own_core[b, 1] + other_core[b, 1],
            NN,
        )
        for part, value in enumerate((real, imag, real + imag)):
            product[part] = left_stack(value, 1)
        second_copy(True, b).wait()
        if n_before:
            loading.wait()
        for at in range(0, columns, 256):
            spot = slice(at, at + 256)
            right_real, right_imag = second[b, 0, spot], second[b, 1, spot]
            one = dot_stacks(product[0], right_stack(right_real, 1), NT)
            two = dot_stacks(product[1], right_stack(right_imag, 1), NT)
            three = dot_stacks(product[2], right_stack(right_real + right_imag, 1), NT)
            for plane, value in enumerate((one - two, three - one - two)):
                if n_before:
                    value = value + held[plane, :, spot]
                for number, out in enumerate(outs):
                    part = value[number * piece : (number + 1) * piece]
                    if n_before:
                        out[plane, :, spot] = part
                    else:
                        out[plane, :, spot] += part
        return carry

    if count == 1:
        one_value(0, 0)
    else:
        lax.fori_loop(0, count, one_value, 0)


def chunks_of(count):
    return count - 1, 1


def overlapped(left_factor, right_factor):
    idx_size = lax.axis_size("idx")
    _, _, local_batch, rows, inner = left_factor.shape
    _, _, batch, inner_part, between = right_factor.shape
    own_rows = rows // (idx_size * 2)
    half_rows = rows // 2
    half_cols = between // 2
    scale = 1.0 / math.sqrt(2.0 * batch * between)
    place = jnp.stack([lax.axis_index("half"), lax.axis_index("idx")]).astype(jnp.int32)
    depth = idx_size // 2
    right = right_factor.reshape(2, idx_size, local_batch, inner_part, between)
    params = pltpu.CompilerParams(vmem_limit_bytes=44 * MIB)
    shape = (2, local_batch, idx_size, 2, own_rows, inner)
    own_left = left_factor.reshape(shape)

    def dealt(start, count):
        return pl.pallas_call(
            functools.partial(deal_kernel, start, count, half_cols),
            out_shape=jax.ShapeDtypeStruct((idx_size, 2, 2, count, inner_part, half_cols), jnp.float32),
            in_specs=[ANYWHERE],
            out_specs=IN_VMEM,
            scratch_shapes=[pltpu.SemaphoreType.DMA((4,))],
            cost_estimate=BRIEF,
            compiler_params=pltpu.CompilerParams(vmem_limit_bytes=38 * MIB),
        )(right)

    def sent(pieces):
        flat = pieces.reshape(2 * idx_size, *pieces.shape[2:])
        return lax.all_to_all(flat, ("idx", "half"), 0, 0, tiled=True).reshape(pieces.shape)

    def core_of(count, arrived, after=()):
        return pl.pallas_call(
            functools.partial(core_kernel, count, scale),
            out_shape=jax.ShapeDtypeStruct((count, 2, inner, inner), jnp.float32),
            in_specs=[ANYWHERE] + [IN_VMEM] * len(after),
            out_specs=IN_VMEM,
            scratch_shapes=[
                pltpu.VMEM((count, 4, idx_size, inner_part, half_cols), jnp.float32),
                pltpu.SemaphoreType.DMA((count, 4)),
            ],
            cost_estimate=BRIEF,
            compiler_params=params,
        )(arrived, *after)

    def added(start, count, slots, n_out, core, other_core, other_left, before):
        flat = (2, local_batch, rows, inner)
        kept_rows = len(slots) * own_rows
        return pl.pallas_call(
            functools.partial(amplitude_kernel, start, count, slots, len(before), n_out),
            out_shape=[jax.ShapeDtypeStruct((2, kept_rows // n_out, rows), jnp.float32)] * n_out,
            in_specs=[IN_SMEM, IN_VMEM, IN_VMEM] + [ANYWHERE] * (4 + len(before)),
            out_specs=[IN_VMEM] * n_out,
            scratch_shapes=[
                pltpu.VMEM((count, 2, len(slots), own_rows, inner), jnp.float32),
                pltpu.VMEM((count, 2, rows, inner), jnp.float32),
                pltpu.VMEM((3, kept_rows, 3 * inner), jnp.bfloat16),
                pltpu.SemaphoreType.DMA((2, count)),
            ]
            + [pltpu.VMEM(part.shape, jnp.float32) for part in before]
            + [pltpu.SemaphoreType.DMA] * len(before),
            cost_estimate=BRIEF,
            compiler_params=params,
        )(
            place, core, other_core, own_left, other_left,
            own_left.reshape(flat), other_left.reshape(flat), *before,
        )

    def hop(x, mask):
        return lax.ppermute(x, "idx", [(i, i ^ mask) for i in range(idx_size)])

    many, few = chunks_of(local_batch)
    other_left = swapped(left_factor, "half").reshape(shape)
    arrived = sent(dealt(0, many))
    pieces = dealt(many, few)
    late = sent(pieces)
    arrived, pieces = lax.optimization_barrier((arrived, pieces))
    core = core_of(many, arrived)
    odd = list(range(idx_size - 1, 0, -2))
    even = [slot - 1 for slot in odd]
    sums = added(0, many, odd + even, 2, core, swapped(core, "half"), other_left, [])
    core = core_of(few, late, (sums[0][0, :8, :128],))
    other_core = swapped(core, "half")
    leaving = added(many, few, odd, PIECES * depth, core, other_core, other_left, [sums[0]])
    core, leaving = lax.optimization_barrier((core, leaving))
    staying = list(added(many, few, even, PIECES * depth, core, other_core, other_left, [sums[1]]))
    mine, coming = [], {}
    for n, block in enumerate(leaving):
        if n >= WINDOW:
            block, mine[n - WINDOW] = lax.optimization_barrier((block, mine[n - WINDOW]))
        if n - 3 * PIECES in coming:
            block, coming[n - 3 * PIECES] = lax.optimization_barrier((block, coming[n - 3 * PIECES]))
        mine.append(staying[n] + hop(block, 1))
        if even[n // PIECES] // 2 % 2:
            coming[n] = hop(mine[n], 2)
    for n, block in coming.items():
        target = n + PIECES
        mine[target] = mine[target] + block
    blocks = {even[n // PIECES] // 2: mine[n : n + PIECES] for n in range(0, PIECES * depth, PIECES)}
    bit = 2
    while bit < depth:
        for d in range(bit, depth, 2 * bit):
            arriving = [hop(block, 2 * bit) for block in blocks[d]]
            blocks[d - bit] = [block + new for block, new in zip(blocks[d - bit], arriving)]
        bit *= 2
    return jnp.moveaxis(jnp.concatenate(blocks[0], axis=1), 0, 1)


def on_device(left_factor, right_factor):
    idx_size = lax.axis_size("idx")
    rows, inner_part, between = left_factor.shape[3], right_factor.shape[3], right_factor.shape[4]
    aligned = (
        lax.axis_size("half") == 2
        and left_factor.shape[2] > 1
        and idx_size in (2, 4, 8)
        and inner_part % 8 == 0
        and between % 256 == 0
        and rows % 256 == 0
        and rows % (32 * idx_size) == 0
        and 256 % (rows // idx_size) == 0
    )
    return (overlapped if aligned else general)(left_factor, right_factor)


def solution(mesh):
    return jax.shard_map(
        on_device,
        mesh=mesh,
        in_specs=(P("half", "cuts", "idx", None, None), P("half", "cuts", None, "idx", None)),
        out_specs=P(("idx", "half"), "cuts", None),
        check_vma=False,
    )
```

```python
import functools
import math

import jax
import jax.numpy as jnp
from jax import lax
from jax.experimental import pallas as pl
from jax.experimental.pallas import tpu as pltpu
from jax.sharding import PartitionSpec as P

HIGH = lax.Precision.HIGH
MIB = 1 << 20
PIECES = 2
WINDOW = 4
ANYWHERE = pl.BlockSpec(memory_space=pl.ANY)
IN_HBM = pl.BlockSpec(memory_space=pltpu.HBM)
IN_VMEM = pl.BlockSpec(memory_space=pltpu.VMEM)
IN_SMEM = pl.BlockSpec(memory_space=pltpu.SMEM)


def swapped(x, axis):
    return lax.ppermute(x, axis, [(i, i ^ 1) for i in range(lax.axis_size(axis))])


def complex_terms(left_real, left_imag, right_real, right_imag, pattern):
    first = jnp.einsum(pattern, left_real, right_real, precision=HIGH)
    second = jnp.einsum(pattern, left_imag, right_imag, precision=HIGH)
    mixed = jnp.einsum(pattern, left_real + left_imag, right_real + right_imag, precision=HIGH)
    return first, second, mixed


def general(left_factor, right_factor):
    idx_size = lax.axis_size("idx")
    half_size = lax.axis_size("half")
    left = left_factor[0]
    right = right_factor[0]
    _, local_batch, rows, inner = left.shape
    _, batch, inner_part, between = right.shape
    own_rows = rows // (idx_size * half_size)
    half_rows = rows // half_size
    half_cols = between // half_size
    is_lower = lax.axis_index("half") == 0
    scale = 1.0 / math.sqrt(2.0 * batch * between)
    pieces = right.reshape(2, idx_size, local_batch, inner_part, half_size, half_cols)
    split_rows = left.reshape(2, local_batch, idx_size, half_size, own_rows, inner)
    upper_rows = lax.ppermute(split_rows[:, :, :, 1], "half", [(0, 1)])
    other_whole = lax.ppermute(left, "half", [(1, 0)])
    first_left = jnp.where(is_lower, split_rows[:, :, :, 0], upper_rows)
    first_left = first_left.reshape(2, local_batch, half_rows, inner)
    second_left = jnp.where(is_lower, other_whole, left)
    totals = None
    for b in range(local_batch):
        outgoing = jnp.transpose(pieces[:, :, b], (1, 3, 0, 2, 4))
        outgoing = outgoing.reshape(idx_size * half_size, 2, inner_part, half_cols)
        arrived = lax.all_to_all(outgoing, ("idx", "half"), 0, 0, tiled=True)
        arrived = arrived.reshape(idx_size, half_size, 2, inner_part, half_cols)
        factors = jnp.transpose(arrived, (1, 2, 0, 3, 4)).reshape(2, 2, inner, half_cols)
        first, second, mixed = complex_terms(
            factors[0, 0], factors[0, 1], factors[1, 0], factors[1, 1], "kn,ln->kl"
        )
        core = jnp.stack([first - second, mixed - first - second]) * scale
        core = core + swapped(core, "half")
        first, second, mixed = complex_terms(
            first_left[0, b], first_left[1, b], core[0], core[1], "mk,kl->ml"
        )
        terms = complex_terms(
            first - second, mixed - first - second, second_left[0, b], second_left[1, b], "ml,ol->mo"
        )
        totals = terms if totals is None else [t + u for t, u in zip(totals, terms)]
    first, second, mixed = totals
    partial = jnp.stack([first - second, mixed - first - second], axis=1)
    return lax.psum_scatter(partial, "idx", scatter_dimension=0, tiled=True)


def split_float(x):
    high = x.astype(jnp.bfloat16)
    return high, (x - high.astype(jnp.float32)).astype(jnp.bfloat16)


def stacked(parts, axis):
    return jnp.concatenate(parts, axis=axis)


def left_stack(x, axis):
    high, low = split_float(x)
    return stacked([high, high, low], axis)


def right_stack(x, axis):
    high, low = split_float(x)
    return stacked([high, low, high], axis)


def dot_stacks(left, right, dims):
    return lax.dot_general(left, right, (dims, ((), ())), preferred_element_type=jnp.float32)


def complex_dot(left_real, left_imag, right_real, right_imag, dims):
    left_axis, right_axis = dims[0][0], dims[1][0]

    def term(left, right):
        return dot_stacks(left_stack(left, left_axis), right_stack(right, right_axis), dims)

    first = term(left_real, right_real)
    second = term(left_imag, right_imag)
    mixed = term(left_real + left_imag, right_real + right_imag)
    return first - second, mixed - first - second


BRIEF = pl.CostEstimate(flops=0, bytes_accessed=1024, transcendentals=0)
NT = ((1,), (1,))
NN = ((1,), (0,))


def deal_kernel(start, count, half_cols, right, out, sems):
    copies = []
    for half in range(2):
        for plane in range(2):
            source = right.at[plane, :, pl.ds(start, count), :, pl.ds(half * half_cols, half_cols)]
            copies.append(pltpu.make_async_copy(source, out.at[:, half, plane], sems.at[2 * half + plane]))
    for copy in copies:
        copy.start()
    for copy in copies:
        copy.wait()


def core_kernel(count, scale, arrived, *refs):
    core, factors, sems = refs[-3:]
    inner = core.shape[2]
    copies = {}
    for b in range(count):
        for part in range(4):
            source = arrived.at[:, part // 2, part % 2, b]
            copies[b, part] = pltpu.make_async_copy(source, factors.at[b, part], sems.at[b, part])
            copies[b, part].start()
    for b in range(count):
        for part in range(4):
            copies[b, part].wait()
        planes = [factors[b, part].reshape(inner, factors.shape[4]) for part in range(4)]
        real, imag = complex_dot(*planes, NT)
        core[b, 0] = real * scale
        core[b, 1] = imag * scale


def amplitude_kernel(start, count, slots, n_before, n_out, place, own_core, other_core, *refs):
    own_split, other_split, own_flat, other_flat = refs[:4]
    before = refs[4 : 4 + n_before]
    outs = refs[4 + n_before : 4 + n_before + n_out]
    first, second, product, sems = refs[4 + n_before + n_out :]
    half, idx = place[0], place[1]
    _, _, groups, own_rows, inner = first.shape
    rows, columns = groups * own_rows, second.shape[2]

    def first_copy(lower, b, position, slot):
        source = own_split if lower else other_split
        return pltpu.make_async_copy(
            source.at[:, start + b, idx ^ slot, 0 if lower else 1], first.at[b, :, position], sems.at[0, b]
        )

    def second_copy(lower, b):
        source = other_flat if lower else own_flat
        return pltpu.make_async_copy(source.at[:, start + b], second.at[b], sems.at[1, b])

    for lower in (True, False):

        @pl.when(half == (0 if lower else 1))
        def _():
            for b in range(count):
                for position, slot in enumerate(slots):
                    first_copy(lower, b, position, slot).start()
                second_copy(lower, b).start()

    if not n_before:
        for out in outs:
            out[...] = jnp.zeros_like(out)
    piece = rows // n_out

    def one_value(b, carry):
        whole = own_split.at[:, start + b, :groups, 0]
        pltpu.make_async_copy(whole, first.at[b], sems.at[0, b]).wait()
        real, imag = complex_dot(
            first[b, 0].reshape(rows, inner),
            first[b, 1].reshape(rows, inner),
            own_core[b, 0] + other_core[b, 0],
            own_core[b, 1] + other_core[b, 1],
            NN,
        )
        for part, value in enumerate((real, imag, real + imag)):
            product[part] = left_stack(value, 1)
        second_copy(True, b).wait()
        for at in range(0, columns, 256):
            spot = slice(at, at + 256)
            right_real, right_imag = second[b, 0, spot], second[b, 1, spot]
            one = dot_stacks(product[0], right_stack(right_real, 1), NT)
            two = dot_stacks(product[1], right_stack(right_imag, 1), NT)
            three = dot_stacks(product[2], right_stack(right_real + right_imag, 1), NT)
            for plane, value in enumerate((one - two, three - one - two)):
                if n_before:
                    value = value + before[0][plane, :, spot]
                for number, out in enumerate(outs):
                    part = value[number * piece : (number + 1) * piece]
                    if n_before:
                        out[plane, :, spot] = part
                    else:
                        out[plane, :, spot] += part
        return carry

    if count == 1:
        one_value(0, 0)
    else:
        lax.fori_loop(0, count, one_value, 0)


def chunks_of(count):
    return count - 1, 1


def overlapped(left_factor, right_factor):
    idx_size = lax.axis_size("idx")
    _, _, local_batch, rows, inner = left_factor.shape
    _, _, batch, inner_part, between = right_factor.shape
    own_rows = rows // (idx_size * 2)
    half_rows = rows // 2
    half_cols = between // 2
    scale = 1.0 / math.sqrt(2.0 * batch * between)
    place = jnp.stack([lax.axis_index("half"), lax.axis_index("idx")]).astype(jnp.int32)
    depth = idx_size // 2
    right = right_factor.reshape(2, idx_size, local_batch, inner_part, between)
    params = pltpu.CompilerParams(vmem_limit_bytes=44 * MIB)
    small = pltpu.CompilerParams(vmem_limit_bytes=20 * MIB)
    shape = (2, local_batch, idx_size, 2, own_rows, inner)
    own_left = left_factor.reshape(shape)

    def dealt(start, count):
        return pl.pallas_call(
            functools.partial(deal_kernel, start, count, half_cols),
            out_shape=jax.ShapeDtypeStruct((idx_size, 2, 2, count, inner_part, half_cols), jnp.float32),
            in_specs=[ANYWHERE],
            out_specs=IN_VMEM,
            scratch_shapes=[pltpu.SemaphoreType.DMA((4,))],
            cost_estimate=BRIEF,
            compiler_params=pltpu.CompilerParams(vmem_limit_bytes=38 * MIB),
        )(right)

    def sent(pieces):
        flat = pieces.reshape(2 * idx_size, *pieces.shape[2:])
        return lax.all_to_all(flat, ("idx", "half"), 0, 0, tiled=True).reshape(pieces.shape)

    def core_of(count, arrived, after=()):
        return pl.pallas_call(
            functools.partial(core_kernel, count, scale),
            out_shape=jax.ShapeDtypeStruct((count, 2, inner, inner), jnp.float32),
            in_specs=[ANYWHERE] + [IN_VMEM] * len(after),
            out_specs=IN_VMEM,
            scratch_shapes=[
                pltpu.VMEM((count, 4, idx_size, inner_part, half_cols), jnp.float32),
                pltpu.SemaphoreType.DMA((count, 4)),
            ],
            cost_estimate=BRIEF,
            compiler_params=params if count > 1 else small,
        )(arrived, *after)

    def added(start, count, slots, n_out, core, other_core, other_left, before):
        flat = (2, local_batch, rows, inner)
        kept_rows = len(slots) * own_rows
        return pl.pallas_call(
            functools.partial(amplitude_kernel, start, count, slots, len(before), n_out),
            out_shape=[jax.ShapeDtypeStruct((2, kept_rows // n_out, rows), jnp.float32)] * n_out,
            in_specs=[IN_SMEM, IN_VMEM, IN_VMEM] + [IN_HBM] * 4 + [IN_VMEM] * len(before),
            out_specs=[IN_VMEM] * n_out,
            scratch_shapes=[
                pltpu.VMEM((count, 2, len(slots), own_rows, inner), jnp.float32),
                pltpu.VMEM((count, 2, rows, inner), jnp.float32),
                pltpu.VMEM((3, kept_rows, 3 * inner), jnp.bfloat16),
                pltpu.SemaphoreType.DMA((2, count)),
            ],
            cost_estimate=BRIEF,
            compiler_params=small if before else params,
        )(
            place, core, other_core, own_left, other_left,
            own_left.reshape(flat), other_left.reshape(flat), *before,
        )

    def hop(x, mask):
        return lax.ppermute(x, "idx", [(i, i ^ mask) for i in range(idx_size)])

    many, few = chunks_of(local_batch)
    other_left = swapped(left_factor, "half").reshape(shape)
    arrived = sent(dealt(0, many))
    pieces = dealt(many, few)
    late = sent(pieces)
    arrived, pieces = lax.optimization_barrier((arrived, pieces))
    core = core_of(many, arrived)
    odd = list(range(idx_size - 1, 0, -2))
    even = [slot - 1 for slot in odd]
    sums = added(0, many, odd + even, 2, core, swapped(core, "half"), other_left, [])
    core = core_of(few, late, (sums[0][0, :8, :128],))
    other_core = swapped(core, "half")
    leaving = added(many, few, odd, PIECES * depth, core, other_core, other_left, [sums[0]])
    core, leaving = lax.optimization_barrier((core, leaving))
    staying = list(added(many, few, even, PIECES * depth, core, other_core, other_left, [sums[1]]))
    mine, coming = [], {}
    for n, block in enumerate(leaving):
        if n >= WINDOW:
            block, mine[n - WINDOW] = lax.optimization_barrier((block, mine[n - WINDOW]))
        if n - WINDOW - 2 in coming:
            block, coming[n - WINDOW - 2] = lax.optimization_barrier((block, coming[n - WINDOW - 2]))
        mine.append(staying[n] + hop(block, 1))
        if even[n // PIECES] // 2 % 2:
            coming[n] = hop(mine[n], 2)
    for n, block in coming.items():
        target = n + PIECES
        mine[target] = mine[target] + block
    blocks = {even[n // PIECES] // 2: mine[n : n + PIECES] for n in range(0, PIECES * depth, PIECES)}
    bit = 2
    while bit < depth:
        for d in range(bit, depth, 2 * bit):
            arriving = [hop(block, 2 * bit) for block in blocks[d]]
            blocks[d - bit] = [block + new for block, new in zip(blocks[d - bit], arriving)]
        bit *= 2
    return jnp.moveaxis(jnp.concatenate(blocks[0], axis=1), 0, 1)


def on_device(left_factor, right_factor):
    idx_size = lax.axis_size("idx")
    rows, inner_part, between = left_factor.shape[3], right_factor.shape[3], right_factor.shape[4]
    aligned = (
        lax.axis_size("half") == 2
        and left_factor.shape[2] > 1
        and idx_size in (2, 4, 8)
        and inner_part % 8 == 0
        and between % 256 == 0
        and rows % 256 == 0
        and rows % (32 * idx_size) == 0
        and 256 % (rows // idx_size) == 0
    )
    return (overlapped if aligned else general)(left_factor, right_factor)


def solution(mesh):
    return jax.shard_map(
        on_device,
        mesh=mesh,
        in_specs=(P("half", "cuts", "idx", None, None), P("half", "cuts", None, "idx", None)),
        out_specs=P(("idx", "half"), "cuts", None),
        check_vma=False,
    )
```

```python
import functools
import math

import jax
import jax.numpy as jnp
from jax import lax
from jax.experimental import pallas as pl
from jax.experimental.pallas import tpu as pltpu
from jax.sharding import PartitionSpec as P

HIGH = lax.Precision.HIGH
MIB = 1 << 20
PIECES = 2
WINDOW = 4
ANYWHERE = pl.BlockSpec(memory_space=pl.ANY)
IN_VMEM = pl.BlockSpec(memory_space=pltpu.VMEM)
IN_SMEM = pl.BlockSpec(memory_space=pltpu.SMEM)


def swapped(x, axis):
    return lax.ppermute(x, axis, [(i, i ^ 1) for i in range(lax.axis_size(axis))])


def complex_terms(left_real, left_imag, right_real, right_imag, pattern):
    first = jnp.einsum(pattern, left_real, right_real, precision=HIGH)
    second = jnp.einsum(pattern, left_imag, right_imag, precision=HIGH)
    mixed = jnp.einsum(pattern, left_real + left_imag, right_real + right_imag, precision=HIGH)
    return first, second, mixed


def general(left_factor, right_factor):
    idx_size = lax.axis_size("idx")
    half_size = lax.axis_size("half")
    left = left_factor[0]
    right = right_factor[0]
    _, local_batch, rows, inner = left.shape
    _, batch, inner_part, between = right.shape
    own_rows = rows // (idx_size * half_size)
    half_rows = rows // half_size
    half_cols = between // half_size
    is_lower = lax.axis_index("half") == 0
    scale = 1.0 / math.sqrt(2.0 * batch * between)
    pieces = right.reshape(2, idx_size, local_batch, inner_part, half_size, half_cols)
    split_rows = left.reshape(2, local_batch, idx_size, half_size, own_rows, inner)
    upper_rows = lax.ppermute(split_rows[:, :, :, 1], "half", [(0, 1)])
    other_whole = lax.ppermute(left, "half", [(1, 0)])
    first_left = jnp.where(is_lower, split_rows[:, :, :, 0], upper_rows)
    first_left = first_left.reshape(2, local_batch, half_rows, inner)
    second_left = jnp.where(is_lower, other_whole, left)
    totals = None
    for b in range(local_batch):
        outgoing = jnp.transpose(pieces[:, :, b], (1, 3, 0, 2, 4))
        outgoing = outgoing.reshape(idx_size * half_size, 2, inner_part, half_cols)
        arrived = lax.all_to_all(outgoing, ("idx", "half"), 0, 0, tiled=True)
        arrived = arrived.reshape(idx_size, half_size, 2, inner_part, half_cols)
        factors = jnp.transpose(arrived, (1, 2, 0, 3, 4)).reshape(2, 2, inner, half_cols)
        first, second, mixed = complex_terms(
            factors[0, 0], factors[0, 1], factors[1, 0], factors[1, 1], "kn,ln->kl"
        )
        core = jnp.stack([first - second, mixed - first - second]) * scale
        core = core + swapped(core, "half")
        first, second, mixed = complex_terms(
            first_left[0, b], first_left[1, b], core[0], core[1], "mk,kl->ml"
        )
        terms = complex_terms(
            first - second, mixed - first - second, second_left[0, b], second_left[1, b], "ml,ol->mo"
        )
        totals = terms if totals is None else [t + u for t, u in zip(totals, terms)]
    first, second, mixed = totals
    partial = jnp.stack([first - second, mixed - first - second], axis=1)
    return lax.psum_scatter(partial, "idx", scatter_dimension=0, tiled=True)


def split_float(x):
    high = x.astype(jnp.bfloat16)
    return high, (x - high.astype(jnp.float32)).astype(jnp.bfloat16)


def stacked(parts, axis):
    return jnp.concatenate(parts, axis=axis)


def left_stack(x, axis):
    high, low = split_float(x)
    return stacked([high, high, low], axis)


def right_stack(x, axis):
    high, low = split_float(x)
    return stacked([high, low, high], axis)


def dot_stacks(left, right, dims):
    return lax.dot_general(left, right, (dims, ((), ())), preferred_element_type=jnp.float32)


def complex_dot(left_real, left_imag, right_real, right_imag, dims):
    left_axis, right_axis = dims[0][0], dims[1][0]

    def term(left, right):
        return dot_stacks(left_stack(left, left_axis), right_stack(right, right_axis), dims)

    first = term(left_real, right_real)
    second = term(left_imag, right_imag)
    mixed = term(left_real + left_imag, right_real + right_imag)
    return first - second, mixed - first - second


BRIEF = pl.CostEstimate(flops=0, bytes_accessed=1024, transcendentals=0)
NT = ((1,), (1,))
NN = ((1,), (0,))


def deal_kernel(start, count, half_cols, right, out, sems):
    copies = []
    for half in range(2):
        for plane in range(2):
            source = right.at[plane, :, pl.ds(start, count), :, pl.ds(half * half_cols, half_cols)]
            copies.append(pltpu.make_async_copy(source, out.at[:, half, plane], sems.at[2 * half + plane]))
    for copy in copies:
        copy.start()
    for copy in copies:
        copy.wait()


def core_kernel(count, scale, arrived, *refs):
    core, factors, sems = refs[-3:]
    inner = core.shape[2]
    copies = {}
    for b in range(count):
        for part in range(4):
            source = arrived.at[:, part // 2, part % 2, b]
            copies[b, part] = pltpu.make_async_copy(source, factors.at[b, part], sems.at[b, part])
            copies[b, part].start()
    for b in range(count):
        for part in range(4):
            copies[b, part].wait()
        planes = [factors[b, part].reshape(inner, factors.shape[4]) for part in range(4)]
        real, imag = complex_dot(*planes, NT)
        core[b, 0] = real * scale
        core[b, 1] = imag * scale


def amplitude_kernel(start, count, slots, n_before, n_out, place, own_core, other_core, *refs):
    own_split, other_split, own_flat, other_flat = refs[:4]
    before = refs[4 : 4 + n_before]
    outs = refs[4 + n_before : 4 + n_before + n_out]
    rest = refs[4 + n_before + n_out :]
    if not n_before:
        rest[0][...] = jnp.zeros_like(rest[0])
        rest = rest[1:]
    first, second, product, sems, *more = rest
    half, idx = place[0], place[1]
    _, _, groups, own_rows, inner = first.shape
    rows, columns = groups * own_rows, second.shape[2]

    def first_copy(lower, b, position, slot):
        source = own_split if lower else other_split
        return pltpu.make_async_copy(
            source.at[:, start + b, idx ^ slot, 0 if lower else 1], first.at[b, :, position], sems.at[0, b]
        )

    def second_copy(lower, b):
        source = other_flat if lower else own_flat
        return pltpu.make_async_copy(source.at[:, start + b], second.at[b], sems.at[1, b])

    for lower in (True, False):

        @pl.when(half == (0 if lower else 1))
        def _():
            for b in range(count):
                for position, slot in enumerate(slots):
                    first_copy(lower, b, position, slot).start()
                second_copy(lower, b).start()

    if n_before:
        held, held_sem = more
        loading = pltpu.make_async_copy(before[0], held, held_sem)
        loading.start()
    else:
        for out in outs:
            out[...] = jnp.zeros_like(out)
    piece = rows // n_out

    def one_value(b, carry):
        whole = own_split.at[:, start + b, :groups, 0]
        pltpu.make_async_copy(whole, first.at[b], sems.at[0, b]).wait()
        real, imag = complex_dot(
            first[b, 0].reshape(rows, inner),
            first[b, 1].reshape(rows, inner),
            own_core[b, 0] + other_core[b, 0],
            own_core[b, 1] + other_core[b, 1],
            NN,
        )
        for part, value in enumerate((real, imag, real + imag)):
            product[part] = left_stack(value, 1)
        second_copy(True, b).wait()
        if n_before:
            loading.wait()
        for at in range(0, columns, 256):
            spot = slice(at, at + 256)
            right_real, right_imag = second[b, 0, spot], second[b, 1, spot]
            one = dot_stacks(product[0], right_stack(right_real, 1), NT)
            two = dot_stacks(product[1], right_stack(right_imag, 1), NT)
            three = dot_stacks(product[2], right_stack(right_real + right_imag, 1), NT)
            for plane, value in enumerate((one - two, three - one - two)):
                if n_before:
                    value = value + held[plane, :, spot]
                for number, out in enumerate(outs):
                    part = value[number * piece : (number + 1) * piece]
                    if n_before:
                        out[plane, :, spot] = part
                    else:
                        out[plane, :, spot] += part
        return carry

    if count == 1:
        one_value(0, 0)
    else:
        lax.fori_loop(0, count, one_value, 0)


def chunks_of(count):
    return count - 1, 1


def overlapped(left_factor, right_factor):
    idx_size = lax.axis_size("idx")
    _, _, local_batch, rows, inner = left_factor.shape
    _, _, batch, inner_part, between = right_factor.shape
    own_rows = rows // (idx_size * 2)
    half_rows = rows // 2
    half_cols = between // 2
    scale = 1.0 / math.sqrt(2.0 * batch * between)
    place = jnp.stack([lax.axis_index("half"), lax.axis_index("idx")]).astype(jnp.int32)
    depth = idx_size // 2
    right = right_factor.reshape(2, idx_size, local_batch, inner_part, between)
    params = pltpu.CompilerParams(vmem_limit_bytes=44 * MIB)
    shape = (2, local_batch, idx_size, 2, own_rows, inner)
    own_left = left_factor.reshape(shape)

    def dealt(start, count):
        return pl.pallas_call(
            functools.partial(deal_kernel, start, count, half_cols),
            out_shape=jax.ShapeDtypeStruct((idx_size, 2, 2, count, inner_part, half_cols), jnp.float32),
            in_specs=[ANYWHERE],
            out_specs=IN_VMEM,
            scratch_shapes=[pltpu.SemaphoreType.DMA((4,))],
            cost_estimate=BRIEF,
            compiler_params=pltpu.CompilerParams(vmem_limit_bytes=38 * MIB),
        )(right)

    def sent(pieces):
        flat = pieces.reshape(2 * idx_size, *pieces.shape[2:])
        return lax.all_to_all(flat, ("idx", "half"), 0, 0, tiled=True).reshape(pieces.shape)

    def core_of(count, arrived, after=()):
        return pl.pallas_call(
            functools.partial(core_kernel, count, scale),
            out_shape=jax.ShapeDtypeStruct((count, 2, inner, inner), jnp.float32),
            in_specs=[ANYWHERE] + [IN_VMEM] * len(after),
            out_specs=IN_VMEM,
            scratch_shapes=[
                pltpu.VMEM((count, 4, idx_size, inner_part, half_cols), jnp.float32),
                pltpu.SemaphoreType.DMA((count, 4)),
            ],
            cost_estimate=BRIEF,
            compiler_params=params,
        )(arrived, *after)

    def added(start, count, slots, n_out, core, other_core, other_left, before):
        flat = (2, local_batch, rows, inner)
        kept_rows = len(slots) * own_rows
        return pl.pallas_call(
            functools.partial(amplitude_kernel, start, count, slots, len(before), n_out),
            out_shape=[jax.ShapeDtypeStruct((2, kept_rows // n_out, rows), jnp.float32)] * n_out
            + [jax.ShapeDtypeStruct((8, 128), jnp.float32)] * (not before),
            in_specs=[IN_SMEM, IN_VMEM, IN_VMEM] + [ANYWHERE] * (4 + len(before)),
            out_specs=[IN_VMEM] * (n_out + (not before)),
            scratch_shapes=[
                pltpu.VMEM((count, 2, len(slots), own_rows, inner), jnp.float32),
                pltpu.VMEM((count, 2, rows, inner), jnp.float32),
                pltpu.VMEM((3, kept_rows, 3 * inner), jnp.bfloat16),
                pltpu.SemaphoreType.DMA((2, count)),
            ]
            + [pltpu.VMEM(part.shape, jnp.float32) for part in before]
            + [pltpu.SemaphoreType.DMA] * len(before),
            cost_estimate=BRIEF,
            compiler_params=params,
        )(
            place, core, other_core, own_left, other_left,
            own_left.reshape(flat), other_left.reshape(flat), *before,
        )

    def hop(x, mask):
        return lax.ppermute(x, "idx", [(i, i ^ mask) for i in range(idx_size)])

    many, few = chunks_of(local_batch)
    other_left = swapped(left_factor, "half").reshape(shape)
    arrived = sent(dealt(0, many))
    pieces = dealt(many, few)
    late = sent(pieces)
    arrived, pieces = lax.optimization_barrier((arrived, pieces))
    core = core_of(many, arrived)
    odd = list(range(idx_size - 1, 0, -2))
    even = [slot - 1 for slot in odd]
    sums = added(0, many, odd + even, 2, core, swapped(core, "half"), other_left, [])
    core = core_of(few, late, (sums[2],))
    other_core = swapped(core, "half")
    leaving = added(many, few, odd, PIECES * depth, core, other_core, other_left, [sums[0]])
    core, leaving = lax.optimization_barrier((core, leaving))
    staying = list(added(many, few, even, PIECES * depth, core, other_core, other_left, [sums[1]]))
    mine, coming = [], {}
    for n, block in enumerate(leaving):
        if n >= WINDOW:
            block, mine[n - WINDOW] = lax.optimization_barrier((block, mine[n - WINDOW]))
        if n - WINDOW - 2 in coming:
            block, coming[n - WINDOW - 2] = lax.optimization_barrier((block, coming[n - WINDOW - 2]))
        mine.append(staying[n] + hop(block, 1))
        if even[n // PIECES] // 2 % 2:
            coming[n] = hop(mine[n], 2)
    for n, block in coming.items():
        target = n + PIECES
        mine[target] = mine[target] + block
    blocks = {even[n // PIECES] // 2: mine[n : n + PIECES] for n in range(0, PIECES * depth, PIECES)}
    bit = 2
    while bit < depth:
        for d in range(bit, depth, 2 * bit):
            arriving = [hop(block, 2 * bit) for block in blocks[d]]
            blocks[d - bit] = [block + new for block, new in zip(blocks[d - bit], arriving)]
        bit *= 2
    return jnp.moveaxis(jnp.concatenate(blocks[0], axis=1), 0, 1)


def on_device(left_factor, right_factor):
    idx_size = lax.axis_size("idx")
    rows, inner_part, between = left_factor.shape[3], right_factor.shape[3], right_factor.shape[4]
    aligned = (
        lax.axis_size("half") == 2
        and left_factor.shape[2] > 1
        and idx_size in (2, 4, 8)
        and inner_part % 8 == 0
        and between % 256 == 0
        and rows % 256 == 0
        and rows % (32 * idx_size) == 0
        and 256 % (rows // idx_size) == 0
    )
    return (overlapped if aligned else general)(left_factor, right_factor)


def solution(mesh):
    return jax.shard_map(
        on_device,
        mesh=mesh,
        in_specs=(P("half", "cuts", "idx", None, None), P("half", "cuts", None, "idx", None)),
        out_specs=P(("idx", "half"), "cuts", None),
        check_vma=False,
    )
```

```python
import functools
import math

import jax
import jax.numpy as jnp
from jax import lax
from jax.experimental import pallas as pl
from jax.experimental.pallas import tpu as pltpu
from jax.sharding import PartitionSpec as P

HIGH = lax.Precision.HIGH
MIB = 1 << 20
PIECES = 2
WINDOW = 4
ANYWHERE = pl.BlockSpec(memory_space=pl.ANY)
IN_VMEM = pl.BlockSpec(memory_space=pltpu.VMEM)
IN_SMEM = pl.BlockSpec(memory_space=pltpu.SMEM)


def swapped(x, axis):
    return lax.ppermute(x, axis, [(i, i ^ 1) for i in range(lax.axis_size(axis))])


def complex_terms(left_real, left_imag, right_real, right_imag, pattern):
    first = jnp.einsum(pattern, left_real, right_real, precision=HIGH)
    second = jnp.einsum(pattern, left_imag, right_imag, precision=HIGH)
    mixed = jnp.einsum(pattern, left_real + left_imag, right_real + right_imag, precision=HIGH)
    return first, second, mixed


def general(left_factor, right_factor):
    idx_size = lax.axis_size("idx")
    half_size = lax.axis_size("half")
    left = left_factor[0]
    right = right_factor[0]
    _, local_batch, rows, inner = left.shape
    _, batch, inner_part, between = right.shape
    own_rows = rows // (idx_size * half_size)
    half_rows = rows // half_size
    half_cols = between // half_size
    is_lower = lax.axis_index("half") == 0
    scale = 1.0 / math.sqrt(2.0 * batch * between)
    pieces = right.reshape(2, idx_size, local_batch, inner_part, half_size, half_cols)
    split_rows = left.reshape(2, local_batch, idx_size, half_size, own_rows, inner)
    upper_rows = lax.ppermute(split_rows[:, :, :, 1], "half", [(0, 1)])
    other_whole = lax.ppermute(left, "half", [(1, 0)])
    first_left = jnp.where(is_lower, split_rows[:, :, :, 0], upper_rows)
    first_left = first_left.reshape(2, local_batch, half_rows, inner)
    second_left = jnp.where(is_lower, other_whole, left)
    totals = None
    for b in range(local_batch):
        outgoing = jnp.transpose(pieces[:, :, b], (1, 3, 0, 2, 4))
        outgoing = outgoing.reshape(idx_size * half_size, 2, inner_part, half_cols)
        arrived = lax.all_to_all(outgoing, ("idx", "half"), 0, 0, tiled=True)
        arrived = arrived.reshape(idx_size, half_size, 2, inner_part, half_cols)
        factors = jnp.transpose(arrived, (1, 2, 0, 3, 4)).reshape(2, 2, inner, half_cols)
        first, second, mixed = complex_terms(
            factors[0, 0], factors[0, 1], factors[1, 0], factors[1, 1], "kn,ln->kl"
        )
        core = jnp.stack([first - second, mixed - first - second]) * scale
        core = core + swapped(core, "half")
        first, second, mixed = complex_terms(
            first_left[0, b], first_left[1, b], core[0], core[1], "mk,kl->ml"
        )
        terms = complex_terms(
            first - second, mixed - first - second, second_left[0, b], second_left[1, b], "ml,ol->mo"
        )
        totals = terms if totals is None else [t + u for t, u in zip(totals, terms)]
    first, second, mixed = totals
    partial = jnp.stack([first - second, mixed - first - second], axis=1)
    return lax.psum_scatter(partial, "idx", scatter_dimension=0, tiled=True)


def split_float(x):
    high = x.astype(jnp.bfloat16)
    return high, (x - high.astype(jnp.float32)).astype(jnp.bfloat16)


def stacked(parts, axis):
    return jnp.concatenate(parts, axis=axis)


def left_stack(x, axis):
    high, low = split_float(x)
    return stacked([high, high, low], axis)


def right_stack(x, axis):
    high, low = split_float(x)
    return stacked([high, low, high], axis)


def dot_stacks(left, right, dims):
    return lax.dot_general(left, right, (dims, ((), ())), preferred_element_type=jnp.float32)


def complex_dot(left_real, left_imag, right_real, right_imag, dims):
    left_axis, right_axis = dims[0][0], dims[1][0]

    def term(left, right):
        return dot_stacks(left_stack(left, left_axis), right_stack(right, right_axis), dims)

    first = term(left_real, right_real)
    second = term(left_imag, right_imag)
    mixed = term(left_real + left_imag, right_real + right_imag)
    return first - second, mixed - first - second


BRIEF = pl.CostEstimate(flops=0, bytes_accessed=1024, transcendentals=0)
NT = ((1,), (1,))
NN = ((1,), (0,))


def deal_kernel(start, count, half_cols, right, out, sems):
    copies = []
    for half in range(2):
        for plane in range(2):
            source = right.at[plane, :, pl.ds(start, count), :, pl.ds(half * half_cols, half_cols)]
            copies.append(pltpu.make_async_copy(source, out.at[:, half, plane], sems.at[2 * half + plane]))
    for copy in copies:
        copy.start()
    for copy in copies:
        copy.wait()


def core_kernel(count, scale, arrived, *refs):
    core, factors, sems = refs[-3:]
    inner = core.shape[2]
    copies = {}
    for b in range(count):
        for part in range(4):
            source = arrived.at[:, part // 2, part % 2, b]
            copies[b, part] = pltpu.make_async_copy(source, factors.at[b, part], sems.at[b, part])
            copies[b, part].start()
    for b in range(count):
        for part in range(4):
            copies[b, part].wait()
        planes = [factors[b, part].reshape(inner, factors.shape[4]) for part in range(4)]
        real, imag = complex_dot(*planes, NT)
        core[b, 0] = real * scale
        core[b, 1] = imag * scale


def amplitude_kernel(start, count, slots, n_before, n_out, place, own_core, other_core, *refs):
    own_split, other_split, own_flat, other_flat = refs[:4]
    before = refs[4 : 4 + n_before]
    outs = refs[4 + n_before : 4 + n_before + n_out]
    first, second, product, sems, *more = refs[4 + n_before + n_out :]
    half, idx = place[0], place[1]
    _, _, groups, own_rows, inner = first.shape
    rows, columns = groups * own_rows, second.shape[2]

    def first_copy(lower, b, position, slot):
        source = own_split if lower else other_split
        return pltpu.make_async_copy(
            source.at[:, start + b, idx ^ slot, 0 if lower else 1], first.at[b, :, position], sems.at[0, b]
        )

    def second_copy(lower, b):
        source = other_flat if lower else own_flat
        return pltpu.make_async_copy(source.at[:, start + b], second.at[b], sems.at[1, b])

    for lower in (True, False):

        @pl.when(half == (0 if lower else 1))
        def _():
            for b in range(count):
                for position, slot in enumerate(slots):
                    first_copy(lower, b, position, slot).start()
                second_copy(lower, b).start()

    if n_before:
        held, held_sem = more
        loading = pltpu.make_async_copy(before[0], held, held_sem)
        loading.start()
    else:
        for out in outs:
            out[...] = jnp.zeros_like(out)
    piece = rows // n_out

    def one_value(b, carry):
        whole = own_split.at[:, start + b, :groups, 0]
        pltpu.make_async_copy(whole, first.at[b], sems.at[0, b]).wait()
        real, imag = complex_dot(
            first[b, 0].reshape(rows, inner),
            first[b, 1].reshape(rows, inner),
            own_core[b, 0] + other_core[b, 0],
            own_core[b, 1] + other_core[b, 1],
            NN,
        )
        for part, value in enumerate((real, imag, real + imag)):
            product[part] = left_stack(value, 1)
        second_copy(True, b).wait()
        if n_before:
            loading.wait()
        for at in range(0, columns, 256):
            spot = slice(at, at + 256)
            right_real, right_imag = second[b, 0, spot], second[b, 1, spot]
            one = dot_stacks(product[0], right_stack(right_real, 1), NT)
            two = dot_stacks(product[1], right_stack(right_imag, 1), NT)
            three = dot_stacks(product[2], right_stack(right_real + right_imag, 1), NT)
            for plane, value in enumerate((one - two, three - one - two)):
                if n_before:
                    value = value + held[plane, :, spot]
                for number, out in enumerate(outs):
                    part = value[number * piece : (number + 1) * piece]
                    if n_before:
                        out[plane, :, spot] = part
                    else:
                        out[plane, :, spot] += part
        return carry

    if count == 1:
        one_value(0, 0)
    else:
        lax.fori_loop(0, count, one_value, 0)


def chunks_of(count):
    return count - 1, 1


def overlapped(left_factor, right_factor):
    idx_size = lax.axis_size("idx")
    _, _, local_batch, rows, inner = left_factor.shape
    _, _, batch, inner_part, between = right_factor.shape
    own_rows = rows // (idx_size * 2)
    half_rows = rows // 2
    half_cols = between // 2
    scale = 1.0 / math.sqrt(2.0 * batch * between)
    place = jnp.stack([lax.axis_index("half"), lax.axis_index("idx")]).astype(jnp.int32)
    depth = idx_size // 2
    right = right_factor.reshape(2, idx_size, local_batch, inner_part, between)
    params = pltpu.CompilerParams(vmem_limit_bytes=44 * MIB)
    shape = (2, local_batch, idx_size, 2, own_rows, inner)
    own_left = left_factor.reshape(shape)

    def dealt(start, count):
        return pl.pallas_call(
            functools.partial(deal_kernel, start, count, half_cols),
            out_shape=jax.ShapeDtypeStruct((idx_size, 2, 2, count, inner_part, half_cols), jnp.float32),
            in_specs=[ANYWHERE],
            out_specs=IN_VMEM,
            scratch_shapes=[pltpu.SemaphoreType.DMA((4,))],
            cost_estimate=BRIEF,
            compiler_params=pltpu.CompilerParams(vmem_limit_bytes=38 * MIB),
        )(right)

    def sent(pieces):
        flat = pieces.reshape(2 * idx_size, *pieces.shape[2:])
        return lax.all_to_all(flat, ("idx", "half"), 0, 0, tiled=True).reshape(pieces.shape)

    def core_of(count, arrived, after=()):
        return pl.pallas_call(
            functools.partial(core_kernel, count, scale),
            out_shape=jax.ShapeDtypeStruct((count, 2, inner, inner), jnp.float32),
            in_specs=[ANYWHERE] + [IN_VMEM] * len(after),
            out_specs=IN_VMEM,
            scratch_shapes=[
                pltpu.VMEM((count, 4, idx_size, inner_part, half_cols), jnp.float32),
                pltpu.SemaphoreType.DMA((count, 4)),
            ],
            cost_estimate=BRIEF,
            compiler_params=params,
        )(arrived, *after)

    def added(start, count, slots, n_out, core, other_core, other_left, before):
        flat = (2, local_batch, rows, inner)
        kept_rows = len(slots) * own_rows
        return pl.pallas_call(
            functools.partial(amplitude_kernel, start, count, slots, len(before), n_out),
            out_shape=[jax.ShapeDtypeStruct((2, kept_rows // n_out, rows), jnp.float32)] * n_out,
            in_specs=[IN_SMEM, IN_VMEM, IN_VMEM] + [ANYWHERE] * (4 + len(before)),
            out_specs=[IN_VMEM] * n_out,
            scratch_shapes=[
                pltpu.VMEM((count, 2, len(slots), own_rows, inner), jnp.float32),
                pltpu.VMEM((count, 2, rows, inner), jnp.float32),
                pltpu.VMEM((3, kept_rows, 3 * inner), jnp.bfloat16),
                pltpu.SemaphoreType.DMA((2, count)),
            ]
            + [pltpu.VMEM(part.shape, jnp.float32) for part in before]
            + [pltpu.SemaphoreType.DMA] * len(before),
            cost_estimate=BRIEF,
            compiler_params=params,
        )(
            place, core, other_core, own_left, other_left,
            own_left.reshape(flat), other_left.reshape(flat), *before,
        )

    def hop(x, mask):
        return lax.ppermute(x, "idx", [(i, i ^ mask) for i in range(idx_size)])

    many, few = chunks_of(local_batch)
    other_left = swapped(left_factor, "half").reshape(shape)
    arrived = sent(dealt(0, many))
    pieces = dealt(many, few)
    late = sent(pieces)
    arrived, pieces = lax.optimization_barrier((arrived, pieces))
    core = core_of(many, arrived)
    odd = list(range(idx_size - 1, 0, -2))
    even = [slot - 1 for slot in odd]
    groups = 2 if depth % 2 == 0 else 1
    sums = added(0, many, odd + even, 2 * groups, core, swapped(core, "half"), other_left, [])
    core = core_of(few, late, (sums[0][0, :8, :128],))
    other_core = swapped(core, "half")
    formed = []
    per = depth // groups
    for number, kept in enumerate(sums):
        slots = (odd + even)[number * per : (number + 1) * per]
        formed.append(added(many, few, slots, PIECES * per, core, other_core, other_left, [kept]))
        if number + 1 < len(sums):
            core, formed[-1] = lax.optimization_barrier((core, formed[-1]))
    flat = [block for part in formed for block in part]
    leaving, staying = flat[: PIECES * depth], flat[PIECES * depth :]
    mine, coming = [], {}
    for n, block in enumerate(leaving):
        if n >= WINDOW:
            block, mine[n - WINDOW] = lax.optimization_barrier((block, mine[n - WINDOW]))
        if n - WINDOW - 2 in coming:
            block, coming[n - WINDOW - 2] = lax.optimization_barrier((block, coming[n - WINDOW - 2]))
        mine.append(staying[n] + hop(block, 1))
        if even[n // PIECES] // 2 % 2:
            coming[n] = hop(mine[n], 2)
    for n, block in coming.items():
        target = n + PIECES
        mine[target] = mine[target] + block
    blocks = {even[n // PIECES] // 2: mine[n : n + PIECES] for n in range(0, PIECES * depth, PIECES)}
    bit = 2
    while bit < depth:
        for d in range(bit, depth, 2 * bit):
            arriving = [hop(block, 2 * bit) for block in blocks[d]]
            blocks[d - bit] = [block + new for block, new in zip(blocks[d - bit], arriving)]
        bit *= 2
    return jnp.moveaxis(jnp.concatenate(blocks[0], axis=1), 0, 1)


def on_device(left_factor, right_factor):
    idx_size = lax.axis_size("idx")
    rows, inner_part, between = left_factor.shape[3], right_factor.shape[3], right_factor.shape[4]
    aligned = (
        lax.axis_size("half") == 2
        and left_factor.shape[2] > 1
        and idx_size in (2, 4, 8)
        and inner_part % 8 == 0
        and between % 256 == 0
        and rows % 256 == 0
        and rows % (32 * idx_size) == 0
        and 256 % (rows // idx_size) == 0
    )
    return (overlapped if aligned else general)(left_factor, right_factor)


def solution(mesh):
    return jax.shard_map(
        on_device,
        mesh=mesh,
        in_specs=(P("half", "cuts", "idx", None, None), P("half", "cuts", None, "idx", None)),
        out_specs=P(("idx", "half"), "cuts", None),
        check_vma=False,
    )
```
